512 devices in a mesh: server: 32 (over x, z), worker: 16 (over y, core).
Axes of the slice: x: 4, y: 8, z: 8, core: 2. Of those that a mesh axis runs over, the one named last changes fastest.
Arguments:
- factors: float32 [16384, 256], P('server'), may hold values from -0.3 to 0.3
- linear: float32 [16384], P('server'), may hold values from -0.6 to 0.6
- acc_factors: float32 [16384, 256], P(('server', 'worker')), may hold values from 0.5 to 20
- acc_linear: float32 [16384], P(('server', 'worker')), may hold values from 10 to 300
- feature_slot: int32 [131072, 39], P(('server', 'worker')), may hold values from 0 to 511, as said below
- requests: int32 [16384, 16], P(('server', 'worker')), may hold values from 0 to 511, as said below
- clicks: int32 [131072], P(('server', 'worker')), may hold values from 0 to 1
Outputs:
- new_factors: float32 [16384, 256], P('server')
- new_linear: float32 [16384], P('server')
- new_acc_factors: float32 [16384, 256], P(('server', 'worker'))
- new_acc_linear: float32 [16384], P(('server', 'worker'))
The draws below stay inside these ranges and needn't reach their ends.
Inputs may be any that keep to these rules, and one draw needn't show every extreme that they name: Within each device's list for one owner, the first entries (its live requests, at most 16) are distinct and increasing, the rest are 0. The owner that is fullest gets 16 live requests from every device, and owners' loads differ. `feature_slot`: every feature of a sample names a live slot of its device's request list: o * 16 + j with j below the number of live requests of that device to owner o.
All inputs are finite; a program needn't handle non-finite values.
Results may differ from the reference program's by a relative error of at most 0.006.
Values may be sent and summed in bfloat16 or wider, within the bound.
No kernel may reach another device: no remote copies, remote signals or barrier semaphores. Data moves between devices by JAX's collectives and lax.ppermute only.
A program may use at most 64 MiB of HBM per device.

```python
import math
import jax
import jax.numpy as jnp
from jax import lax

K = 256
FIELDS = 39
B_DEV = 256
ROWS_DEV = 512
CAP = 16
TABLE_ROWS = 16384
SAMPLES = 131072
N_SERVER = 32
DEVICES = 512


def live_counts(key):
    base_key = jax.random.fold_in(key, 11)
    owner_heat = jax.random.randint(jax.random.fold_in(base_key, 1), (N_SERVER,), 1, 5)
    lowest = CAP * owner_heat // 8
    highest = CAP * owner_heat // 4 + 1
    counts = jax.random.randint(jax.random.fold_in(base_key, 2), (DEVICES, N_SERVER), lowest[None, :], highest[None, :])
    hottest = jax.random.randint(jax.random.fold_in(base_key, 3), (), 0, N_SERVER)
    owners = jnp.arange(N_SERVER)[None, :]
    return jnp.where(owners == hottest, CAP, counts)


def draw_requests(key, part):
    counts = live_counts(key).reshape(-1)
    base_key = jax.random.fold_in(key, 23)
    bin_width = ROWS_DEV // CAP
    columns = jnp.arange(CAP)[None, :]
    picks = columns * bin_width + jax.random.randint(jax.random.fold_in(base_key, 1), (DEVICES * N_SERVER, CAP), 0, bin_width)
    ranking = jax.random.permutation(jax.random.fold_in(base_key, 2), jnp.broadcast_to(jnp.arange(CAP), (DEVICES * N_SERVER, CAP)), axis=1, independent=True)
    chosen = ranking < counts[:, None]
    placing = jnp.argsort(jnp.where(chosen, 0, CAP) + columns, axis=1)
    listed = jnp.take_along_axis(picks, placing, axis=1)
    list_ids = jnp.arange(DEVICES * N_SERVER)[:, None]
    topmost = (list_ids < N_SERVER) & (counts[:, None] == CAP) & (columns == CAP - 1)
    listed = jnp.where(topmost, ROWS_DEV - 1, listed)
    return jnp.where(columns < counts[:, None], listed, 0).astype(jnp.int32)


def draw_feature_slot(key, part):
    counts = live_counts(key)
    totals = jnp.sum(counts, axis=1)
    base_key = jax.random.fold_in(key, 37)
    picked = jax.random.randint(jax.random.fold_in(base_key, 1), (DEVICES, B_DEV * FIELDS), 0, totals[:, None])
    limits = jnp.cumsum(counts, axis=1)
    owner_ids = jax.vmap(lambda bounds, drawn: jnp.searchsorted(bounds, drawn, side='right'))(limits, picked)
    before = jnp.take_along_axis(limits - counts, owner_ids, axis=1)
    slot_ids = owner_ids * CAP + picked - before
    return slot_ids.reshape(DEVICES * B_DEV, FIELDS).astype(jnp.int32)


def with_ends(entries, own_key, low, top_value):
    longest = entries.shape.index(max(entries.shape))
    spots = []
    for shift in (0, 1):
        where = [jax.random.randint(jax.random.fold_in(own_key, axis), (), 0, length) for axis, length in enumerate(entries.shape)]
        where[longest] = (where[longest] + shift) % entries.shape[longest]
        spots.append(tuple(where))
    return entries.at[spots[0]].set(low).at[spots[1]].set(top_value)


def levels(stream_key, shape, split, low, top_value):
    def one(position, blocks):
        steps = jax.random.uniform(jax.random.fold_in(jax.random.fold_in(stream_key, 6), position), (blocks,), jnp.float32, low / len(split), top_value / len(split))
        return jnp.repeat(jnp.exp(steps), shape[position] // blocks).reshape((-1,) + (1,) * (len(shape) - position - 1))

    factor_of = one(*split[0])
    for cut in split[1:]:
        factor_of = factor_of * one(*cut)
    return factor_of


def centred(key, dims, deviation, reach, shards=(), held_as=jnp.bfloat16):
    entries = deviation * jax.random.normal(key, dims, jnp.float32)
    if shards:
        entries = entries * levels(key, dims, shards, -0.22, 0.18)
    return jnp.clip(entries, -reach, reach).astype(held_as)


def setup_inputs(seed: int = 0) -> dict:
    splits = jax.random.split(jax.random.key(seed), 8)
    return {
        "factors": centred(splits[0], (TABLE_ROWS, K), 0.05, 0.3, ((0, 32),), jnp.float32),
        "linear": centred(splits[1], (TABLE_ROWS,), 0.1, 0.6, ((0, 32),), jnp.float32),
        "acc_factors": jnp.clip(jnp.exp(math.log(20.0) - 3.6888795 * jax.random.uniform(splits[2], (TABLE_ROWS, K), jnp.float32) ** levels(splits[2], (TABLE_ROWS, K), ((0, 512),), -0.2, 0.2)), 0.5, 20.0),
        "acc_linear": jnp.clip(jnp.exp(math.log(300.0) - 3.4011974 * jax.random.uniform(splits[3], (TABLE_ROWS,), jnp.float32) ** levels(splits[3], (TABLE_ROWS,), ((0, 512),), -0.2, 0.2)), 10.0, 300.0),
        "feature_slot": draw_feature_slot(jax.random.fold_in(splits[7], 71), 0),
        "requests": draw_requests(jax.random.fold_in(splits[7], 71), 0),
        "clicks": with_ends(jax.random.randint(splits[6], (SAMPLES,), 0, 2), jax.random.fold_in(splits[6], 1), 0, 1).astype(jnp.int32),
    }


step_size = 0.5

def reference(factors, linear, acc_factors, acc_linear, feature_slot, requests, clicks):
    slot_blocks = feature_slot.reshape(DEVICES, B_DEV, FIELDS).astype(jnp.int32)
    request_blocks = requests.reshape(DEVICES, N_SERVER, CAP).astype(jnp.int32)
    label_blocks = clicks.reshape(DEVICES, B_DEV).astype(jnp.float32)
    owner_base = (jnp.arange(N_SERVER, dtype=jnp.int32) * ROWS_DEV)[:, None]

    def device_step(totals, inputs):
        grad_rows, grad_linear = totals
        slot_ids, asked_rows, labels = inputs
        row_ids = (asked_rows + owner_base).reshape(-1).astype(jnp.int32)
        pulled_rows = factors[row_ids].astype(jnp.bfloat16)
        pulled_lin = linear[row_ids].astype(jnp.bfloat16)
        vectors = pulled_rows.astype(jnp.float32)[slot_ids]
        factor_sums = lax.optimization_barrier(jnp.sum(vectors, axis=1))
        squares = lax.optimization_barrier(jnp.sum(vectors * vectors, axis=(1, 2)))
        linear_part = lax.optimization_barrier(jnp.sum(pulled_lin.astype(jnp.float32)[slot_ids], axis=1))
        logits = linear_part + 0.5 * (lax.optimization_barrier(jnp.sum(factor_sums * factor_sums, axis=1)) - squares)
        errors = jax.nn.sigmoid(logits) - labels
        weighted = (errors[:, None] * factor_sums).astype(jnp.bfloat16)
        weighted = lax.optimization_barrier(weighted).astype(jnp.float32)
        per_slot = weighted[:, None, :] - errors[:, None, None] * vectors
        targets = row_ids[slot_ids].reshape(-1)
        grad_rows = grad_rows.at[targets].add(per_slot.reshape(-1, K))
        grad_linear = grad_linear.at[targets].add(jnp.broadcast_to(errors[:, None], slot_ids.shape).reshape(-1))
        return ((grad_rows, grad_linear), None)
    start_totals = (jnp.zeros((TABLE_ROWS, K), jnp.float32), jnp.zeros((TABLE_ROWS,), jnp.float32))
    (factor_grad, linear_grad), unused = lax.scan(device_step, start_totals, (slot_blocks, request_blocks, label_blocks))
    new_acc_factors = acc_factors + factor_grad * factor_grad
    new_acc_linear = acc_linear + linear_grad * linear_grad
    new_factors = factors - step_size * factor_grad / jnp.sqrt(new_acc_factors)
    new_linear = linear - step_size * linear_grad / jnp.sqrt(new_acc_linear)
    return (new_factors, new_linear, new_acc_factors, new_acc_linear)
```

```python
import jax
import jax.numpy as jnp
from jax import lax
from jax.experimental import pallas as pl
from jax.experimental.pallas import tpu as pltpu
from jax.sharding import Mesh, PartitionSpec as P

step_size = 0.5
bf16 = jnp.bfloat16
f32 = jnp.float32

OWNERS = 32
CAP = 16
SLOTS = OWNERS * CAP
ROWS = 512
K = 256
WIDE = K + 128
SAMPLES = 256
FIELDS = 39
N_Y = 8
N_CORE = 2
N_WORKER = N_Y * N_CORE
SHARE = ROWS // N_WORKER


def iota(shape, axis):
    return lax.broadcasted_iota(jnp.int32, shape, axis)


def dot(a, b, ca=1, cb=0):
    return lax.dot_general(a, b, (((ca,), (cb,)), ((), ())), preferred_element_type=f32)


def parts(x, lanes):
    first = x.astype(bf16).astype(f32)
    rest = x - first
    second = rest.astype(bf16).astype(f32)
    third = rest - second
    out = jnp.where(lanes == 0, first, jnp.where(lanes == 1, second, jnp.where(lanes == 2, third, 0.0)))
    return out.astype(bf16)


def split_requests(req_t):
    high = jnp.bitwise_and(req_t, -16)
    low = jnp.bitwise_and(req_t, 15)
    pad = jnp.zeros((96, OWNERS), jnp.int32)
    return jnp.concatenate([high, low, pad], axis=0).astype(f32).astype(bf16)


def pick_slot(a, slot_axis):
    place_axis = 1 - slot_axis
    place = iota(a.shape, place_axis)
    position = jnp.bitwise_and(iota(a.shape, slot_axis), CAP - 1)
    keep = (place < 2 * CAP) & (jnp.bitwise_and(place, CAP - 1) == position)
    return jnp.sum(jnp.where(keep, a, 0.0), axis=place_axis, keepdims=True)


def ask_kernel(req_t_ref, lin_ref, out_ref):
    lists = split_requests(req_t_ref[...])
    block = jnp.right_shift(iota((8 * OWNERS, OWNERS), 0), 3)
    sub = jnp.bitwise_and(iota((8 * OWNERS, OWNERS), 0), 7)
    to_owner = (block == iota((8 * OWNERS, OWNERS), 1)) & (sub == 4)
    lin = lin_ref[...].astype(bf16)
    sub4 = jnp.bitwise_and(iota((8 * OWNERS, 4), 0), 7)
    spread = sub4 == iota((8 * OWNERS, 4), 1)
    out = dot(to_owner.astype(f32).astype(bf16), lists, 1, 1) + dot(spread.astype(f32).astype(bf16), lin)
    out_ref[...] = out.reshape(OWNERS, 8, 128)


def count_kernel(fs_t_ref, clicks_ref, counts_t_ref, counts_ref, clicks_col_ref):
    chunk = 64

    def one(i, carry):
        base = pl.multiple_of(i * chunk, chunk)
        slots = iota((chunk, SAMPLES), 0) + base
        total = jnp.zeros((chunk, SAMPLES), f32)
        for f in range(FIELDS):
            total = total + jnp.where(fs_t_ref[pl.ds(f, 1), :] == slots, 1.0, 0.0)
        counts_t_ref[pl.ds(base, chunk), :] = total.astype(bf16)
        return carry

    lax.fori_loop(0, SLOTS // chunk, one, 0)
    counts_ref[...] = jnp.transpose(counts_t_ref[...].astype(f32)).astype(bf16)
    same = iota((SAMPLES, SAMPLES), 0) == iota((SAMPLES, SAMPLES), 1)
    clicks = clicks_ref[...].astype(f32)
    clicks_col_ref[...] = jnp.sum(jnp.where(same, clicks, 0.0), axis=1, keepdims=True)


def asked_rows_matrix(got):
    owner = jnp.right_shift(iota((SLOTS, 8 * OWNERS), 0), 4)
    pick = (owner * 8 + 4 == iota((SLOTS, 8 * OWNERS), 1)).astype(f32).astype(bf16)
    return pick_slot(dot(pick, got), 0)


def gather_kernel(got_ref, factors_ref, out_ref):
    got = got_ref[...].reshape(8 * OWNERS, 128).astype(bf16)
    asked = asked_rows_matrix(got)
    hot = (asked == iota((SLOTS, ROWS), 1).astype(f32)).astype(f32).astype(bf16)
    found = dot(hot, factors_ref[...].astype(bf16))
    out_ref[...] = found.astype(bf16).reshape(OWNERS, CAP, K)


def side_kernel(got_ref, req_t_ref, lin_ref, hot_t_ref):
    got = got_ref[...].reshape(8 * OWNERS, 128).astype(bf16)
    lists = split_requests(req_t_ref[...])
    owner = jnp.right_shift(iota((SLOTS, OWNERS), 0), 4)
    mine = (owner == iota((SLOTS, OWNERS), 1)).astype(f32).astype(bf16)
    wanted = pick_slot(dot(mine, lists, 1, 1), 0)
    block = jnp.right_shift(iota((SLOTS, 8 * OWNERS), 0), 4) * 8
    column = iota((SLOTS, 8 * OWNERS), 1)
    lanes = iota((SLOTS, 128), 1).astype(f32)
    total = jnp.zeros((SLOTS, 128), f32)
    for k in range(4):
        pick = (block + k == column).astype(f32).astype(bf16)
        values = dot(pick, got)
        total = total + jnp.where(wanted == lanes + 128.0 * k, values, 0.0)
    lin_ref[...] = jnp.sum(total, axis=1, keepdims=True)
    owner_t = jnp.right_shift(iota((8 * OWNERS, SLOTS), 1), 4)
    pick_t = (owner_t * 8 + 4 == iota((8 * OWNERS, SLOTS), 0)).astype(f32).astype(bf16)
    asked_t = pick_slot(dot(got, pick_t, 0, 0), 1)
    hot_t_ref[...] = (asked_t == iota((ROWS, SLOTS), 0).astype(f32)).astype(f32).astype(bf16)


def learn_kernel(rows_ref, counts_ref, counts_t_ref, clicks_ref, lin_ref, out_ref):
    rows = rows_ref[...].reshape(SLOTS, K)
    wide_rows = rows.astype(f32)
    counts = counts_ref[...]
    sums = dot(counts, rows)
    norms = jnp.sum(wide_rows * wide_rows, axis=1, keepdims=True)
    lanes = iota((SLOTS, 128), 1)
    terms = parts(lin_ref[...] - 0.5 * norms, lanes)
    base = jnp.sum(dot(counts, terms), axis=1, keepdims=True)
    logits = base + 0.5 * jnp.sum(sums * sums, axis=1, keepdims=True)
    errors = jax.nn.sigmoid(logits) - clicks_ref[...]
    weighted = (errors * sums).astype(bf16)
    error_parts = parts(errors, iota((SAMPLES, 128), 1))
    counts_t = counts_t_ref[...]
    gathered = dot(counts_t, weighted)
    error_sums = jnp.sum(dot(counts_t, error_parts), axis=1, keepdims=True)
    grads = gathered - error_sums * wide_rows
    out_ref[:, :, :K] = grads.astype(bf16).reshape(OWNERS, CAP, K)
    out_ref[:, :, K:] = parts(error_sums, lanes).reshape(OWNERS, CAP, 128)


def scatter_kernel(push_ref, hot_t_ref, out_ref):
    pushed = push_ref[...].reshape(SLOTS, WIDE)
    total = dot(hot_t_ref[...], pushed)
    linear = jnp.sum(total[:, K:], axis=1, keepdims=True)
    out_ref[:, :, :K] = total[:, :K].astype(bf16).reshape(N_WORKER, SHARE, K)
    out_ref[:, :, K:] = parts(linear, iota((ROWS, 128), 1)).reshape(N_WORKER, SHARE, 128)


def update_kernel(part_ref, acc_ref, acc_lin_ref, delta_ref, new_acc_ref, new_acc_lin_ref):
    total = part_ref[0].astype(f32)
    for w in range(1, N_WORKER):
        total = total + part_ref[w].astype(f32)
    grad = total[:, :K]
    grad_lin = jnp.sum(total[:, K:], axis=1, keepdims=True)
    state = acc_ref[...] + grad * grad
    new_acc_ref[...] = state
    delta = (step_size * grad / jnp.sqrt(state)).astype(bf16)
    same = iota((SHARE, SHARE), 0) == iota((SHARE, SHARE), 1)
    acc_lin = jnp.sum(jnp.where(same, acc_lin_ref[...], 0.0), axis=1, keepdims=True)
    state_lin = acc_lin + grad_lin * grad_lin
    new_acc_lin_ref[...] = jnp.sum(jnp.where(same, state_lin, 0.0), axis=0, keepdims=True)
    delta_lin = parts(step_size * grad_lin / jnp.sqrt(state_lin), iota((SHARE, 128), 1))
    for y in range(N_Y):
        delta_ref[y, :, :K] = delta
        delta_ref[y, :, K:] = delta_lin


def apply_kernel(delta_ref, factors_ref, linear_ref, new_factors_ref, new_linear_ref):
    lin = jnp.zeros((1, ROWS), f32)
    place = iota((SHARE, ROWS), 1) - iota((SHARE, ROWS), 0)
    for y in range(N_Y):
        for c in range(N_CORE):
            first = (y * N_CORE + c) * SHARE
            block = delta_ref[c * N_Y + y]
            here = pl.ds(first, SHARE)
            new_factors_ref[here, :] = factors_ref[here, :] - block[:, :K].astype(f32)
            step = jnp.sum(block[:, K:].astype(f32), axis=1, keepdims=True)
            lin = lin + jnp.sum(jnp.where(place == first, step, 0.0), axis=0, keepdims=True)
    new_linear_ref[...] = linear_ref[...] - lin


def call(kernel, out, flops, *args):
    size = sum(a.size * a.dtype.itemsize for a in args)
    return pl.pallas_call(
        kernel,
        out_shape=out,
        in_specs=[pl.BlockSpec(memory_space=pltpu.VMEM)] * len(args),
        out_specs=jax.tree.map(lambda _: pl.BlockSpec(memory_space=pltpu.VMEM), out),
        compiler_params=pltpu.CompilerParams(vmem_limit_bytes=24 * 1024 * 1024),
        cost_estimate=pl.CostEstimate(flops=flops, bytes_accessed=size, transcendentals=0),
    )(*args)


def shape(dims, dtype):
    return jax.ShapeDtypeStruct(dims, dtype)


def exchange(x, axis):
    return lax.all_to_all(x, axis, split_axis=0, concat_axis=0, tiled=True)


def body(factors, linear, acc_factors, acc_linear, feature_slot, requests, clicks):
    req_t = requests.T
    ask = call(ask_kernel, shape((OWNERS, 8, 128), f32), 1 << 20, req_t, linear.reshape(4, 128))
    got = exchange(ask, "server")
    counts_t, counts, clicks_col = call(
        count_kernel,
        [shape((SLOTS, SAMPLES), bf16), shape((SAMPLES, SLOTS), bf16), shape((SAMPLES, 1), f32)],
        1 << 30,
        feature_slot.T,
        clicks.reshape(1, SAMPLES),
    )
    found = call(gather_kernel, shape((OWNERS, CAP, K), bf16), 1 << 28, got, factors)
    rows = exchange(found, "server")
    lin_col, hot_t = call(
        side_kernel, [shape((SLOTS, 1), f32), shape((ROWS, SLOTS), bf16)], 1 << 28, got, req_t
    )
    push = call(
        learn_kernel,
        shape((OWNERS, CAP, WIDE), bf16),
        1 << 28,
        rows,
        counts,
        counts_t,
        clicks_col,
        lin_col,
    )
    pushed = exchange(push, "server")
    dense = call(scatter_kernel, shape((N_WORKER, SHARE, WIDE), bf16), 1 << 28, pushed, hot_t)
    shared = exchange(dense, ("y", "core"))
    delta, new_acc, new_acc_lin = call(
        update_kernel,
        [shape((N_Y, SHARE, WIDE), bf16), shape((SHARE, K), f32), shape((1, SHARE), f32)],
        1 << 20,
        shared,
        acc_factors,
        acc_linear.reshape(1, SHARE),
    )
    deltas = exchange(delta, "y")
    deltas = lax.all_gather(deltas, "core", axis=0, tiled=True)
    new_factors, new_linear = call(
        apply_kernel,
        [shape((ROWS, K), f32), shape((1, ROWS), f32)],
        1 << 20,
        deltas,
        factors,
        linear.reshape(1, ROWS),
    )
    return new_factors, new_linear.reshape(ROWS), new_acc, new_acc_lin.reshape(SHARE)


def solution(mesh):
    mesh = Mesh(mesh.devices.reshape(OWNERS, N_Y, N_CORE), ("server", "y", "core"))
    every = ("server", "y", "core")
    in_specs = (
        P("server", None),
        P("server"),
        P(every, None),
        P(every),
        P(every, None),
        P(every, None),
        P(every),
    )
    out_specs = (P("server", None), P("server"), P(every, None), P(every))
    return jax.shard_map(body, mesh=mesh, in_specs=in_specs, out_specs=out_specs, check_vma=False)
```

```python
import jax
import jax.numpy as jnp
from jax import lax
from jax.experimental import pallas as pl
from jax.experimental.pallas import tpu as pltpu
from jax.sharding import Mesh, PartitionSpec as P

step_size = 0.5
bf16 = jnp.bfloat16
f32 = jnp.float32

OWNERS = 32
CAP = 16
SLOTS = OWNERS * CAP
ROWS = 512
K = 256
WIDE = K + 128
SAMPLES = 256
FIELDS = 39
N_Y = 8
N_CORE = 2
N_WORKER = N_Y * N_CORE
SHARE = ROWS // N_WORKER


def iota(shape, axis):
    return lax.broadcasted_iota(jnp.int32, shape, axis)


def dot(a, b, ca=1, cb=0):
    return lax.dot_general(a, b, (((ca,), (cb,)), ((), ())), preferred_element_type=f32)


def parts(x, lanes):
    first = x.astype(bf16).astype(f32)
    rest = x - first
    second = rest.astype(bf16).astype(f32)
    third = rest - second
    out = jnp.where(lanes == 0, first, jnp.where(lanes == 1, second, jnp.where(lanes == 2, third, 0.0)))
    return out.astype(bf16)


def split_requests(req_t):
    high = jnp.bitwise_and(req_t, -16)
    low = jnp.bitwise_and(req_t, 15)
    pad = jnp.zeros((96, OWNERS), jnp.int32)
    return jnp.concatenate([high, low, pad], axis=0).astype(f32).astype(bf16)


def pick_slot(a, slot_axis):
    place_axis = 1 - slot_axis
    place = iota(a.shape, place_axis)
    position = jnp.bitwise_and(iota(a.shape, slot_axis), CAP - 1)
    keep = (place < 2 * CAP) & (jnp.bitwise_and(place, CAP - 1) == position)
    return jnp.sum(jnp.where(keep, a, 0.0), axis=place_axis, keepdims=True)


def ask_kernel(req_t_hbm, lin_hbm, out_ref, req_t_ref, lin_ref, sems):
    copies = [
        pltpu.make_async_copy(req_t_hbm, req_t_ref, sems.at[0]),
        pltpu.make_async_copy(lin_hbm, lin_ref, sems.at[1]),
    ]
    for copy in copies:
        copy.start()
    block = jnp.right_shift(iota((8 * OWNERS, OWNERS), 0), 3)
    sub = jnp.bitwise_and(iota((8 * OWNERS, OWNERS), 0), 7)
    to_owner = (block == iota((8 * OWNERS, OWNERS), 1)) & (sub == 4)
    sub4 = jnp.bitwise_and(iota((8 * OWNERS, 4), 0), 7)
    spread = sub4 == iota((8 * OWNERS, 4), 1)
    for copy in copies:
        copy.wait()
    lists = split_requests(req_t_ref[...])
    lin = lin_ref[...].astype(bf16)
    out = dot(to_owner.astype(f32).astype(bf16), lists, 1, 1) + dot(spread.astype(f32).astype(bf16), lin)
    out_ref[...] = out.reshape(OWNERS, 8, 128)


def prep_kernel(
    fs_t_ref,
    clicks_ref,
    req_t_in,
    factors_in,
    acc_in,
    acc_lin_row_ref,
    linear_in,
    counts_t_ref,
    counts_ref,
    clicks_col_ref,
    req_t_ref,
    factors_ref,
    narrow_ref,
    acc_ref,
    acc_lin_ref,
    linear_ref,
):
    for here, there in (
        (req_t_in, req_t_ref),
        (factors_in, factors_ref),
        (acc_in, acc_ref),
        (linear_in, linear_ref),
    ):
        there[...] = here[...]
    narrow_ref[...] = factors_in[...].astype(bf16)
    same_share = iota((SHARE, SHARE), 0) == iota((SHARE, SHARE), 1)
    acc_lin = jnp.sum(jnp.where(same_share, acc_lin_row_ref[...], 0.0), axis=1, keepdims=True)
    acc_lin_ref[...] = jnp.sum(jnp.where(of_share(), acc_lin, 0.0), axis=0, keepdims=True)
    chunk = 64

    def one(i, carry):
        base = pl.multiple_of(i * chunk, chunk)
        slots = iota((chunk, SAMPLES), 0) + base
        total = jnp.zeros((chunk, SAMPLES), f32)
        for f in range(FIELDS):
            total = total + jnp.where(fs_t_ref[pl.ds(f, 1), :] == slots, 1.0, 0.0)
        counts_t_ref[pl.ds(base, chunk), :] = total.astype(bf16)
        return carry

    lax.fori_loop(0, SLOTS // chunk, one, 0)
    counts_ref[...] = jnp.transpose(counts_t_ref[...].astype(f32)).astype(bf16)
    same = iota((SAMPLES, SAMPLES), 0) == iota((SAMPLES, SAMPLES), 1)
    clicks = clicks_ref[...].astype(f32)
    clicks_col_ref[...] = jnp.sum(jnp.where(same, clicks, 0.0), axis=1, keepdims=True)


def of_share():
    return jnp.bitwise_and(iota((SHARE, 128), 1), SHARE - 1) == iota((SHARE, 128), 0)


def asked_rows_matrix(got):
    owner = jnp.right_shift(iota((SLOTS, 8 * OWNERS), 0), 4)
    pick = (owner * 8 + 4 == iota((SLOTS, 8 * OWNERS), 1)).astype(f32).astype(bf16)
    return pick_slot(dot(pick, got), 0)


def gather_kernel(got_ref, narrow_ref, out_ref):
    got = got_ref[...].reshape(8 * OWNERS, 128).astype(bf16)
    asked = asked_rows_matrix(got)
    hot = (asked == iota((SLOTS, ROWS), 1).astype(f32)).astype(f32).astype(bf16)
    found = dot(hot, narrow_ref[...])
    out_ref[...] = found.astype(bf16).reshape(OWNERS, CAP, K)


def side_kernel(got_ref, req_t_ref, lin_ref, hot_t_ref):
    got = got_ref[...].reshape(8 * OWNERS, 128).astype(bf16)
    lists = split_requests(req_t_ref[...])
    owner = jnp.right_shift(iota((SLOTS, OWNERS), 0), 4)
    mine = (owner == iota((SLOTS, OWNERS), 1)).astype(f32).astype(bf16)
    wanted = pick_slot(dot(mine, lists, 1, 1), 0)
    block = jnp.right_shift(iota((SLOTS, 8 * OWNERS), 0), 4) * 8
    column = iota((SLOTS, 8 * OWNERS), 1)
    lanes = iota((SLOTS, 128), 1).astype(f32)
    total = jnp.zeros((SLOTS, 128), f32)
    for k in range(4):
        pick = (block + k == column).astype(f32).astype(bf16)
        values = dot(pick, got)
        total = total + jnp.where(wanted == lanes + 128.0 * k, values, 0.0)
    lin_ref[...] = jnp.sum(total, axis=1, keepdims=True)
    owner_t = jnp.right_shift(iota((8 * OWNERS, SLOTS), 1), 4)
    pick_t = (owner_t * 8 + 4 == iota((8 * OWNERS, SLOTS), 0)).astype(f32).astype(bf16)
    asked_t = pick_slot(dot(got, pick_t, 0, 0), 1)
    hot_t_ref[...] = (asked_t == iota((ROWS, SLOTS), 0).astype(f32)).astype(f32).astype(bf16)


def learn_kernel(rows_ref, counts_ref, counts_t_ref, clicks_ref, lin_ref, out_ref):
    rows = rows_ref[...].reshape(SLOTS, K)
    wide_rows = rows.astype(f32)
    counts = counts_ref[...]
    sums = dot(counts, rows)
    norms = jnp.sum(wide_rows * wide_rows, axis=1, keepdims=True)
    lanes = iota((SLOTS, 128), 1)
    terms = parts(lin_ref[...] - 0.5 * norms, lanes)
    base = jnp.sum(dot(counts, terms), axis=1, keepdims=True)
    logits = base + 0.5 * jnp.sum(sums * sums, axis=1, keepdims=True)
    errors = jax.nn.sigmoid(logits) - clicks_ref[...]
    weighted = (errors * sums).astype(bf16)
    error_parts = parts(errors, iota((SAMPLES, 128), 1))
    counts_t = counts_t_ref[...]
    gathered = dot(counts_t, weighted)
    error_sums = jnp.sum(dot(counts_t, error_parts), axis=1, keepdims=True)
    grads = gathered - error_sums * wide_rows
    out_ref[:, :, :K] = grads.astype(bf16).reshape(OWNERS, CAP, K)
    out_ref[:, :, K:] = parts(error_sums, lanes).reshape(OWNERS, CAP, 128)


def part_rows(x):
    rows = iota((8, x.shape[1]), 0)
    first = x.astype(bf16).astype(f32)
    rest = x - first
    second = rest.astype(bf16).astype(f32)
    third = rest - second
    out = jnp.where(rows == 0, first, jnp.where(rows == 1, second, jnp.where(rows == 2, third, 0.0)))
    return out.astype(bf16)


def scatter_kernel(push_ref, hot_t_ref, out_ref):
    pushed = push_ref[...].reshape(SLOTS, WIDE)
    hot_t = hot_t_ref[...]
    total = dot(hot_t, pushed[:, :K]).astype(bf16)
    out_ref[:, :SHARE, :] = total[:, :128].reshape(N_WORKER, SHARE, 128)
    out_ref[:, SHARE : 2 * SHARE, :] = total[:, 128:].reshape(N_WORKER, SHARE, 128)
    linear = part_rows(jnp.sum(dot(pushed[:, K:], hot_t, 0, 1), axis=0, keepdims=True))
    for w in range(N_WORKER):
        lanes = w // 4 * 128
        out_ref[w, 2 * SHARE :, :] = linear[:, lanes : lanes + 128]


def add_parts(part_ref):
    total = part_ref[0].astype(f32)
    for w in range(1, N_WORKER):
        total = total + part_ref[w].astype(f32)
    left, right = total[:SHARE], total[SHARE : 2 * SHARE]
    return left, right, jnp.sum(total[2 * SHARE :], axis=0, keepdims=True)


def my_lanes():
    me = lax.axis_index("y") * N_CORE + lax.axis_index("core")
    return jnp.right_shift(iota((1, 128), 1), 5) == lax.rem(me, 4)


def update_kernel(part_ref, acc_ref, acc_lin_ref, delta_ref):
    left, right, linear = add_parts(part_ref)
    acc = acc_ref[...]

    def step(grad, state):
        return step_size * grad / jnp.sqrt(state + grad * grad)

    left = step(left, acc[:, :128]).astype(bf16)
    right = step(right, acc[:, 128:]).astype(bf16)
    linear = part_rows(jnp.where(my_lanes(), step(linear, acc_lin_ref[...]), 0.0))
    for y in range(N_Y):
        delta_ref[y, :SHARE, :] = left
        delta_ref[y, SHARE : 2 * SHARE, :] = right
        delta_ref[y, 2 * SHARE :, :] = linear


def state_kernel(part_ref, acc_ref, acc_lin_ref, new_acc_ref, new_acc_lin_ref):
    left, right, linear = add_parts(part_ref)
    new_acc_ref[:, :128] = acc_ref[:, :128] + left * left
    new_acc_ref[:, 128:] = acc_ref[:, 128:] + right * right
    state = jnp.where(my_lanes(), acc_lin_ref[...] + linear * linear, 0.0)
    column = jnp.sum(jnp.where(of_share(), state, 0.0), axis=1, keepdims=True)
    same = iota((SHARE, SHARE), 0) == iota((SHARE, SHARE), 1)
    new_acc_lin_ref[...] = jnp.sum(jnp.where(same, column, 0.0), axis=0, keepdims=True)


def apply_kernel(delta_ref, factors_ref, linear_ref, new_factors_ref, new_linear_ref):
    for q in range(4):
        lin = jnp.zeros((8, 128), f32)
        for w in range(4 * q, 4 * q + 4):
            block = delta_ref[w % N_CORE * N_Y + w // N_CORE].astype(f32)
            here = pl.ds(w * SHARE, SHARE)
            new_factors_ref[here, :128] = factors_ref[here, :128] - block[:SHARE]
            new_factors_ref[here, 128:] = factors_ref[here, 128:] - block[SHARE : 2 * SHARE]
            lin = lin + block[2 * SHARE :]
        lanes = pl.ds(q * 128, 128)
        new_linear_ref[:, lanes] = linear_ref[:, lanes] - jnp.sum(lin, axis=0, keepdims=True)


def call(kernel, out, flops, *args, scratch=(), far=False):
    size = sum(a.size * a.dtype.itemsize for a in args)
    return pl.pallas_call(
        kernel,
        out_shape=out,
        in_specs=[pl.BlockSpec(memory_space=pltpu.HBM if far else pltpu.VMEM)] * len(args),
        out_specs=jax.tree.map(lambda _: pl.BlockSpec(memory_space=pltpu.VMEM), out),
        scratch_shapes=scratch,
        compiler_params=pltpu.CompilerParams(vmem_limit_bytes=None if far else 24 * 1024 * 1024),
        cost_estimate=pl.CostEstimate(flops=flops, bytes_accessed=size, transcendentals=0),
    )(*args)


def shape(dims, dtype):
    return jax.ShapeDtypeStruct(dims, dtype)


def exchange(x, axis):
    return lax.all_to_all(x, axis, split_axis=0, concat_axis=0, tiled=True)


TALL = 2 * SHARE + 8


def body(factors, linear, acc_factors, acc_linear, feature_slot, requests, clicks):
    dma = pltpu.SemaphoreType.DMA
    ask = call(
        ask_kernel,
        shape((OWNERS, 8, 128), f32),
        1 << 20,
        requests.T,
        linear.reshape(4, 128),
        scratch=[pltpu.VMEM((CAP, OWNERS), jnp.int32), pltpu.VMEM((4, 128), f32), dma((2,))],
        far=True,
    )
    got = exchange(ask, "server")
    counts_t, counts, clicks_col, req_t, wide, narrow, acc, acc_lin, lin_row = call(
        prep_kernel,
        [
            shape((SLOTS, SAMPLES), bf16),
            shape((SAMPLES, SLOTS), bf16),
            shape((SAMPLES, 1), f32),
            shape((CAP, OWNERS), jnp.int32),
            shape((ROWS, K), f32),
            shape((ROWS, K), bf16),
            shape((SHARE, K), f32),
            shape((1, 128), f32),
            shape((1, ROWS), f32),
        ],
        1 << 30,
        feature_slot.T,
        clicks.reshape(1, SAMPLES),
        requests.T,
        factors,
        acc_factors,
        acc_linear.reshape(1, SHARE),
        linear.reshape(1, ROWS),
    )
    found = call(gather_kernel, shape((OWNERS, CAP, K), bf16), 1 << 28, got, narrow)
    rows = exchange(found, "server")
    lin_col, hot_t = call(
        side_kernel, [shape((SLOTS, 1), f32), shape((ROWS, SLOTS), bf16)], 1 << 28, got, req_t
    )
    push = call(
        learn_kernel,
        shape((OWNERS, CAP, WIDE), bf16),
        1 << 28,
        rows,
        counts,
        counts_t,
        clicks_col,
        lin_col,
    )
    pushed = exchange(push, "server")
    dense = call(scatter_kernel, shape((N_WORKER, TALL, 128), bf16), 1 << 28, pushed, hot_t)
    shared = exchange(dense, ("y", "core"))
    delta = call(update_kernel, shape((N_Y, TALL, 128), bf16), 1 << 20, shared, acc, acc_lin)
    deltas = exchange(delta, "y")
    new_acc, new_acc_lin = call(
        state_kernel, [shape((SHARE, K), f32), shape((1, SHARE), f32)], 1 << 20, shared, acc, acc_lin
    )
    deltas = lax.all_gather(deltas, "core", axis=0, tiled=True)
    new_factors, new_linear = call(
        apply_kernel, [shape((ROWS, K), f32), shape((1, ROWS), f32)], 1 << 20, deltas, wide, lin_row
    )
    return new_factors, new_linear.reshape(ROWS), new_acc, new_acc_lin.reshape(SHARE)


def solution(mesh):
    mesh = Mesh(mesh.devices.reshape(OWNERS, N_Y, N_CORE), ("server", "y", "core"))
    every = ("server", "y", "core")
    in_specs = (
        P("server", None),
        P("server"),
        P(every, None),
        P(every),
        P(every, None),
        P(every, None),
        P(every),
    )
    out_specs = (P("server", None), P("server"), P(every, None), P(every))
    return jax.shard_map(body, mesh=mesh, in_specs=in_specs, out_specs=out_specs, check_vma=False)
```

```python
import jax
import jax.numpy as jnp
from jax import lax
from jax.experimental import pallas as pl
from jax.experimental.pallas import tpu as pltpu
from jax.sharding import Mesh, PartitionSpec as P

step_size = 0.5
bf16 = jnp.bfloat16
f32 = jnp.float32

OWNERS = 32
CAP = 16
SLOTS = OWNERS * CAP
ROWS = 512
K = 256
WIDE = K + 128
SAMPLES = 256
FIELDS = 39
N_Y = 8
N_CORE = 2
N_WORKER = N_Y * N_CORE
SHARE = ROWS // N_WORKER


def iota(shape, axis):
    return lax.broadcasted_iota(jnp.int32, shape, axis)


def dot(a, b, ca=1, cb=0):
    return lax.dot_general(a, b, (((ca,), (cb,)), ((), ())), preferred_element_type=f32)


def split_requests(req_t):
    high = jnp.bitwise_and(req_t, -16)
    low = jnp.bitwise_and(req_t, 15)
    pad = jnp.zeros((96, OWNERS), jnp.int32)
    return jnp.concatenate([high, low, pad], axis=0).astype(f32).astype(bf16)


def own_lists(req_t):
    owner = jnp.right_shift(iota((SLOTS, OWNERS), 0), 4)
    mine = (owner == iota((SLOTS, OWNERS), 1)).astype(f32).astype(bf16)
    lists = dot(mine, split_requests(req_t), 1, 1)
    lane = iota((SLOTS, 128), 1)
    position = jnp.bitwise_and(iota((SLOTS, 128), 0), CAP - 1)
    keep = (lane < 2 * CAP) & (jnp.bitwise_and(lane, CAP - 1) == position)
    return jnp.where(keep, lists, 0.0)


def ones(dims, axis):
    return (iota(dims, axis) < 2 * CAP).astype(f32).astype(bf16)


def ask_kernel(req_t_hbm, lin_hbm, out_ref, req_t_ref, lin_ref, sems):
    copies = [
        pltpu.make_async_copy(req_t_hbm, req_t_ref, sems.at[0]),
        pltpu.make_async_copy(lin_hbm, lin_ref, sems.at[1]),
    ]
    for copy in copies:
        copy.start()
    for copy in copies:
        copy.wait()
    lists = own_lists(req_t_ref[...])
    spread = (jnp.right_shift(iota((CAP, 4), 0), 1) == iota((CAP, 4), 1)).astype(f32).astype(bf16)
    lin = dot(spread, lin_ref[...].astype(bf16))
    odd = jnp.bitwise_and(iota((CAP, 128), 0), 1) == 1
    lin = jnp.where(odd, lin, pltpu.roll(lin, 64, 1))
    lin = jnp.where(iota((CAP, 128), 1) >= 64, lin, 0.0)
    out_ref[...] = (lists.reshape(OWNERS, CAP, 128) + lin[None]).astype(bf16)


def prep_kernel(
    fs_t_ref,
    clicks_ref,
    req_t_in,
    factors_in,
    acc_in,
    acc_lin_row_ref,
    linear_in,
    counts_t_ref,
    counts_ref,
    clicks_col_ref,
    req_t_ref,
    factors_ref,
    narrow_ref,
    acc_ref,
    acc_lin_ref,
    linear_ref,
):
    for here, there in (
        (req_t_in, req_t_ref),
        (factors_in, factors_ref),
        (acc_in, acc_ref),
        (linear_in, linear_ref),
    ):
        there[...] = here[...]
    narrow_ref[...] = factors_in[...].astype(bf16)
    same_share = iota((SHARE, SHARE), 0) == iota((SHARE, SHARE), 1)
    acc_lin = jnp.sum(jnp.where(same_share, acc_lin_row_ref[...], 0.0), axis=1, keepdims=True)
    acc_lin_ref[...] = jnp.sum(jnp.where(of_share(), acc_lin, 0.0), axis=0, keepdims=True)
    chunk = 64

    def one(i, carry):
        base = pl.multiple_of(i * chunk, chunk)
        slots = iota((chunk, SAMPLES), 0) + base
        total = jnp.zeros((chunk, SAMPLES), f32)
        for f in range(FIELDS):
            total = total + jnp.where(fs_t_ref[pl.ds(f, 1), :] == slots, 1.0, 0.0)
        counts_t_ref[pl.ds(base, chunk), :] = total.astype(bf16)
        return carry

    lax.fori_loop(0, SLOTS // chunk, one, 0)
    counts_ref[...] = jnp.transpose(counts_t_ref[...].astype(f32)).astype(bf16)
    same = iota((SAMPLES, SAMPLES), 0) == iota((SAMPLES, SAMPLES), 1)
    clicks = clicks_ref[...].astype(f32)
    clicks_col_ref[...] = jnp.sum(jnp.where(same, clicks, 0.0), axis=1, keepdims=True)


def of_share():
    return jnp.bitwise_and(iota((SHARE, 128), 1), SHARE - 1) == iota((SHARE, 128), 0)


def gather_kernel(got_ref, narrow_ref, out_ref):
    asked = dot(got_ref[...].reshape(SLOTS, 128), ones((128, ROWS), 0))
    hot = (asked == iota((SLOTS, ROWS), 1).astype(f32)).astype(f32).astype(bf16)
    out_ref[...] = dot(hot, narrow_ref[...]).astype(bf16).reshape(OWNERS, CAP, K)


def side_kernel(got_ref, req_t_ref, lin_ref, hot_t_ref):
    got = got_ref[...].reshape(SLOTS, 128)
    wanted = dot(own_lists(req_t_ref[...]).astype(bf16), ones((128, SLOTS), 0)).astype(jnp.int32)
    first = jnp.bitwise_and(iota((SLOTS, SLOTS), 0), -CAP)
    pick = iota((SLOTS, SLOTS), 1) == first + jnp.right_shift(wanted, 6)
    values = dot(pick.astype(f32).astype(bf16), got)
    here = iota((SLOTS, 128), 1) == jnp.bitwise_and(wanted[:, :128], 63) + 64
    lin_ref[...] = jnp.where(here, values, 0.0).astype(bf16)
    asked_t = dot(ones((ROWS, 128), 1), got, 1, 1)
    hot_t_ref[...] = (asked_t == iota((ROWS, SLOTS), 0).astype(f32)).astype(f32).astype(bf16)


def learn_kernel(rows_ref, counts_ref, counts_t_ref, clicks_ref, lin_ref, out_ref):
    rows = rows_ref[...].reshape(SLOTS, K)
    wide_rows = rows.astype(f32)
    counts = counts_ref[...]
    sums = dot(counts, rows)
    square = wide_rows * wide_rows
    high = square.astype(bf16)
    low = (square - high.astype(f32)).astype(bf16)
    terms = sums * sums - dot(counts, high) - dot(counts, low)
    terms = 0.5 * (terms[:, :128] + terms[:, 128:]) + dot(counts, lin_ref[...])
    logits = jnp.sum(terms, axis=1, keepdims=True)
    errors = jnp.broadcast_to(jax.nn.sigmoid(logits) - clicks_ref[...], (SAMPLES, K))
    weighted = (errors * sums).astype(bf16)
    first = errors.astype(bf16)
    second = (errors - first.astype(f32)).astype(bf16)
    counts_t = counts_t_ref[...]
    error_sums = dot(counts_t, first) + dot(counts_t, second)
    grads = dot(counts_t, weighted) - error_sums * wide_rows
    out_ref[:, :, :K] = grads.astype(bf16).reshape(OWNERS, CAP, K)
    total = error_sums[:, :128]
    lane = iota((SLOTS, 128), 1)
    first = total.astype(bf16).astype(f32)
    linear = jnp.where(lane == 0, first, jnp.where(lane == 1, total - first, 0.0))
    out_ref[:, :, K:] = linear.astype(bf16).reshape(OWNERS, CAP, 128)


def part_rows(x):
    rows = iota((8, x.shape[1]), 0)
    first = x.astype(bf16).astype(f32)
    rest = x - first
    second = rest.astype(bf16).astype(f32)
    third = rest - second
    out = jnp.where(rows == 0, first, jnp.where(rows == 1, second, jnp.where(rows == 2, third, 0.0)))
    return out.astype(bf16)


def scatter_kernel(push_ref, hot_t_ref, out_ref):
    pushed = push_ref[...].reshape(SLOTS, WIDE)
    hot_t = hot_t_ref[...]
    total = dot(hot_t, pushed[:, :K]).astype(bf16)
    out_ref[:, :SHARE, :] = total[:, :128].reshape(N_WORKER, SHARE, 128)
    out_ref[:, SHARE : 2 * SHARE, :] = total[:, 128:].reshape(N_WORKER, SHARE, 128)
    linear = part_rows(jnp.sum(dot(pushed[:, K:], hot_t, 0, 1), axis=0, keepdims=True))
    for w in range(N_WORKER):
        lanes = w // 4 * 128
        out_ref[w, 2 * SHARE :, :] = linear[:, lanes : lanes + 128]


def add_parts(part_ref):
    total = part_ref[0].astype(f32)
    for w in range(1, N_WORKER):
        total = total + part_ref[w].astype(f32)
    left, right = total[:SHARE], total[SHARE : 2 * SHARE]
    return left, right, jnp.sum(total[2 * SHARE :], axis=0, keepdims=True)


def my_lanes():
    me = lax.axis_index("y") * N_CORE + lax.axis_index("core")
    return jnp.right_shift(iota((1, 128), 1), 5) == lax.rem(me, 4)


def update_kernel(part_ref, acc_ref, acc_lin_ref, delta_ref):
    left, right, linear = add_parts(part_ref)
    acc = acc_ref[...]

    def step(grad, state):
        return step_size * grad / jnp.sqrt(state + grad * grad)

    left = step(left, acc[:, :128]).astype(bf16)
    right = step(right, acc[:, 128:]).astype(bf16)
    linear = part_rows(jnp.where(my_lanes(), step(linear, acc_lin_ref[...]), 0.0))
    for y in range(N_Y):
        delta_ref[y, :SHARE, :] = left
        delta_ref[y, SHARE : 2 * SHARE, :] = right
        delta_ref[y, 2 * SHARE :, :] = linear


def state_kernel(part_ref, acc_ref, acc_lin_ref, new_acc_ref, new_acc_lin_ref):
    left, right, linear = add_parts(part_ref)
    new_acc_ref[:, :128] = acc_ref[:, :128] + left * left
    new_acc_ref[:, 128:] = acc_ref[:, 128:] + right * right
    state = jnp.where(my_lanes(), acc_lin_ref[...] + linear * linear, 0.0)
    column = jnp.sum(jnp.where(of_share(), state, 0.0), axis=1, keepdims=True)
    same = iota((SHARE, SHARE), 0) == iota((SHARE, SHARE), 1)
    new_acc_lin_ref[...] = jnp.sum(jnp.where(same, column, 0.0), axis=0, keepdims=True)


def apply_kernel(delta_ref, factors_ref, linear_ref, new_factors_ref, new_linear_ref):
    for q in range(4):
        lin = jnp.zeros((8, 128), f32)
        for w in range(4 * q, 4 * q + 4):
            block = delta_ref[w % N_CORE * N_Y + w // N_CORE].astype(f32)
            here = pl.ds(w * SHARE, SHARE)
            new_factors_ref[here, :128] = factors_ref[here, :128] - block[:SHARE]
            new_factors_ref[here, 128:] = factors_ref[here, 128:] - block[SHARE : 2 * SHARE]
            lin = lin + block[2 * SHARE :]
        lanes = pl.ds(q * 128, 128)
        new_linear_ref[:, lanes] = linear_ref[:, lanes] - jnp.sum(lin, axis=0, keepdims=True)


def call(kernel, out, flops, *args, scratch=(), far=False):
    size = sum(a.size * a.dtype.itemsize for a in args)
    return pl.pallas_call(
        kernel,
        out_shape=out,
        in_specs=[pl.BlockSpec(memory_space=pltpu.HBM if far else pltpu.VMEM)] * len(args),
        out_specs=jax.tree.map(lambda _: pl.BlockSpec(memory_space=pltpu.VMEM), out),
        scratch_shapes=scratch,
        compiler_params=pltpu.CompilerParams(vmem_limit_bytes=None if far else 24 * 1024 * 1024),
        cost_estimate=pl.CostEstimate(flops=flops, bytes_accessed=size, transcendentals=0),
    )(*args)


def shape(dims, dtype):
    return jax.ShapeDtypeStruct(dims, dtype)


def exchange(x, axis):
    return lax.all_to_all(x, axis, split_axis=0, concat_axis=0, tiled=True)


TALL = 2 * SHARE + 8


def body(factors, linear, acc_factors, acc_linear, feature_slot, requests, clicks):
    dma = pltpu.SemaphoreType.DMA
    ask = call(
        ask_kernel,
        shape((OWNERS, CAP, 128), bf16),
        1 << 20,
        requests.T,
        linear.reshape(4, 128),
        scratch=[pltpu.VMEM((CAP, OWNERS), jnp.int32), pltpu.VMEM((4, 128), f32), dma((2,))],
        far=True,
    )
    got = exchange(ask, "server")
    counts_t, counts, clicks_col, req_t, wide, narrow, acc, acc_lin, lin_row = call(
        prep_kernel,
        [
            shape((SLOTS, SAMPLES), bf16),
            shape((SAMPLES, SLOTS), bf16),
            shape((SAMPLES, 1), f32),
            shape((CAP, OWNERS), jnp.int32),
            shape((ROWS, K), f32),
            shape((ROWS, K), bf16),
            shape((SHARE, K), f32),
            shape((1, 128), f32),
            shape((1, ROWS), f32),
        ],
        1 << 30,
        feature_slot.T,
        clicks.reshape(1, SAMPLES),
        requests.T,
        factors,
        acc_factors,
        acc_linear.reshape(1, SHARE),
        linear.reshape(1, ROWS),
    )
    found = call(gather_kernel, shape((OWNERS, CAP, K), bf16), 1 << 28, got, narrow)
    rows = exchange(found, "server")
    lin_terms, hot_t = call(
        side_kernel, [shape((SLOTS, 128), bf16), shape((ROWS, SLOTS), bf16)], 1 << 28, got, req_t
    )
    push = call(
        learn_kernel,
        shape((OWNERS, CAP, WIDE), bf16),
        1 << 28,
        rows,
        counts,
        counts_t,
        clicks_col,
        lin_terms,
    )
    pushed = exchange(push, "server")
    dense = call(scatter_kernel, shape((N_WORKER, TALL, 128), bf16), 1 << 28, pushed, hot_t)
    shared = exchange(dense, ("y", "core"))
    delta = call(update_kernel, shape((N_Y, TALL, 128), bf16), 1 << 20, shared, acc, acc_lin)
    deltas = exchange(delta, "y")
    new_acc, new_acc_lin = call(
        state_kernel, [shape((SHARE, K), f32), shape((1, SHARE), f32)], 1 << 20, shared, acc, acc_lin
    )
    deltas = lax.all_gather(deltas, "core", axis=0, tiled=True)
    new_factors, new_linear = call(
        apply_kernel, [shape((ROWS, K), f32), shape((1, ROWS), f32)], 1 << 20, deltas, wide, lin_row
    )
    return new_factors, new_linear.reshape(ROWS), new_acc, new_acc_lin.reshape(SHARE)


def solution(mesh):
    mesh = Mesh(mesh.devices.reshape(OWNERS, N_Y, N_CORE), ("server", "y", "core"))
    every = ("server", "y", "core")
    in_specs = (
        P("server", None),
        P("server"),
        P(every, None),
        P(every),
        P(every, None),
        P(every, None),
        P(every),
    )
    out_specs = (P("server", None), P("server"), P(every, None), P(every))
    return jax.shard_map(body, mesh=mesh, in_specs=in_specs, out_specs=out_specs, check_vma=False)
```

```python
import jax
import jax.numpy as jnp
from jax import lax
from jax.experimental import pallas as pl
from jax.experimental.pallas import tpu as pltpu
from jax.sharding import Mesh, PartitionSpec as P

step_size = 0.5
bf16 = jnp.bfloat16
f32 = jnp.float32

OWNERS = 32
CAP = 16
SLOTS = OWNERS * CAP
ROWS = 512
K = 256
WIDE = K + 128
SAMPLES = 256
FIELDS = 39
N_Y = 8
N_CORE = 2
N_WORKER = N_Y * N_CORE
SHARE = ROWS // N_WORKER


def iota(shape, axis):
    return lax.broadcasted_iota(jnp.int32, shape, axis)


def dot(a, b, ca=1, cb=0):
    return lax.dot_general(a, b, (((ca,), (cb,)), ((), ())), preferred_element_type=f32)


def split_requests(req_t):
    high = jnp.bitwise_and(req_t, -16)
    low = jnp.bitwise_and(req_t, 15)
    pad = jnp.zeros((96, OWNERS), jnp.int32)
    return jnp.concatenate([high, low, pad], axis=0).astype(f32).astype(bf16)


def own_lists(req_t):
    owner = jnp.right_shift(iota((SLOTS, OWNERS), 0), 4)
    mine = (owner == iota((SLOTS, OWNERS), 1)).astype(f32).astype(bf16)
    lists = dot(mine, split_requests(req_t), 1, 1)
    lane = iota((SLOTS, 128), 1)
    position = jnp.bitwise_and(iota((SLOTS, 128), 0), CAP - 1)
    keep = (lane < 2 * CAP) & (jnp.bitwise_and(lane, CAP - 1) == position)
    return jnp.where(keep, lists, 0.0)


def ones(dims, axis):
    return (iota(dims, axis) < 2 * CAP).astype(f32).astype(bf16)


def ask_kernel(req_t_hbm, lin_hbm, out_ref, req_t_ref, lin_ref, sems):
    copies = [
        pltpu.make_async_copy(req_t_hbm, req_t_ref, sems.at[0]),
        pltpu.make_async_copy(lin_hbm, lin_ref, sems.at[1]),
    ]
    for copy in copies:
        copy.start()
    for copy in copies:
        copy.wait()
    lists = own_lists(req_t_ref[...])
    spread = (jnp.right_shift(iota((CAP, 4), 0), 1) == iota((CAP, 4), 1)).astype(f32).astype(bf16)
    lin = dot(spread, lin_ref[...].astype(bf16))
    odd = jnp.bitwise_and(iota((CAP, 128), 0), 1) == 1
    lin = jnp.where(odd, lin, pltpu.roll(lin, 64, 1))
    lin = jnp.where(iota((CAP, 128), 1) >= 64, lin, 0.0)
    out_ref[...] = (lists.reshape(OWNERS, CAP, 128) + lin[None]).astype(bf16)


def prep_kernel(
    fs_t_ref,
    clicks_ref,
    req_t_in,
    factors_in,
    acc_in,
    acc_lin_row_ref,
    linear_in,
    counts_t_ref,
    counts_ref,
    clicks_col_ref,
    req_t_ref,
    factors_ref,
    narrow_ref,
    acc_ref,
    acc_lin_ref,
    linear_ref,
):
    for here, there in (
        (req_t_in, req_t_ref),
        (factors_in, factors_ref),
        (acc_in, acc_ref),
        (linear_in, linear_ref),
    ):
        there[...] = here[...]
    narrow_ref[...] = factors_in[...].astype(bf16)
    same_share = iota((SHARE, SHARE), 0) == iota((SHARE, SHARE), 1)
    acc_lin = jnp.sum(jnp.where(same_share, acc_lin_row_ref[...], 0.0), axis=1, keepdims=True)
    acc_lin_ref[...] = jnp.sum(jnp.where(of_share(), acc_lin, 0.0), axis=0, keepdims=True)
    chunk = 64

    def one(i, carry):
        base = pl.multiple_of(i * chunk, chunk)
        slots = iota((chunk, SAMPLES), 0) + base
        total = jnp.zeros((chunk, SAMPLES), f32)
        for f in range(FIELDS):
            total = total + jnp.where(fs_t_ref[pl.ds(f, 1), :] == slots, 1.0, 0.0)
        counts_t_ref[pl.ds(base, chunk), :] = total.astype(bf16)
        return carry

    lax.fori_loop(0, SLOTS // chunk, one, 0)
    counts_ref[...] = jnp.transpose(counts_t_ref[...].astype(f32)).astype(bf16)
    same = iota((SAMPLES, SAMPLES), 0) == iota((SAMPLES, SAMPLES), 1)
    clicks = clicks_ref[...].astype(f32)
    clicks_col_ref[...] = jnp.sum(jnp.where(same, clicks, 0.0), axis=1, keepdims=True)


def of_share():
    return jnp.bitwise_and(iota((SHARE, 128), 1), SHARE - 1) == iota((SHARE, 128), 0)


def gather_kernel(got_ref, narrow_ref, out_ref):
    asked = dot(got_ref[...].reshape(SLOTS, 128), ones((128, ROWS), 0))
    hot = (asked == iota((SLOTS, ROWS), 1).astype(f32)).astype(f32).astype(bf16)
    out_ref[...] = dot(hot, narrow_ref[...]).astype(bf16).reshape(OWNERS, CAP, K)


def side_kernel(got_ref, both_ref, req_t_ref, lin_ref, hot_t_ref):
    got = got_ref[...].reshape(SLOTS, 128)
    wanted = dot(own_lists(req_t_ref[...]).astype(bf16), ones((128, SLOTS), 0)).astype(jnp.int32)
    first = jnp.bitwise_and(iota((SLOTS, SLOTS), 0), -CAP)
    pick = iota((SLOTS, SLOTS), 1) == first + jnp.right_shift(wanted, 6)
    values = dot(pick.astype(f32).astype(bf16), got)
    here = iota((SLOTS, 128), 1) == jnp.bitwise_and(wanted[:, :128], 63) + 64
    lin_ref[...] = jnp.where(here, values, 0.0).astype(bf16)
    asked_t = dot(ones((ROWS, 128), 1), both_ref[...].reshape(N_CORE * SLOTS, 128), 1, 1)
    hot = asked_t == iota((ROWS, N_CORE * SLOTS), 0).astype(f32)
    hot_t_ref[...] = hot.astype(f32).astype(bf16)


def learn_kernel(rows_ref, counts_ref, counts_t_ref, clicks_ref, lin_ref, out_ref):
    rows = rows_ref[...].reshape(SLOTS, K)
    wide_rows = rows.astype(f32)
    counts = counts_ref[...]
    sums = dot(counts, rows)
    square = wide_rows * wide_rows
    high = square.astype(bf16)
    low = (square - high.astype(f32)).astype(bf16)
    terms = sums * sums - dot(counts, high) - dot(counts, low)
    terms = 0.5 * (terms[:, :128] + terms[:, 128:]) + dot(counts, lin_ref[...])
    logits = jnp.sum(terms, axis=1, keepdims=True)
    errors = jnp.broadcast_to(jax.nn.sigmoid(logits) - clicks_ref[...], (SAMPLES, K))
    weighted = (errors * sums).astype(bf16)
    first = errors.astype(bf16)
    second = (errors - first.astype(f32)).astype(bf16)
    counts_t = counts_t_ref[...]
    error_sums = dot(counts_t, first) + dot(counts_t, second)
    grads = dot(counts_t, weighted) - error_sums * wide_rows
    out_ref[:, :, :K] = grads.astype(bf16).reshape(OWNERS, CAP, K)
    total = error_sums[:, :128]
    lane = iota((SLOTS, 128), 1)
    first = total.astype(bf16).astype(f32)
    linear = jnp.where(lane == 0, first, jnp.where(lane == 1, total - first, 0.0))
    out_ref[:, :, K:] = linear.astype(bf16).reshape(OWNERS, CAP, 128)


def part_rows(x):
    rows = iota((8, x.shape[1]), 0)
    first = x.astype(bf16).astype(f32)
    rest = x - first
    second = rest.astype(bf16).astype(f32)
    third = rest - second
    out = jnp.where(rows == 0, first, jnp.where(rows == 1, second, jnp.where(rows == 2, third, 0.0)))
    return out.astype(bf16)


def scatter_kernel(push_ref, hot_t_ref, out_ref):
    core = lax.axis_index("core")
    pushed = push_ref[...].reshape(N_CORE * SLOTS, WIDE)
    shares = [
        hot_t_ref[pl.ds(pl.multiple_of((y * N_CORE + core) * SHARE, SHARE), SHARE), :] for y in range(N_Y)
    ]
    total = dot(jnp.concatenate(shares, axis=0), pushed[:, :K]).astype(bf16)
    out_ref[:, :SHARE, :] = total[:, :128].reshape(N_Y, SHARE, 128)
    out_ref[:, SHARE : 2 * SHARE, :] = total[:, 128:].reshape(N_Y, SHARE, 128)
    linear = part_rows(jnp.sum(dot(pushed[:, K:], hot_t_ref[...], 0, 1), axis=0, keepdims=True))
    for y in range(N_Y):
        lanes = y // 2 * 128
        out_ref[y, 2 * SHARE :, :] = linear[:, lanes : lanes + 128]


def add_parts(part_ref):
    total = part_ref[0].astype(f32)
    for y in range(1, N_Y):
        total = total + part_ref[y].astype(f32)
    left, right = total[:SHARE], total[SHARE : 2 * SHARE]
    return left, right, jnp.sum(total[2 * SHARE :], axis=0, keepdims=True)


def my_lanes():
    me = lax.axis_index("y") * N_CORE + lax.axis_index("core")
    return jnp.right_shift(iota((1, 128), 1), 5) == lax.rem(me, 4)


def update_kernel(part_ref, acc_ref, acc_lin_ref, delta_ref):
    left, right, linear = add_parts(part_ref)
    acc = acc_ref[...]

    def step(grad, state):
        return step_size * grad / jnp.sqrt(state + grad * grad)

    left = step(left, acc[:, :128]).astype(bf16)
    right = step(right, acc[:, 128:]).astype(bf16)
    linear = part_rows(jnp.where(my_lanes(), step(linear, acc_lin_ref[...]), 0.0))
    for y in range(N_Y):
        delta_ref[y, :SHARE, :] = left
        delta_ref[y, SHARE : 2 * SHARE, :] = right
        delta_ref[y, 2 * SHARE :, :] = linear


def state_kernel(part_ref, acc_ref, acc_lin_ref, new_acc_ref, new_acc_lin_ref):
    left, right, linear = add_parts(part_ref)
    new_acc_ref[:, :128] = acc_ref[:, :128] + left * left
    new_acc_ref[:, 128:] = acc_ref[:, 128:] + right * right
    state = jnp.where(my_lanes(), acc_lin_ref[...] + linear * linear, 0.0)
    column = jnp.sum(jnp.where(of_share(), state, 0.0), axis=1, keepdims=True)
    same = iota((SHARE, SHARE), 0) == iota((SHARE, SHARE), 1)
    new_acc_lin_ref[...] = jnp.sum(jnp.where(same, column, 0.0), axis=0, keepdims=True)


def apply_kernel(delta_ref, factors_ref, linear_ref, new_factors_ref, new_linear_ref):
    for q in range(4):
        lin = jnp.zeros((8, 128), f32)
        for w in range(4 * q, 4 * q + 4):
            block = delta_ref[w % N_CORE * N_Y + w // N_CORE].astype(f32)
            here = pl.ds(w * SHARE, SHARE)
            new_factors_ref[here, :128] = factors_ref[here, :128] - block[:SHARE]
            new_factors_ref[here, 128:] = factors_ref[here, 128:] - block[SHARE : 2 * SHARE]
            lin = lin + block[2 * SHARE :]
        lanes = pl.ds(q * 128, 128)
        new_linear_ref[:, lanes] = linear_ref[:, lanes] - jnp.sum(lin, axis=0, keepdims=True)


def call(kernel, out, flops, *args, scratch=(), far=False):
    size = sum(a.size * a.dtype.itemsize for a in args)
    return pl.pallas_call(
        kernel,
        out_shape=out,
        in_specs=[pl.BlockSpec(memory_space=pltpu.HBM if far else pltpu.VMEM)] * len(args),
        out_specs=jax.tree.map(lambda _: pl.BlockSpec(memory_space=pltpu.VMEM), out),
        scratch_shapes=scratch,
        compiler_params=pltpu.CompilerParams(vmem_limit_bytes=None if far else 24 * 1024 * 1024),
        cost_estimate=pl.CostEstimate(flops=flops, bytes_accessed=size, transcendentals=0),
    )(*args)


def shape(dims, dtype):
    return jax.ShapeDtypeStruct(dims, dtype)


def exchange(x, axis):
    return lax.all_to_all(x, axis, split_axis=0, concat_axis=0, tiled=True)


TALL = 2 * SHARE + 8


def body(factors, linear, acc_factors, acc_linear, feature_slot, requests, clicks):
    dma = pltpu.SemaphoreType.DMA
    ask = call(
        ask_kernel,
        shape((OWNERS, CAP, 128), bf16),
        1 << 20,
        requests.T,
        linear.reshape(4, 128),
        scratch=[pltpu.VMEM((CAP, OWNERS), jnp.int32), pltpu.VMEM((4, 128), f32), dma((2,))],
        far=True,
    )
    got = exchange(ask, "server")
    counts_t, counts, clicks_col, req_t, wide, narrow, acc, acc_lin, lin_row = call(
        prep_kernel,
        [
            shape((SLOTS, SAMPLES), bf16),
            shape((SAMPLES, SLOTS), bf16),
            shape((SAMPLES, 1), f32),
            shape((CAP, OWNERS), jnp.int32),
            shape((ROWS, K), f32),
            shape((ROWS, K), bf16),
            shape((SHARE, K), f32),
            shape((1, 128), f32),
            shape((1, ROWS), f32),
        ],
        1 << 30,
        feature_slot.T,
        clicks.reshape(1, SAMPLES),
        requests.T,
        factors,
        acc_factors,
        acc_linear.reshape(1, SHARE),
        linear.reshape(1, ROWS),
    )
    found = call(gather_kernel, shape((OWNERS, CAP, K), bf16), 1 << 28, got, narrow)
    rows = exchange(found, "server")
    both = lax.all_gather(got, "core", axis=0, tiled=True)
    lin_terms, hot_t = call(
        side_kernel,
        [shape((SLOTS, 128), bf16), shape((ROWS, N_CORE * SLOTS), bf16)],
        1 << 28,
        got,
        both,
        req_t,
    )
    push = call(
        learn_kernel,
        shape((OWNERS, CAP, WIDE), bf16),
        1 << 28,
        rows,
        counts,
        counts_t,
        clicks_col,
        lin_terms,
    )
    pushed = exchange(push, "server")
    pushed = lax.all_gather(pushed, "core", axis=0, tiled=True)
    dense = call(scatter_kernel, shape((N_Y, TALL, 128), bf16), 1 << 28, pushed, hot_t)
    shared = exchange(dense, "y")
    delta = call(update_kernel, shape((N_Y, TALL, 128), bf16), 1 << 20, shared, acc, acc_lin)
    deltas = exchange(delta, "y")
    new_acc, new_acc_lin = call(
        state_kernel, [shape((SHARE, K), f32), shape((1, SHARE), f32)], 1 << 20, shared, acc, acc_lin
    )
    deltas = lax.all_gather(deltas, "core", axis=0, tiled=True)
    new_factors, new_linear = call(
        apply_kernel, [shape((ROWS, K), f32), shape((1, ROWS), f32)], 1 << 20, deltas, wide, lin_row
    )
    return new_factors, new_linear.reshape(ROWS), new_acc, new_acc_lin.reshape(SHARE)


def solution(mesh):
    mesh = Mesh(mesh.devices.reshape(OWNERS, N_Y, N_CORE), ("server", "y", "core"))
    every = ("server", "y", "core")
    in_specs = (
        P("server", None),
        P("server"),
        P(every, None),
        P(every),
        P(every, None),
        P(every, None),
        P(every),
    )
    out_specs = (P("server", None), P("server"), P(every, None), P(every))
    return jax.shard_map(body, mesh=mesh, in_specs=in_specs, out_specs=out_specs, check_vma=False)
```

```python
import jax
import jax.numpy as jnp
from jax import lax
from jax.experimental import pallas as pl
from jax.experimental.pallas import tpu as pltpu
from jax.sharding import Mesh, PartitionSpec as P

step_size = 0.5
bf16 = jnp.bfloat16
f32 = jnp.float32

OWNERS = 32
CAP = 16
SLOTS = OWNERS * CAP
ROWS = 512
K = 256
SAMPLES = 256
FIELDS = 39
N_Y = 8
N_CORE = 2
N_WORKER = N_Y * N_CORE
SHARE = ROWS // N_WORKER


def iota(shape, axis):
    return lax.broadcasted_iota(jnp.int32, shape, axis)


def dot(a, b, ca=1, cb=0):
    return lax.dot_general(a, b, (((ca,), (cb,)), ((), ())), preferred_element_type=f32)


def split_requests(req_t):
    high = jnp.bitwise_and(req_t, -16)
    low = jnp.bitwise_and(req_t, 15)
    pad = jnp.zeros((96, OWNERS), jnp.int32)
    return jnp.concatenate([high, low, pad], axis=0).astype(f32).astype(bf16)


def own_lists(req_t):
    owner = jnp.right_shift(iota((SLOTS, OWNERS), 0), 4)
    mine = (owner == iota((SLOTS, OWNERS), 1)).astype(f32).astype(bf16)
    lists = dot(mine, split_requests(req_t), 1, 1)
    lane = iota((SLOTS, 128), 1)
    position = jnp.bitwise_and(iota((SLOTS, 128), 0), CAP - 1)
    keep = (lane < 2 * CAP) & (jnp.bitwise_and(lane, CAP - 1) == position)
    return jnp.where(keep, lists, 0.0)


def ones(dims, axis):
    return (iota(dims, axis) < 2 * CAP).astype(f32).astype(bf16)


def ask_kernel(req_t_hbm, lin_hbm, factors_hbm, out_ref, factors_ref, req_t_ref, lin_ref, sems):
    copies = [
        pltpu.make_async_copy(req_t_hbm, req_t_ref, sems.at[0]),
        pltpu.make_async_copy(lin_hbm, lin_ref, sems.at[1]),
        pltpu.make_async_copy(factors_hbm, factors_ref, sems.at[2]),
    ]
    for copy in copies:
        copy.start()
    for copy in copies[:2]:
        copy.wait()
    lists = own_lists(req_t_ref[...])
    spread = (jnp.right_shift(iota((CAP, 4), 0), 1) == iota((CAP, 4), 1)).astype(f32).astype(bf16)
    lin = dot(spread, lin_ref[...].astype(bf16))
    odd = jnp.bitwise_and(iota((CAP, 128), 0), 1) == 1
    lin = jnp.where(odd, lin, pltpu.roll(lin, 64, 1))
    lin = jnp.where(iota((CAP, 128), 1) >= 64, lin, 0.0)
    out_ref[...] = (lists.reshape(OWNERS, CAP, 128) + lin[None]).astype(bf16)
    copies[2].wait()


def of_share():
    return jnp.bitwise_and(iota((SHARE, 128), 1), SHARE - 1) == iota((SHARE, 128), 0)


def gather_kernel(got_ref, factors_ref, out_ref):
    asked = dot(got_ref[...].reshape(SLOTS, 128), ones((128, ROWS), 0))
    hot = (asked == iota((SLOTS, ROWS), 1).astype(f32)).astype(f32).astype(bf16)
    out_ref[...] = dot(hot, factors_ref[...].astype(bf16)).astype(bf16).reshape(OWNERS, CAP, K)


def side_kernel(
    got_ref,
    both_ref,
    req_t_ref,
    fs_t_ref,
    clicks_ref,
    acc_in,
    acc_lin_row_ref,
    linear_in,
    lin_ref,
    hot_t_ref,
    counts_t_ref,
    counts_ref,
    clicks_col_ref,
    acc_ref,
    acc_lin_ref,
    linear_ref,
):
    acc_ref[...] = acc_in[...]
    linear_ref[...] = linear_in[...]
    got = got_ref[...].reshape(SLOTS, 128)
    wanted = dot(own_lists(req_t_ref[...]).astype(bf16), ones((128, SLOTS), 0)).astype(jnp.int32)
    first = jnp.bitwise_and(iota((SLOTS, SLOTS), 0), -CAP)
    pick = iota((SLOTS, SLOTS), 1) == first + jnp.right_shift(wanted, 6)
    values = dot(pick.astype(f32).astype(bf16), got)
    here = iota((SLOTS, 128), 1) == jnp.bitwise_and(wanted[:, :128], 63) + 64
    lin_ref[...] = jnp.where(here, values, 0.0).astype(bf16)

    asked_t = dot(ones((ROWS, 128), 1), both_ref[...].reshape(N_CORE * SLOTS, 128), 1, 1)
    hot = asked_t == iota((ROWS, N_CORE * SLOTS), 0).astype(f32)
    hot_t_ref[...] = hot.astype(f32).astype(bf16)
    same_share = iota((SHARE, SHARE), 0) == iota((SHARE, SHARE), 1)
    acc_lin = jnp.sum(jnp.where(same_share, acc_lin_row_ref[...], 0.0), axis=1, keepdims=True)
    acc_lin_ref[...] = jnp.sum(jnp.where(of_share(), acc_lin, 0.0), axis=0, keepdims=True)
    chunk = 64

    def one(i, carry):
        base = pl.multiple_of(i * chunk, chunk)
        slots = iota((chunk, SAMPLES), 0) + base
        total = jnp.zeros((chunk, SAMPLES), f32)
        for f in range(FIELDS):
            total = total + jnp.where(fs_t_ref[pl.ds(f, 1), :] == slots, 1.0, 0.0)
        counts_t_ref[pl.ds(base, chunk), :] = total.astype(bf16)
        return carry

    lax.fori_loop(0, SLOTS // chunk, one, 0)
    counts_ref[...] = jnp.transpose(counts_t_ref[...].astype(f32)).astype(bf16)
    same = iota((SAMPLES, SAMPLES), 0) == iota((SAMPLES, SAMPLES), 1)
    clicks = clicks_ref[...].astype(f32)
    clicks_col_ref[...] = jnp.sum(jnp.where(same, clicks, 0.0), axis=1, keepdims=True)


def learn_kernel(rows_ref, counts_ref, counts_t_ref, clicks_ref, lin_ref, out_ref):
    rows = rows_ref[...].reshape(SLOTS, K)
    wide_rows = rows.astype(f32)
    counts = counts_ref[...]
    sums = dot(counts, rows)
    square = wide_rows * wide_rows
    high = square.astype(bf16)
    low = (square - high.astype(f32)).astype(bf16)
    terms = sums * sums - dot(counts, high) - dot(counts, low)
    terms = 0.5 * (terms[:, :128] + terms[:, 128:]) + dot(counts, lin_ref[...])
    logits = jnp.sum(terms, axis=1, keepdims=True)
    errors = jnp.broadcast_to(jax.nn.sigmoid(logits) - clicks_ref[...], (SAMPLES, K))
    weighted = (errors * sums).astype(bf16)
    first = errors.astype(bf16)
    second = (errors - first.astype(f32)).astype(bf16)
    counts_t = counts_t_ref[...]
    error_sums = dot(counts_t, first) + dot(counts_t, second)
    grads = dot(counts_t, weighted) - error_sums * wide_rows
    grads = grads.astype(bf16)
    out_ref[:, :CAP, :] = grads[:, :128].reshape(OWNERS, CAP, 128)
    out_ref[:, CAP : 2 * CAP, :] = grads[:, 128:].reshape(OWNERS, CAP, 128)
    place = lax.rem(lax.axis_index("server"), 8)
    sums_row = (dot(first[:, :128], counts, 0, 0) + dot(second[:, :128], counts, 0, 0))[:8]
    high = sums_row.astype(bf16).astype(f32)
    row = iota((8, SLOTS), 0)
    sums_row = jnp.where(row == 0, high, jnp.where(row == 1, sums_row - high, 0.0))
    mine = jnp.right_shift(iota((8, 128), 1), 4) == place
    for owner in range(OWNERS):
        lanes = owner // 8 * 128
        turn = lax.rem(place + 8 - owner % 8, 8) * CAP
        tile = pltpu.roll(sums_row[:, lanes : lanes + 128], turn, 1)
        out_ref[owner, 2 * CAP :, :] = jnp.where(mine, tile, 0.0).astype(bf16)


def part_rows(x):
    rows = iota((8, x.shape[1]), 0)
    first = x.astype(bf16).astype(f32)
    rest = x - first
    second = rest.astype(bf16).astype(f32)
    third = rest - second
    out = jnp.where(rows == 0, first, jnp.where(rows == 1, second, jnp.where(rows == 2, third, 0.0)))
    return out.astype(bf16)


def scatter_kernel(push_ref, hot_t_ref, out_ref):
    core = lax.axis_index("core")
    left = push_ref[:, :CAP, :].reshape(N_CORE * SLOTS, 128)
    right = push_ref[:, CAP : 2 * CAP, :].reshape(N_CORE * SLOTS, 128)
    shares = [
        hot_t_ref[pl.ds(pl.multiple_of((y * N_CORE + core) * SHARE, SHARE), SHARE), :] for y in range(N_Y)
    ]
    total = dot(jnp.concatenate(shares, axis=0), jnp.concatenate([left, right], axis=1)).astype(bf16)
    out_ref[:, :SHARE, :] = total[:, :128].reshape(N_Y, SHARE, 128)
    out_ref[:, SHARE : 2 * SHARE, :] = total[:, 128:].reshape(N_Y, SHARE, 128)
    chunks = []
    for q in range(N_CORE * OWNERS // 8):
        chunk = push_ref[8 * q, 2 * CAP :, :].astype(f32)
        for i in range(1, 8):
            chunk = chunk + push_ref[8 * q + i, 2 * CAP :, :].astype(f32)
        chunks.append(chunk.astype(bf16))
    linear = dot(jnp.concatenate(chunks, axis=1), hot_t_ref[...], 1, 1)
    linear = part_rows(jnp.sum(linear, axis=0, keepdims=True))
    for y in range(N_Y):
        lanes = y // 2 * 128
        out_ref[y, 2 * SHARE :, :] = linear[:, lanes : lanes + 128]


def add_parts(part_ref):
    total = part_ref[0].astype(f32)
    for y in range(1, N_Y):
        total = total + part_ref[y].astype(f32)
    left, right = total[:SHARE], total[SHARE : 2 * SHARE]
    return left, right, jnp.sum(total[2 * SHARE :], axis=0, keepdims=True)


def my_lanes():
    me = lax.axis_index("y") * N_CORE + lax.axis_index("core")
    return jnp.right_shift(iota((1, 128), 1), 5) == lax.rem(me, 4)


def update_kernel(part_ref, acc_ref, acc_lin_ref, delta_ref):
    left, right, linear = add_parts(part_ref)
    acc = acc_ref[...]

    def step(grad, state):
        return step_size * grad / jnp.sqrt(state + grad * grad)

    left = step(left, acc[:, :128]).astype(bf16)
    right = step(right, acc[:, 128:]).astype(bf16)
    linear = part_rows(jnp.where(my_lanes(), step(linear, acc_lin_ref[...]), 0.0))
    for y in range(N_Y):
        delta_ref[y, :SHARE, :] = left
        delta_ref[y, SHARE : 2 * SHARE, :] = right
        delta_ref[y, 2 * SHARE :, :] = linear


def write_state(part_ref, acc_ref, acc_lin_ref, new_acc_ref, new_acc_lin_ref):
    left, right, linear = add_parts(part_ref)
    new_acc_ref[:, :128] = acc_ref[:, :128] + left * left
    new_acc_ref[:, 128:] = acc_ref[:, 128:] + right * right
    state = jnp.where(my_lanes(), acc_lin_ref[...] + linear * linear, 0.0)
    column = jnp.sum(jnp.where(of_share(), state, 0.0), axis=1, keepdims=True)
    same = iota((SHARE, SHARE), 0) == iota((SHARE, SHARE), 1)
    new_acc_lin_ref[...] = jnp.sum(jnp.where(same, column, 0.0), axis=0, keepdims=True)


def apply_kernel(
    delta_ref,
    factors_ref,
    linear_ref,
    part_ref,
    acc_ref,
    acc_lin_ref,
    new_factors_ref,
    new_linear_ref,
    new_acc_ref,
    new_acc_lin_ref,
):
    write_state(part_ref, acc_ref, acc_lin_ref, new_acc_ref, new_acc_lin_ref)
    for q in range(4):
        lin = jnp.zeros((8, 128), f32)
        for w in range(4 * q, 4 * q + 4):
            block = delta_ref[w % N_CORE * N_Y + w // N_CORE].astype(f32)
            here = pl.ds(w * SHARE, SHARE)
            new_factors_ref[here, :128] = factors_ref[here, :128] - block[:SHARE]
            new_factors_ref[here, 128:] = factors_ref[here, 128:] - block[SHARE : 2 * SHARE]
            lin = lin + block[2 * SHARE :]
        lanes = pl.ds(q * 128, 128)
        new_linear_ref[:, lanes] = linear_ref[:, lanes] - jnp.sum(lin, axis=0, keepdims=True)


def call(kernel, out, flops, *args, scratch=(), far=False):
    size = sum(a.size * a.dtype.itemsize for a in args)
    if far:
        args = [pltpu.with_memory_space_constraint(a, pltpu.HBM) for a in args]
    return pl.pallas_call(
        kernel,
        out_shape=out,
        in_specs=[pl.BlockSpec(memory_space=pltpu.HBM if far else pltpu.VMEM)] * len(args),
        out_specs=jax.tree.map(lambda _: pl.BlockSpec(memory_space=pltpu.VMEM), out),
        scratch_shapes=scratch,
        compiler_params=pltpu.CompilerParams(vmem_limit_bytes=24 * 1024 * 1024),
        cost_estimate=pl.CostEstimate(flops=flops, bytes_accessed=size, transcendentals=0),
    )(*args)


def shape(dims, dtype):
    return jax.ShapeDtypeStruct(dims, dtype)


def exchange(x, axis):
    return lax.all_to_all(x, axis, split_axis=0, concat_axis=0, tiled=True)


TALL = 2 * SHARE + 8


def body(factors, linear, acc_factors, acc_linear, feature_slot, requests, clicks):
    dma = pltpu.SemaphoreType.DMA
    req_t = requests.T
    ask, wide = call(
        ask_kernel,
        [shape((OWNERS, CAP, 128), bf16), shape((ROWS, K), f32)],
        1 << 20,
        req_t,
        linear.reshape(4, 128),
        factors,
        scratch=[pltpu.VMEM((CAP, OWNERS), jnp.int32), pltpu.VMEM((4, 128), f32), dma((3,))],
        far=True,
    )
    got = exchange(ask, "server")
    found = call(gather_kernel, shape((OWNERS, CAP, K), bf16), 1 << 28, got, wide)
    rows = exchange(found, "server")
    both = lax.all_gather(got, "core", axis=0, tiled=True)
    lin_terms, hot_t, counts_t, counts, clicks_col, acc, acc_lin, lin_row = call(
        side_kernel,
        [
            shape((SLOTS, 128), bf16),
            shape((ROWS, N_CORE * SLOTS), bf16),
            shape((SLOTS, SAMPLES), bf16),
            shape((SAMPLES, SLOTS), bf16),
            shape((SAMPLES, 1), f32),
            shape((SHARE, K), f32),
            shape((1, 128), f32),
            shape((1, ROWS), f32),
        ],
        1 << 30,
        got,
        both,
        req_t,
        feature_slot.T,
        clicks.reshape(1, SAMPLES),
        acc_factors,
        acc_linear.reshape(1, SHARE),
        linear.reshape(1, ROWS),
    )
    push = call(
        learn_kernel,
        shape((OWNERS, 2 * CAP + 8, 128), bf16),
        1 << 28,
        rows,
        counts,
        counts_t,
        clicks_col,
        lin_terms,
    )
    pushed = exchange(push, "server")
    pushed = lax.all_gather(pushed, "core", axis=0, tiled=True)
    dense = call(
        scatter_kernel, shape((N_Y, TALL, 128), bf16), 1 << 28, pushed, hot_t
    )
    shared = exchange(dense, "y")
    delta = call(update_kernel, shape((N_Y, TALL, 128), bf16), 1 << 20, shared, acc, acc_lin)
    deltas = exchange(delta, "y")
    deltas = lax.all_gather(deltas, "core", axis=0, tiled=True)
    new_factors, new_linear, new_acc, new_acc_lin = call(
        apply_kernel,
        [shape((ROWS, K), f32), shape((1, ROWS), f32), shape((SHARE, K), f32), shape((1, SHARE), f32)],
        1 << 20,
        deltas,
        wide,
        lin_row,
        shared,
        acc,
        acc_lin,
    )
    return new_factors, new_linear.reshape(ROWS), new_acc, new_acc_lin.reshape(SHARE)


def solution(mesh):
    mesh = Mesh(mesh.devices.reshape(OWNERS, N_Y, N_CORE), ("server", "y", "core"))
    every = ("server", "y", "core")
    in_specs = (
        P("server", None),
        P("server"),
        P(every, None),
        P(every),
        P(every, None),
        P(every, None),
        P(every),
    )
    out_specs = (P("server", None), P("server"), P(every, None), P(every))
    return jax.shard_map(body, mesh=mesh, in_specs=in_specs, out_specs=out_specs, check_vma=False)
```

```python
import jax
import jax.numpy as jnp
from jax import lax
from jax.experimental import pallas as pl
from jax.experimental.pallas import tpu as pltpu
from jax.sharding import Mesh, PartitionSpec as P

step_size = 0.5
bf16 = jnp.bfloat16
f32 = jnp.float32

OWNERS = 32
CAP = 16
SLOTS = OWNERS * CAP
ROWS = 512
K = 256
SAMPLES = 256
FIELDS = 39
N_Y = 8
N_CORE = 2
N_WORKER = N_Y * N_CORE
SHARE = ROWS // N_WORKER


def iota(shape, axis):
    return lax.broadcasted_iota(jnp.int32, shape, axis)


def dot(a, b, ca=1, cb=0):
    return lax.dot_general(a, b, (((ca,), (cb,)), ((), ())), preferred_element_type=f32)


def split_requests(req_t):
    high = jnp.bitwise_and(req_t, -16)
    low = jnp.bitwise_and(req_t, 15)
    pad = jnp.zeros((96, OWNERS), jnp.int32)
    return jnp.concatenate([high, low, pad], axis=0).astype(f32).astype(bf16)


def own_lists(req_t, rows):
    owner = jnp.right_shift(iota((OWNERS * rows, OWNERS), 0), 4 if rows == CAP else 3)
    mine = (owner == iota((OWNERS * rows, OWNERS), 1)).astype(f32).astype(bf16)
    lists = dot(mine, split_requests(req_t), 1, 1)
    lane = iota((OWNERS * rows, 128), 1)
    position = jnp.bitwise_and(iota((OWNERS * rows, 128), 0), rows - 1)
    keep = (lane < 2 * CAP) & (jnp.bitwise_and(lane, rows - 1) == position)
    return jnp.where(keep, lists, 0.0)


def one_slot_a_row(got):
    got = got.astype(f32)
    upper = jnp.bitwise_and(iota(got.shape, 2), 8) == 8
    split = jnp.concatenate([jnp.where(upper, 0.0, got), jnp.where(upper, got, 0.0)], axis=1)
    return split.astype(bf16).reshape(got.shape[0] * CAP, 128)


def ones(dims, axis):
    return (iota(dims, axis) < 2 * CAP).astype(f32).astype(bf16)


def ask_kernel(req_t_hbm, lin_hbm, factors_hbm, out_ref, factors_ref, req_t_ref, lin_ref, sems):
    copies = [
        pltpu.make_async_copy(req_t_hbm, req_t_ref, sems.at[0]),
        pltpu.make_async_copy(lin_hbm, lin_ref, sems.at[1]),
        pltpu.make_async_copy(factors_hbm, factors_ref, sems.at[2]),
    ]
    for copy in copies:
        copy.start()
    for copy in copies[:2]:
        copy.wait()
    lists = own_lists(req_t_ref[...], 8)
    spread = (jnp.right_shift(iota((8, 4), 0), 1) == iota((8, 4), 1)).astype(f32).astype(bf16)
    lin = dot(spread, lin_ref[...].astype(bf16))
    odd = jnp.bitwise_and(iota((8, 128), 0), 1) == 1
    lin = jnp.where(odd, lin, pltpu.roll(lin, 64, 1))
    lin = jnp.where(iota((8, 128), 1) >= 64, lin, 0.0)
    out_ref[...] = (lists.reshape(OWNERS, 8, 128) + lin[None]).astype(bf16)
    copies[2].wait()


def of_share():
    return jnp.bitwise_and(iota((SHARE, 128), 1), SHARE - 1) == iota((SHARE, 128), 0)


def gather_kernel(got_ref, factors_ref, out_ref):
    asked = dot(one_slot_a_row(got_ref[...]), ones((128, ROWS), 0))
    hot = (asked == iota((SLOTS, ROWS), 1).astype(f32)).astype(f32).astype(bf16)
    out_ref[...] = dot(hot, factors_ref[...].astype(bf16)).astype(bf16).reshape(OWNERS, CAP, K)


def side_kernel(
    got_ref,
    req_t_ref,
    fs_t_ref,
    clicks_ref,
    acc_in,
    acc_lin_row_ref,
    linear_in,
    lin_ref,
    counts_t_ref,
    counts_ref,
    clicks_col_ref,
    acc_ref,
    acc_lin_ref,
    linear_ref,
):
    acc_ref[...] = acc_in[...]
    linear_ref[...] = linear_in[...]
    got = got_ref[...].astype(f32).reshape(8 * OWNERS, 128).astype(bf16)
    lists = own_lists(req_t_ref[...], CAP).astype(bf16)
    wanted = dot(lists, ones((128, 8 * OWNERS), 0)).astype(jnp.int32)
    first = jnp.right_shift(iota((SLOTS, 8 * OWNERS), 0), 4) * 8
    pick = iota((SLOTS, 8 * OWNERS), 1) == first + jnp.right_shift(wanted, 6)
    values = dot(pick.astype(f32).astype(bf16), got)
    here = iota((SLOTS, 128), 1) == jnp.bitwise_and(wanted[:, :128], 63) + 64
    lin_ref[...] = jnp.where(here, values, 0.0).astype(bf16)
    same_share = iota((SHARE, SHARE), 0) == iota((SHARE, SHARE), 1)
    acc_lin = jnp.sum(jnp.where(same_share, acc_lin_row_ref[...], 0.0), axis=1, keepdims=True)
    acc_lin_ref[...] = jnp.sum(jnp.where(of_share(), acc_lin, 0.0), axis=0, keepdims=True)
    chunk = 64

    def one(i, carry):
        base = pl.multiple_of(i * chunk, chunk)
        slots = iota((chunk, SAMPLES), 0) + base
        total = jnp.zeros((chunk, SAMPLES), f32)
        for f in range(FIELDS):
            total = total + jnp.where(fs_t_ref[pl.ds(f, 1), :] == slots, 1.0, 0.0)
        counts_t_ref[pl.ds(base, chunk), :] = total.astype(bf16)
        return carry

    lax.fori_loop(0, SLOTS // chunk, one, 0)
    counts_ref[...] = jnp.transpose(counts_t_ref[...].astype(f32)).astype(bf16)
    same = iota((SAMPLES, SAMPLES), 0) == iota((SAMPLES, SAMPLES), 1)
    clicks = clicks_ref[...].astype(f32)
    clicks_col_ref[...] = jnp.sum(jnp.where(same, clicks, 0.0), axis=1, keepdims=True)


def asked_kernel(both_ref, hot_t_ref):
    asked_t = dot(ones((ROWS, 128), 1), one_slot_a_row(both_ref[...]), 1, 1)
    hot = asked_t == iota((ROWS, N_CORE * SLOTS), 0).astype(f32)
    hot_t_ref[...] = hot.astype(f32).astype(bf16)


def learn_kernel(rows_ref, counts_ref, counts_t_ref, clicks_ref, lin_ref, got_ref, out_ref, later_ref):
    later_ref[...] = got_ref[...]
    rows = rows_ref[...].reshape(SLOTS, K)
    wide_rows = rows.astype(f32)
    counts = counts_ref[...]
    sums = dot(counts, rows)
    square = wide_rows * wide_rows
    high = square.astype(bf16)
    low = (square - high.astype(f32)).astype(bf16)
    terms = sums * sums - dot(counts, high) - dot(counts, low)
    terms = 0.5 * (terms[:, :128] + terms[:, 128:]) + dot(counts, lin_ref[...])
    logits = jnp.sum(terms, axis=1, keepdims=True)
    errors = jnp.broadcast_to(jax.nn.sigmoid(logits) - clicks_ref[...], (SAMPLES, K))
    weighted = (errors * sums).astype(bf16)
    first = errors.astype(bf16)
    second = (errors - first.astype(f32)).astype(bf16)
    counts_t = counts_t_ref[...]
    error_sums = dot(counts_t, first) + dot(counts_t, second)
    grads = dot(counts_t, weighted) - error_sums * wide_rows
    grads = grads.astype(bf16)
    out_ref[:, :CAP, :] = grads[:, :128].reshape(OWNERS, CAP, 128)
    out_ref[:, CAP : 2 * CAP, :] = grads[:, 128:].reshape(OWNERS, CAP, 128)
    place = lax.rem(lax.axis_index("server"), 8)
    sums_row = (dot(first[:, :128], counts, 0, 0) + dot(second[:, :128], counts, 0, 0))[:8]
    high = sums_row.astype(bf16).astype(f32)
    row = iota((8, SLOTS), 0)
    sums_row = jnp.where(row == 0, high, jnp.where(row == 1, sums_row - high, 0.0))
    mine = jnp.right_shift(iota((8, 128), 1), 4) == place
    for owner in range(OWNERS):
        lanes = owner // 8 * 128
        turn = lax.rem(place + 8 - owner % 8, 8) * CAP
        tile = pltpu.roll(sums_row[:, lanes : lanes + 128], turn, 1)
        out_ref[owner, 2 * CAP :, :] = jnp.where(mine, tile, 0.0).astype(bf16)


def part_rows(x):
    rows = iota((8, x.shape[1]), 0)
    first = x.astype(bf16).astype(f32)
    rest = x - first
    second = rest.astype(bf16).astype(f32)
    third = rest - second
    out = jnp.where(rows == 0, first, jnp.where(rows == 1, second, jnp.where(rows == 2, third, 0.0)))
    return out.astype(bf16)


def scatter_kernel(push_ref, hot_t_ref, out_ref):
    core = lax.axis_index("core")
    left = push_ref[:, :CAP, :].reshape(N_CORE * SLOTS, 128)
    right = push_ref[:, CAP : 2 * CAP, :].reshape(N_CORE * SLOTS, 128)
    shares = [
        hot_t_ref[pl.ds(pl.multiple_of((y * N_CORE + core) * SHARE, SHARE), SHARE), :] for y in range(N_Y)
    ]
    total = dot(jnp.concatenate(shares, axis=0), jnp.concatenate([left, right], axis=1)).astype(bf16)
    out_ref[:, :SHARE, :] = total[:, :128].reshape(N_Y, SHARE, 128)
    out_ref[:, SHARE : 2 * SHARE, :] = total[:, 128:].reshape(N_Y, SHARE, 128)
    chunks = []
    for q in range(N_CORE * OWNERS // 8):
        chunk = push_ref[8 * q, 2 * CAP :, :].astype(f32)
        for i in range(1, 8):
            chunk = chunk + push_ref[8 * q + i, 2 * CAP :, :].astype(f32)
        chunks.append(chunk.astype(bf16))
    linear = dot(jnp.concatenate(chunks, axis=1), hot_t_ref[...], 1, 1)
    linear = part_rows(jnp.sum(linear, axis=0, keepdims=True))
    for y in range(N_Y):
        lanes = y // 2 * 128
        out_ref[y, 2 * SHARE :, :] = linear[:, lanes : lanes + 128]


def add_parts(part_ref):
    total = part_ref[0].astype(f32)
    for y in range(1, N_Y):
        total = total + part_ref[y].astype(f32)
    left, right = total[:SHARE], total[SHARE : 2 * SHARE]
    return left, right, jnp.sum(total[2 * SHARE :], axis=0, keepdims=True)


def my_lanes():
    me = lax.axis_index("y") * N_CORE + lax.axis_index("core")
    return jnp.right_shift(iota((1, 128), 1), 5) == lax.rem(me, 4)


def update_kernel(part_ref, acc_ref, acc_lin_ref, delta_ref):
    left, right, linear = add_parts(part_ref)
    acc = acc_ref[...]

    def step(grad, state):
        return step_size * grad / jnp.sqrt(state + grad * grad)

    left = step(left, acc[:, :128]).astype(bf16)
    right = step(right, acc[:, 128:]).astype(bf16)
    linear = part_rows(jnp.where(my_lanes(), step(linear, acc_lin_ref[...]), 0.0))
    for y in range(N_Y):
        delta_ref[y, :SHARE, :] = left
        delta_ref[y, SHARE : 2 * SHARE, :] = right
        delta_ref[y, 2 * SHARE :, :] = linear


def write_state(part_ref, acc_ref, acc_lin_ref, new_acc_ref, new_acc_lin_ref):
    left, right, linear = add_parts(part_ref)
    new_acc_ref[:, :128] = acc_ref[:, :128] + left * left
    new_acc_ref[:, 128:] = acc_ref[:, 128:] + right * right
    state = jnp.where(my_lanes(), acc_lin_ref[...] + linear * linear, 0.0)
    column = jnp.sum(jnp.where(of_share(), state, 0.0), axis=1, keepdims=True)
    same = iota((SHARE, SHARE), 0) == iota((SHARE, SHARE), 1)
    new_acc_lin_ref[...] = jnp.sum(jnp.where(same, column, 0.0), axis=0, keepdims=True)


def apply_kernel(
    delta_ref,
    factors_ref,
    linear_ref,
    part_ref,
    acc_ref,
    acc_lin_ref,
    new_factors_ref,
    new_linear_ref,
    new_acc_ref,
    new_acc_lin_ref,
):
    write_state(part_ref, acc_ref, acc_lin_ref, new_acc_ref, new_acc_lin_ref)
    for q in range(4):
        lin = jnp.zeros((8, 128), f32)
        for w in range(4 * q, 4 * q + 4):
            block = delta_ref[w % N_CORE * N_Y + w // N_CORE].astype(f32)
            here = pl.ds(w * SHARE, SHARE)
            new_factors_ref[here, :128] = factors_ref[here, :128] - block[:SHARE]
            new_factors_ref[here, 128:] = factors_ref[here, 128:] - block[SHARE : 2 * SHARE]
            lin = lin + block[2 * SHARE :]
        lanes = pl.ds(q * 128, 128)
        new_linear_ref[:, lanes] = linear_ref[:, lanes] - jnp.sum(lin, axis=0, keepdims=True)


def call(kernel, out, flops, *args, scratch=(), far=False):
    size = sum(a.size * a.dtype.itemsize for a in args)
    if far:
        args = [pltpu.with_memory_space_constraint(a, pltpu.HBM) for a in args]
    return pl.pallas_call(
        kernel,
        out_shape=out,
        in_specs=[pl.BlockSpec(memory_space=pltpu.HBM if far else pltpu.VMEM)] * len(args),
        out_specs=jax.tree.map(lambda _: pl.BlockSpec(memory_space=pltpu.VMEM), out),
        scratch_shapes=scratch,
        compiler_params=pltpu.CompilerParams(vmem_limit_bytes=24 * 1024 * 1024),
        cost_estimate=pl.CostEstimate(flops=flops, bytes_accessed=size, transcendentals=0),
    )(*args)


def shape(dims, dtype):
    return jax.ShapeDtypeStruct(dims, dtype)


def exchange(x, axis):
    return lax.all_to_all(x, axis, split_axis=0, concat_axis=0, tiled=True)


TALL = 2 * SHARE + 8


def body(factors, linear, acc_factors, acc_linear, feature_slot, requests, clicks):
    dma = pltpu.SemaphoreType.DMA
    req_t = requests.T
    ask, wide = call(
        ask_kernel,
        [shape((OWNERS, 8, 128), bf16), shape((ROWS, K), f32)],
        1 << 20,
        req_t,
        linear.reshape(4, 128),
        factors,
        scratch=[pltpu.VMEM((CAP, OWNERS), jnp.int32), pltpu.VMEM((4, 128), f32), dma((3,))],
        far=True,
    )
    got = exchange(ask, "server")
    found = call(gather_kernel, shape((OWNERS, CAP, K), bf16), 1 << 28, got, wide)
    rows = exchange(found, "server")
    lin_terms, counts_t, counts, clicks_col, acc, acc_lin, lin_row = call(
        side_kernel,
        [
            shape((SLOTS, 128), bf16),
            shape((SLOTS, SAMPLES), bf16),
            shape((SAMPLES, SLOTS), bf16),
            shape((SAMPLES, 1), f32),
            shape((SHARE, K), f32),
            shape((1, 128), f32),
            shape((1, ROWS), f32),
        ],
        1 << 30,
        got,
        req_t,
        feature_slot.T,
        clicks.reshape(1, SAMPLES),
        acc_factors,
        acc_linear.reshape(1, SHARE),
        linear.reshape(1, ROWS),
    )
    push, later = call(
        learn_kernel,
        [shape((OWNERS, 2 * CAP + 8, 128), bf16), shape((OWNERS, 8, 128), bf16)],
        1 << 28,
        rows,
        counts,
        counts_t,
        clicks_col,
        lin_terms,
        got,
    )
    pushed = exchange(push, "server")
    both = lax.all_gather(later, "core", axis=0, tiled=True)
    hot_t = call(asked_kernel, shape((ROWS, N_CORE * SLOTS), bf16), 1 << 30, both)
    pushed = lax.all_gather(pushed, "core", axis=0, tiled=True)
    dense = call(
        scatter_kernel, shape((N_Y, TALL, 128), bf16), 1 << 28, pushed, hot_t
    )
    shared = exchange(dense, "y")
    delta = call(update_kernel, shape((N_Y, TALL, 128), bf16), 1 << 20, shared, acc, acc_lin)
    deltas = exchange(delta, "y")
    deltas = lax.all_gather(deltas, "core", axis=0, tiled=True)
    new_factors, new_linear, new_acc, new_acc_lin = call(
        apply_kernel,
        [shape((ROWS, K), f32), shape((1, ROWS), f32), shape((SHARE, K), f32), shape((1, SHARE), f32)],
        1 << 20,
        deltas,
        wide,
        lin_row,
        shared,
        acc,
        acc_lin,
    )
    return new_factors, new_linear.reshape(ROWS), new_acc, new_acc_lin.reshape(SHARE)


def solution(mesh):
    mesh = Mesh(mesh.devices.reshape(OWNERS, N_Y, N_CORE), ("server", "y", "core"))
    every = ("server", "y", "core")
    in_specs = (
        P("server", None),
        P("server"),
        P(every, None),
        P(every),
        P(every, None),
        P(every, None),
        P(every),
    )
    out_specs = (P("server", None), P("server"), P(every, None), P(every))
    return jax.shard_map(body, mesh=mesh, in_specs=in_specs, out_specs=out_specs, check_vma=False)
```

```python
import jax
import jax.numpy as jnp
from jax import lax
from jax.experimental import pallas as pl
from jax.experimental.pallas import tpu as pltpu
from jax.sharding import Mesh, PartitionSpec as P

step_size = 0.5
bf16 = jnp.bfloat16
f32 = jnp.float32

OWNERS = 32
CAP = 16
SLOTS = OWNERS * CAP
ROWS = 512
K = 256
SAMPLES = 256
FIELDS = 39
N_Y = 8
N_CORE = 2
N_WORKER = N_Y * N_CORE
SHARE = ROWS // N_WORKER


def iota(shape, axis):
    return lax.broadcasted_iota(jnp.int32, shape, axis)


def dot(a, b, ca=1, cb=0):
    return lax.dot_general(a, b, (((ca,), (cb,)), ((), ())), preferred_element_type=f32)


def split_requests(req_t):
    high = jnp.bitwise_and(req_t, -16)
    low = jnp.bitwise_and(req_t, 15)
    pad = jnp.zeros((96, OWNERS), jnp.int32)
    return jnp.concatenate([high, low, pad], axis=0).astype(f32).astype(bf16)


def own_lists(req_t, rows):
    owner = jnp.right_shift(iota((OWNERS * rows, OWNERS), 0), 4 if rows == CAP else 3)
    mine = (owner == iota((OWNERS * rows, OWNERS), 1)).astype(f32).astype(bf16)
    lists = dot(mine, split_requests(req_t), 1, 1)
    lane = iota((OWNERS * rows, 128), 1)
    position = jnp.bitwise_and(iota((OWNERS * rows, 128), 0), rows - 1)
    keep = (lane < 2 * CAP) & (jnp.bitwise_and(lane, rows - 1) == position)
    return jnp.where(keep, lists, 0.0)


def one_slot_a_row(got):
    got = got.astype(f32)
    upper = jnp.bitwise_and(iota(got.shape, 2), 8) == 8
    split = jnp.concatenate([jnp.where(upper, 0.0, got), jnp.where(upper, got, 0.0)], axis=1)
    return split.astype(bf16).reshape(got.shape[0] * CAP, 128)


def ones(dims, axis):
    return (iota(dims, axis) < 2 * CAP).astype(f32).astype(bf16)


def ask_kernel(req_t_hbm, lin_hbm, factors_hbm, out_ref, factors_ref, req_t_ref, lin_ref, sems):
    copies = [
        pltpu.make_async_copy(req_t_hbm, req_t_ref, sems.at[0]),
        pltpu.make_async_copy(lin_hbm, lin_ref, sems.at[1]),
        pltpu.make_async_copy(factors_hbm, factors_ref, sems.at[2]),
    ]
    for copy in copies:
        copy.start()
    for copy in copies[:2]:
        copy.wait()
    lists = own_lists(req_t_ref[...], 8)
    spread = (jnp.right_shift(iota((8, 4), 0), 1) == iota((8, 4), 1)).astype(f32).astype(bf16)
    lin = dot(spread, lin_ref[...].astype(bf16))
    odd = jnp.bitwise_and(iota((8, 128), 0), 1) == 1
    lin = jnp.where(odd, lin, pltpu.roll(lin, 64, 1))
    lin = jnp.where(iota((8, 128), 1) >= 64, lin, 0.0)
    out_ref[...] = (lists.reshape(OWNERS, 8, 128) + lin[None]).astype(bf16)
    copies[2].wait()


def of_share():
    return jnp.bitwise_and(iota((SHARE, 128), 1), SHARE - 1) == iota((SHARE, 128), 0)


def gather_kernel(got_ref, factors_ref, out_ref):
    asked = dot(one_slot_a_row(got_ref[...]), ones((128, ROWS), 0))
    hot = (asked == iota((SLOTS, ROWS), 1).astype(f32)).astype(f32).astype(bf16)
    out_ref[...] = dot(hot, factors_ref[...].astype(bf16)).astype(bf16).reshape(OWNERS, CAP, K)


def side_kernel(
    got_ref,
    req_t_ref,
    fs_t_ref,
    clicks_ref,
    acc_in,
    acc_lin_row_ref,
    linear_in,
    lin_ref,
    ids_ref,
    counts_t_ref,
    counts_ref,
    clicks_col_ref,
    acc_ref,
    acc_lin_ref,
    linear_ref,
):
    acc_ref[...] = acc_in[...]
    linear_ref[...] = linear_in[...]
    got = got_ref[...].astype(f32).reshape(8 * OWNERS, 128).astype(bf16)
    lists = own_lists(req_t_ref[...], CAP).astype(bf16)
    wanted = dot(lists, ones((128, 8 * OWNERS), 0)).astype(jnp.int32)
    first = jnp.right_shift(iota((SLOTS, 8 * OWNERS), 0), 4) * 8
    pick = iota((SLOTS, 8 * OWNERS), 1) == first + jnp.right_shift(wanted, 6)
    values = dot(pick.astype(f32).astype(bf16), got)
    here = iota((SLOTS, 128), 1) == jnp.bitwise_and(wanted[:, :128], 63) + 64
    lin_ref[...] = jnp.where(here, values, 0.0).astype(bf16)
    spread = jnp.right_shift(iota((OWNERS, SLOTS), 1), 4) == iota((OWNERS, SLOTS), 0)
    lists = dot(split_requests(req_t_ref[...]), spread.astype(f32).astype(bf16))
    place = iota((128, SLOTS), 0)
    position = jnp.bitwise_and(iota((128, SLOTS), 1), CAP - 1)
    high = jnp.sum(jnp.where(place == position, lists, 0.0), axis=0, keepdims=True)
    low = jnp.sum(jnp.where(place == position + CAP, lists, 0.0), axis=0, keepdims=True)
    row = iota((8, SLOTS), 0)
    ids_ref[...] = jnp.where(row == 2, high, jnp.where(row == 3, low, 0.0))
    same_share = iota((SHARE, SHARE), 0) == iota((SHARE, SHARE), 1)
    acc_lin = jnp.sum(jnp.where(same_share, acc_lin_row_ref[...], 0.0), axis=1, keepdims=True)
    acc_lin_ref[...] = jnp.sum(jnp.where(of_share(), acc_lin, 0.0), axis=0, keepdims=True)
    chunk = 64

    def one(i, carry):
        base = pl.multiple_of(i * chunk, chunk)
        slots = iota((chunk, SAMPLES), 0) + base
        total = jnp.zeros((chunk, SAMPLES), f32)
        for f in range(FIELDS):
            total = total + jnp.where(fs_t_ref[pl.ds(f, 1), :] == slots, 1.0, 0.0)
        counts_t_ref[pl.ds(base, chunk), :] = total.astype(bf16)
        return carry

    lax.fori_loop(0, SLOTS // chunk, one, 0)
    counts_ref[...] = jnp.transpose(counts_t_ref[...].astype(f32)).astype(bf16)
    same = iota((SAMPLES, SAMPLES), 0) == iota((SAMPLES, SAMPLES), 1)
    clicks = clicks_ref[...].astype(f32)
    clicks_col_ref[...] = jnp.sum(jnp.where(same, clicks, 0.0), axis=1, keepdims=True)


def learn_kernel(rows_ref, counts_ref, counts_t_ref, clicks_ref, lin_ref, ids_ref, out_ref):
    rows = rows_ref[...].reshape(SLOTS, K)
    wide_rows = rows.astype(f32)
    counts = counts_ref[...]
    sums = dot(counts, rows)
    square = wide_rows * wide_rows
    high = square.astype(bf16)
    low = (square - high.astype(f32)).astype(bf16)
    terms = sums * sums - dot(counts, high) - dot(counts, low)
    terms = 0.5 * (terms[:, :128] + terms[:, 128:]) + dot(counts, lin_ref[...])
    logits = jnp.sum(terms, axis=1, keepdims=True)
    errors = jnp.broadcast_to(jax.nn.sigmoid(logits) - clicks_ref[...], (SAMPLES, K))
    weighted = (errors * sums).astype(bf16)
    first = errors.astype(bf16)
    second = (errors - first.astype(f32)).astype(bf16)
    counts_t = counts_t_ref[...]
    error_sums = dot(counts_t, first) + dot(counts_t, second)
    grads = dot(counts_t, weighted) - error_sums * wide_rows
    grads = grads.astype(bf16)
    out_ref[:, :CAP, :] = grads[:, :128].reshape(OWNERS, CAP, 128)
    out_ref[:, CAP : 2 * CAP, :] = grads[:, 128:].reshape(OWNERS, CAP, 128)
    place = lax.rem(lax.axis_index("server"), 8)
    sums_row = (dot(first[:, :128], counts, 0, 0) + dot(second[:, :128], counts, 0, 0))[:8]
    high = sums_row.astype(bf16).astype(f32)
    row = iota((8, SLOTS), 0)
    sums_row = jnp.where(row == 0, high, jnp.where(row == 1, sums_row - high, ids_ref[...]))
    mine = jnp.right_shift(iota((8, 128), 1), 4) == place
    for owner in range(OWNERS):
        lanes = owner // 8 * 128
        turn = lax.rem(place + 8 - owner % 8, 8) * CAP
        tile = pltpu.roll(sums_row[:, lanes : lanes + 128], turn, 1)
        out_ref[owner, 2 * CAP :, :] = jnp.where(mine, tile, 0.0).astype(bf16)


def part_rows(x):
    rows = iota((8, x.shape[1]), 0)
    first = x.astype(bf16).astype(f32)
    rest = x - first
    second = rest.astype(bf16).astype(f32)
    third = rest - second
    return jnp.where(rows == 0, first, jnp.where(rows == 1, second, jnp.where(rows == 2, third, 0.0)))


def scatter_kernel(push_ref, out_ref):
    core = lax.axis_index("core")
    chunks = []
    for q in range(N_CORE * OWNERS // 8):
        chunk = push_ref[8 * q, 2 * CAP :, :].astype(f32)
        for i in range(1, 8):
            chunk = chunk + push_ref[8 * q + i, 2 * CAP :, :].astype(f32)
        chunks.append(chunk)
    tails = jnp.concatenate(chunks, axis=1)
    row = iota(tails.shape, 0)
    asked = jnp.sum(jnp.where((row == 2) | (row == 3), tails, 0.0), axis=0, keepdims=True)
    asked = asked.astype(jnp.int32)
    ours = jnp.bitwise_and(jnp.right_shift(asked, 5), 1) == core
    place = jnp.right_shift(asked, 6) * SHARE + jnp.bitwise_and(asked, SHARE - 1)
    place = jnp.where(ours, place, -1)
    hot = (iota((ROWS // N_CORE, N_CORE * SLOTS), 0) == place).astype(f32).astype(bf16)
    left = push_ref[:, :CAP, :].reshape(N_CORE * SLOTS, 128)
    right = push_ref[:, CAP : 2 * CAP, :].reshape(N_CORE * SLOTS, 128)
    total = dot(hot, jnp.concatenate([left, right], axis=1)).astype(bf16)
    out_ref[:, :SHARE, :] = total[:, :128].reshape(N_Y, SHARE, 128)
    out_ref[:, SHARE : 2 * SHARE, :] = total[:, 128:].reshape(N_Y, SHARE, 128)
    linear = dot(jnp.where(row < 2, tails, 0.0).astype(bf16), hot, 1, 1)
    linear = part_rows(jnp.sum(linear, axis=0, keepdims=True))
    for y in range(N_Y):
        lanes = y // 4 * 128
        turn = lax.rem(N_CORE * y + core + 4 - y % 4, 4) * SHARE
        out_ref[y, 2 * SHARE :, :] = pltpu.roll(linear[:, lanes : lanes + 128], turn, 1).astype(bf16)


def add_parts(part_ref):
    total = part_ref[0].astype(f32)
    for y in range(1, N_Y):
        total = total + part_ref[y].astype(f32)
    left, right = total[:SHARE], total[SHARE : 2 * SHARE]
    return left, right, jnp.sum(total[2 * SHARE :], axis=0, keepdims=True)


def my_lanes():
    me = lax.axis_index("y") * N_CORE + lax.axis_index("core")
    return jnp.right_shift(iota((1, 128), 1), 5) == lax.rem(me, 4)


def update_kernel(part_ref, acc_ref, acc_lin_ref, delta_ref):
    left, right, linear = add_parts(part_ref)
    acc = acc_ref[...]

    def step(grad, state):
        return step_size * grad / jnp.sqrt(state + grad * grad)

    left = step(left, acc[:, :128]).astype(bf16)
    right = step(right, acc[:, 128:]).astype(bf16)
    linear = part_rows(jnp.where(my_lanes(), step(linear, acc_lin_ref[...]), 0.0)).astype(bf16)
    for y in range(N_Y):
        delta_ref[y, :SHARE, :] = left
        delta_ref[y, SHARE : 2 * SHARE, :] = right
        delta_ref[y, 2 * SHARE :, :] = linear


def write_state(part_ref, acc_ref, acc_lin_ref, new_acc_ref, new_acc_lin_ref):
    left, right, linear = add_parts(part_ref)
    new_acc_ref[:, :128] = acc_ref[:, :128] + left * left
    new_acc_ref[:, 128:] = acc_ref[:, 128:] + right * right
    state = jnp.where(my_lanes(), acc_lin_ref[...] + linear * linear, 0.0)
    column = jnp.sum(jnp.where(of_share(), state, 0.0), axis=1, keepdims=True)
    same = iota((SHARE, SHARE), 0) == iota((SHARE, SHARE), 1)
    new_acc_lin_ref[...] = jnp.sum(jnp.where(same, column, 0.0), axis=0, keepdims=True)


def apply_kernel(
    delta_ref,
    factors_ref,
    linear_ref,
    part_ref,
    acc_ref,
    acc_lin_ref,
    new_factors_ref,
    new_linear_ref,
    new_acc_ref,
    new_acc_lin_ref,
):
    write_state(part_ref, acc_ref, acc_lin_ref, new_acc_ref, new_acc_lin_ref)
    for q in range(4):
        lin = jnp.zeros((8, 128), f32)
        for w in range(4 * q, 4 * q + 4):
            block = delta_ref[w % N_CORE * N_Y + w // N_CORE].astype(f32)
            here = pl.ds(w * SHARE, SHARE)
            new_factors_ref[here, :128] = factors_ref[here, :128] - block[:SHARE]
            new_factors_ref[here, 128:] = factors_ref[here, 128:] - block[SHARE : 2 * SHARE]
            lin = lin + block[2 * SHARE :]
        lanes = pl.ds(q * 128, 128)
        new_linear_ref[:, lanes] = linear_ref[:, lanes] - jnp.sum(lin, axis=0, keepdims=True)


def call(kernel, out, flops, *args, scratch=(), far=False):
    size = sum(a.size * a.dtype.itemsize for a in args)
    if far:
        args = [pltpu.with_memory_space_constraint(a, pltpu.HBM) for a in args]
    return pl.pallas_call(
        kernel,
        out_shape=out,
        in_specs=[pl.BlockSpec(memory_space=pltpu.HBM if far else pltpu.VMEM)] * len(args),
        out_specs=jax.tree.map(lambda _: pl.BlockSpec(memory_space=pltpu.VMEM), out),
        scratch_shapes=scratch,
        compiler_params=pltpu.CompilerParams(vmem_limit_bytes=24 * 1024 * 1024),
        cost_estimate=pl.CostEstimate(flops=flops, bytes_accessed=size, transcendentals=0),
    )(*args)


def shape(dims, dtype):
    return jax.ShapeDtypeStruct(dims, dtype)


def exchange(x, axis):
    return lax.all_to_all(x, axis, split_axis=0, concat_axis=0, tiled=True)


TALL = 2 * SHARE + 8


def body(factors, linear, acc_factors, acc_linear, feature_slot, requests, clicks):
    dma = pltpu.SemaphoreType.DMA
    req_t = requests.T
    ask, wide = call(
        ask_kernel,
        [shape((OWNERS, 8, 128), bf16), shape((ROWS, K), f32)],
        1 << 20,
        req_t,
        linear.reshape(4, 128),
        factors,
        scratch=[pltpu.VMEM((CAP, OWNERS), jnp.int32), pltpu.VMEM((4, 128), f32), dma((3,))],
        far=True,
    )
    got = exchange(ask, "server")
    found = call(gather_kernel, shape((OWNERS, CAP, K), bf16), 1 << 28, got, wide)
    rows = exchange(found, "server")
    lin_terms, ids, counts_t, counts, clicks_col, acc, acc_lin, lin_row = call(
        side_kernel,
        [
            shape((SLOTS, 128), bf16),
            shape((8, SLOTS), f32),
            shape((SLOTS, SAMPLES), bf16),
            shape((SAMPLES, SLOTS), bf16),
            shape((SAMPLES, 1), f32),
            shape((SHARE, K), f32),
            shape((1, 128), f32),
            shape((1, ROWS), f32),
        ],
        1 << 30,
        got,
        req_t,
        feature_slot.T,
        clicks.reshape(1, SAMPLES),
        acc_factors,
        acc_linear.reshape(1, SHARE),
        linear.reshape(1, ROWS),
    )
    push = call(
        learn_kernel,
        shape((OWNERS, 2 * CAP + 8, 128), bf16),
        1 << 28,
        rows,
        counts,
        counts_t,
        clicks_col,
        lin_terms,
        ids,
    )
    pushed = exchange(push, "server")
    pushed = lax.all_gather(pushed, "core", axis=0, tiled=True)
    dense = call(scatter_kernel, shape((N_Y, TALL, 128), bf16), 1 << 28, pushed)
    shared = exchange(dense, "y")
    delta = call(update_kernel, shape((N_Y, TALL, 128), bf16), 1 << 20, shared, acc, acc_lin)
    deltas = exchange(delta, "y")
    deltas = lax.all_gather(deltas, "core", axis=0, tiled=True)
    new_factors, new_linear, new_acc, new_acc_lin = call(
        apply_kernel,
        [shape((ROWS, K), f32), shape((1, ROWS), f32), shape((SHARE, K), f32), shape((1, SHARE), f32)],
        1 << 20,
        deltas,
        wide,
        lin_row,
        shared,
        acc,
        acc_lin,
    )
    return new_factors, new_linear.reshape(ROWS), new_acc, new_acc_lin.reshape(SHARE)


def solution(mesh):
    mesh = Mesh(mesh.devices.reshape(OWNERS, N_Y, N_CORE), ("server", "y", "core"))
    every = ("server", "y", "core")
    in_specs = (
        P("server", None),
        P("server"),
        P(every, None),
        P(every),
        P(every, None),
        P(every, None),
        P(every),
    )
    out_specs = (P("server", None), P("server"), P(every, None), P(every))
    return jax.shard_map(body, mesh=mesh, in_specs=in_specs, out_specs=out_specs, check_vma=False)
```

```python
import jax
import jax.numpy as jnp
from jax import lax
from jax.experimental import pallas as pl
from jax.experimental.pallas import tpu as pltpu
from jax.sharding import Mesh, PartitionSpec as P

step_size = 0.5
bf16 = jnp.bfloat16
f32 = jnp.float32

OWNERS = 32
CAP = 16
SLOTS = OWNERS * CAP
ROWS = 512
K = 256
SAMPLES = 256
FIELDS = 39
N_Y = 8
N_CORE = 2
N_WORKER = N_Y * N_CORE
SHARE = ROWS // N_WORKER


def iota(shape, axis):
    return lax.broadcasted_iota(jnp.int32, shape, axis)


def dot(a, b, ca=1, cb=0):
    return lax.dot_general(a, b, (((ca,), (cb,)), ((), ())), preferred_element_type=f32)


def split_requests(req_t):
    high = jnp.bitwise_and(req_t, -16)
    low = jnp.bitwise_and(req_t, 15)
    pad = jnp.zeros((96, OWNERS), jnp.int32)
    return jnp.concatenate([high, low, pad], axis=0).astype(f32).astype(bf16)


def own_lists(req_t, rows):
    owner = jnp.right_shift(iota((OWNERS * rows, OWNERS), 0), 4 if rows == CAP else 3)
    mine = (owner == iota((OWNERS * rows, OWNERS), 1)).astype(f32).astype(bf16)
    lists = dot(mine, split_requests(req_t), 1, 1)
    lane = iota((OWNERS * rows, 128), 1)
    position = jnp.bitwise_and(iota((OWNERS * rows, 128), 0), rows - 1)
    keep = (lane < 2 * CAP) & (jnp.bitwise_and(lane, rows - 1) == position)
    return jnp.where(keep, lists, 0.0)


def asked_rows(got):
    got = got.astype(f32)
    lane = iota(got.shape, 2)
    upper = jnp.bitwise_and(lane, 8) == 8
    got = jnp.where(lane < 2 * CAP, got, 0.0)
    split = jnp.concatenate([jnp.where(upper, 0.0, got), jnp.where(upper, got, 0.0)], axis=1)
    return jnp.sum(split.reshape(SLOTS, 128), axis=1, keepdims=True)


def ones(dims, axis):
    return (iota(dims, axis) < 2 * CAP).astype(f32).astype(bf16)


def ask_kernel(req_t_hbm, lin_hbm, factors_hbm, out_ref, factors_ref, req_t_ref, lin_ref, sems):
    copies = [
        pltpu.make_async_copy(req_t_hbm, req_t_ref, sems.at[0]),
        pltpu.make_async_copy(lin_hbm, lin_ref, sems.at[1]),
        pltpu.make_async_copy(factors_hbm, factors_ref, sems.at[2]),
    ]
    for copy in copies:
        copy.start()
    for copy in copies[:2]:
        copy.wait()
    lists = own_lists(req_t_ref[...], 8)
    spread = (jnp.right_shift(iota((8, 4), 0), 1) == iota((8, 4), 1)).astype(f32).astype(bf16)
    lin = dot(spread, lin_ref[...].astype(bf16))
    odd = jnp.bitwise_and(iota((8, 128), 0), 1) == 1
    lin = jnp.where(odd, lin, pltpu.roll(lin, 64, 1))
    lin = jnp.where(iota((8, 128), 1) >= 64, lin, 0.0)
    out_ref[...] = (lists.reshape(OWNERS, 8, 128) + lin[None]).astype(bf16)
    copies[2].wait()


def of_share():
    return jnp.bitwise_and(iota((SHARE, 128), 1), SHARE - 1) == iota((SHARE, 128), 0)


def gather_kernel(got_ref, factors_ref, out_ref):
    asked = asked_rows(got_ref[...])
    hot = (asked == iota((SLOTS, ROWS), 1).astype(f32)).astype(f32).astype(bf16)
    out_ref[...] = dot(hot, factors_ref[...].astype(bf16)).astype(bf16).reshape(OWNERS, CAP, K)


def side_kernel(
    got_ref,
    req_t_ref,
    fs_t_ref,
    clicks_ref,
    acc_in,
    acc_lin_row_ref,
    linear_in,
    lin_ref,
    ids_ref,
    counts_t_ref,
    counts_ref,
    clicks_col_ref,
    acc_ref,
    acc_lin_ref,
    linear_ref,
):
    acc_ref[...] = acc_in[...]
    linear_ref[...] = linear_in[...]
    got = got_ref[...].astype(f32).reshape(8 * OWNERS, 128).astype(bf16)
    lists = own_lists(req_t_ref[...], CAP).astype(bf16)
    wanted = dot(lists, ones((128, 8 * OWNERS), 0)).astype(jnp.int32)
    first = jnp.right_shift(iota((SLOTS, 8 * OWNERS), 0), 4) * 8
    pick = iota((SLOTS, 8 * OWNERS), 1) == first + jnp.right_shift(wanted, 6)
    values = dot(pick.astype(f32).astype(bf16), got)
    here = iota((SLOTS, 128), 1) == jnp.bitwise_and(wanted[:, :128], 63) + 64
    lin_ref[...] = jnp.where(here, values, 0.0).astype(bf16)
    spread = jnp.right_shift(iota((OWNERS, SLOTS), 1), 4) == iota((OWNERS, SLOTS), 0)
    lists = dot(split_requests(req_t_ref[...]), spread.astype(f32).astype(bf16))
    place = iota((128, SLOTS), 0)
    position = jnp.bitwise_and(iota((128, SLOTS), 1), CAP - 1)
    high = jnp.sum(jnp.where(place == position, lists, 0.0), axis=0, keepdims=True)
    low = jnp.sum(jnp.where(place == position + CAP, lists, 0.0), axis=0, keepdims=True)
    row = iota((8, SLOTS), 0)
    ids_ref[...] = jnp.where(row == 2, high, jnp.where(row == 3, low, 0.0))
    same_share = iota((SHARE, SHARE), 0) == iota((SHARE, SHARE), 1)
    acc_lin = jnp.sum(jnp.where(same_share, acc_lin_row_ref[...], 0.0), axis=1, keepdims=True)
    acc_lin_ref[...] = jnp.sum(jnp.where(of_share(), acc_lin, 0.0), axis=0, keepdims=True)
    chunk = 64

    def one(i, carry):
        base = pl.multiple_of(i * chunk, chunk)
        slots = iota((chunk, SAMPLES), 0) + base
        total = jnp.zeros((chunk, SAMPLES), f32)
        for f in range(FIELDS):
            total = total + jnp.where(fs_t_ref[pl.ds(f, 1), :] == slots, 1.0, 0.0)
        counts_t_ref[pl.ds(base, chunk), :] = total.astype(bf16)
        return carry

    lax.fori_loop(0, SLOTS // chunk, one, 0)
    counts_ref[...] = jnp.transpose(counts_t_ref[...].astype(f32)).astype(bf16)
    same = iota((SAMPLES, SAMPLES), 0) == iota((SAMPLES, SAMPLES), 1)
    clicks = clicks_ref[...].astype(f32)
    clicks_col_ref[...] = jnp.sum(jnp.where(same, clicks, 0.0), axis=1, keepdims=True)


def learn_kernel(rows_ref, counts_ref, counts_t_ref, clicks_ref, lin_ref, ids_ref, out_ref):
    rows = rows_ref[...].reshape(SLOTS, K)
    wide_rows = rows.astype(f32)
    counts = counts_ref[...]
    sums = dot(counts, rows)
    square = wide_rows * wide_rows
    high = square.astype(bf16)
    low = (square - high.astype(f32)).astype(bf16)
    terms = sums * sums - dot(counts, high) - dot(counts, low)
    terms = 0.5 * (terms[:, :128] + terms[:, 128:]) + dot(counts, lin_ref[...])
    logits = jnp.sum(terms, axis=1, keepdims=True)
    errors = jnp.broadcast_to(jax.nn.sigmoid(logits) - clicks_ref[...], (SAMPLES, 128))
    first = errors.astype(bf16)
    second = (errors - first.astype(f32)).astype(bf16)
    weighted = (jnp.concatenate([errors, errors], axis=1) * sums).astype(bf16)
    counts_t = counts_t_ref[...]
    error_sums = dot(counts_t, jnp.concatenate([first, second], axis=1))
    error_sums = error_sums[:, :128] + error_sums[:, 128:]
    gathered = dot(counts_t, weighted)
    left = gathered[:, :128] - error_sums * wide_rows[:, :128]
    right = gathered[:, 128:] - error_sums * wide_rows[:, 128:]
    out_ref[:, :CAP, :] = left.astype(bf16).reshape(OWNERS, CAP, 128)
    out_ref[:, CAP : 2 * CAP, :] = right.astype(bf16).reshape(OWNERS, CAP, 128)
    place = lax.rem(lax.axis_index("server"), 8)
    pair = jnp.where(iota((SAMPLES, 128), 1) < 8, first.astype(f32), second.astype(f32)).astype(bf16)
    sums_row = dot(pair, counts, 0, 0)
    sums_row = sums_row[:8] + sums_row[8:16]
    high = sums_row.astype(bf16).astype(f32)
    row = iota((8, SLOTS), 0)
    sums_row = jnp.where(row == 0, high, jnp.where(row == 1, sums_row - high, ids_ref[...]))
    mine = jnp.right_shift(iota((8, 128), 1), 4) == place
    for owner in range(OWNERS):
        lanes = owner // 8 * 128
        turn = lax.rem(place + 8 - owner % 8, 8) * CAP
        tile = pltpu.roll(sums_row[:, lanes : lanes + 128], turn, 1)
        out_ref[owner, 2 * CAP :, :] = jnp.where(mine, tile, 0.0).astype(bf16)


def part_rows(x):
    rows = iota((8, x.shape[1]), 0)
    first = x.astype(bf16).astype(f32)
    rest = x - first
    second = rest.astype(bf16).astype(f32)
    third = rest - second
    return jnp.where(rows == 0, first, jnp.where(rows == 1, second, jnp.where(rows == 2, third, 0.0)))


def scatter_kernel(push_ref, out_ref):
    core = lax.axis_index("core")
    chunks = []
    for q in range(N_CORE * OWNERS // 8):
        chunk = push_ref[8 * q, 2 * CAP :, :].astype(f32)
        for i in range(1, 8):
            chunk = chunk + push_ref[8 * q + i, 2 * CAP :, :].astype(f32)
        chunks.append(chunk)
    tails = jnp.concatenate(chunks, axis=1)
    row = iota(tails.shape, 0)
    asked = jnp.sum(jnp.where((row == 2) | (row == 3), tails, 0.0), axis=0, keepdims=True)
    asked = asked.astype(jnp.int32)
    ours = jnp.bitwise_and(jnp.right_shift(asked, 5), 1) == core
    place = jnp.right_shift(asked, 6) * SHARE + jnp.bitwise_and(asked, SHARE - 1)
    place = jnp.where(ours, place, -1)
    hot = (iota((ROWS // N_CORE, N_CORE * SLOTS), 0) == place).astype(f32).astype(bf16)
    left = push_ref[:, :CAP, :].reshape(N_CORE * SLOTS, 128)
    right = push_ref[:, CAP : 2 * CAP, :].reshape(N_CORE * SLOTS, 128)
    total = dot(hot, jnp.concatenate([left, right], axis=1)).astype(bf16)
    out_ref[:, :SHARE, :] = total[:, :128].reshape(N_Y, SHARE, 128)
    out_ref[:, SHARE : 2 * SHARE, :] = total[:, 128:].reshape(N_Y, SHARE, 128)
    linear = dot(jnp.where(row < 2, tails, 0.0).astype(bf16), hot, 1, 1)
    linear = part_rows(jnp.sum(linear, axis=0, keepdims=True))
    for y in range(N_Y):
        lanes = y // 4 * 128
        turn = lax.rem(N_CORE * y + core + 4 - y % 4, 4) * SHARE
        out_ref[y, 2 * SHARE :, :] = pltpu.roll(linear[:, lanes : lanes + 128], turn, 1).astype(bf16)


def add_parts(part_ref):
    total = part_ref[0].astype(f32)
    for y in range(1, N_Y):
        total = total + part_ref[y].astype(f32)
    left, right = total[:SHARE], total[SHARE : 2 * SHARE]
    return left, right, jnp.sum(total[2 * SHARE :], axis=0, keepdims=True)


def my_lanes():
    me = lax.axis_index("y") * N_CORE + lax.axis_index("core")
    return jnp.right_shift(iota((1, 128), 1), 5) == lax.rem(me, 4)


def update_kernel(part_ref, acc_ref, acc_lin_ref, delta_ref):
    left, right, linear = add_parts(part_ref)
    acc = acc_ref[...]

    def step(grad, state):
        return step_size * grad / jnp.sqrt(state + grad * grad)

    left = step(left, acc[:, :128]).astype(bf16)
    right = step(right, acc[:, 128:]).astype(bf16)
    linear = part_rows(jnp.where(my_lanes(), step(linear, acc_lin_ref[...]), 0.0)).astype(bf16)
    for y in range(N_Y):
        delta_ref[y, :SHARE, :] = left
        delta_ref[y, SHARE : 2 * SHARE, :] = right
        delta_ref[y, 2 * SHARE :, :] = linear


def write_state(part_ref, acc_ref, acc_lin_ref, new_acc_ref, new_acc_lin_ref):
    left, right, linear = add_parts(part_ref)
    new_acc_ref[:, :128] = acc_ref[:, :128] + left * left
    new_acc_ref[:, 128:] = acc_ref[:, 128:] + right * right
    state = jnp.where(my_lanes(), acc_lin_ref[...] + linear * linear, 0.0)
    column = jnp.sum(jnp.where(of_share(), state, 0.0), axis=1, keepdims=True)
    same = iota((SHARE, SHARE), 0) == iota((SHARE, SHARE), 1)
    new_acc_lin_ref[...] = jnp.sum(jnp.where(same, column, 0.0), axis=0, keepdims=True)


def apply_kernel(
    delta_ref,
    factors_ref,
    linear_ref,
    part_ref,
    acc_ref,
    acc_lin_ref,
    new_factors_ref,
    new_linear_ref,
    new_acc_ref,
    new_acc_lin_ref,
):
    write_state(part_ref, acc_ref, acc_lin_ref, new_acc_ref, new_acc_lin_ref)
    for q in range(4):
        lin = jnp.zeros((8, 128), f32)
        for w in range(4 * q, 4 * q + 4):
            block = delta_ref[w % N_CORE * N_Y + w // N_CORE].astype(f32)
            here = pl.ds(w * SHARE, SHARE)
            new_factors_ref[here, :128] = factors_ref[here, :128] - block[:SHARE]
            new_factors_ref[here, 128:] = factors_ref[here, 128:] - block[SHARE : 2 * SHARE]
            lin = lin + block[2 * SHARE :]
        lanes = pl.ds(q * 128, 128)
        new_linear_ref[:, lanes] = linear_ref[:, lanes] - jnp.sum(lin, axis=0, keepdims=True)


def call(kernel, out, flops, *args, scratch=(), far=False):
    size = sum(a.size * a.dtype.itemsize for a in args)
    if far:
        args = [pltpu.with_memory_space_constraint(a, pltpu.HBM) for a in args]
    return pl.pallas_call(
        kernel,
        out_shape=out,
        in_specs=[pl.BlockSpec(memory_space=pltpu.HBM if far else pltpu.VMEM)] * len(args),
        out_specs=jax.tree.map(lambda _: pl.BlockSpec(memory_space=pltpu.VMEM), out),
        scratch_shapes=scratch,
        compiler_params=pltpu.CompilerParams(vmem_limit_bytes=24 * 1024 * 1024),
        cost_estimate=pl.CostEstimate(flops=flops, bytes_accessed=size, transcendentals=0),
    )(*args)


def shape(dims, dtype):
    return jax.ShapeDtypeStruct(dims, dtype)


def exchange(x, axis):
    return lax.all_to_all(x, axis, split_axis=0, concat_axis=0, tiled=True)


TALL = 2 * SHARE + 8


def body(factors, linear, acc_factors, acc_linear, feature_slot, requests, clicks):
    dma = pltpu.SemaphoreType.DMA
    req_t = requests.T
    ask, wide = call(
        ask_kernel,
        [shape((OWNERS, 8, 128), bf16), shape((ROWS, K), f32)],
        1 << 20,
        req_t,
        linear.reshape(4, 128),
        factors,
        scratch=[pltpu.VMEM((CAP, OWNERS), jnp.int32), pltpu.VMEM((4, 128), f32), dma((3,))],
        far=True,
    )
    got = exchange(ask, "server")
    found = call(gather_kernel, shape((OWNERS, CAP, K), bf16), 1 << 28, got, wide)
    rows = exchange(found, "server")
    lin_terms, ids, counts_t, counts, clicks_col, acc, acc_lin, lin_row = call(
        side_kernel,
        [
            shape((SLOTS, 128), bf16),
            shape((8, SLOTS), f32),
            shape((SLOTS, SAMPLES), bf16),
            shape((SAMPLES, SLOTS), bf16),
            shape((SAMPLES, 1), f32),
            shape((SHARE, K), f32),
            shape((1, 128), f32),
            shape((1, ROWS), f32),
        ],
        1 << 30,
        got,
        req_t,
        feature_slot.T,
        clicks.reshape(1, SAMPLES),
        acc_factors,
        acc_linear.reshape(1, SHARE),
        linear.reshape(1, ROWS),
    )
    push = call(
        learn_kernel,
        shape((OWNERS, 2 * CAP + 8, 128), bf16),
        1 << 28,
        rows,
        counts,
        counts_t,
        clicks_col,
        lin_terms,
        ids,
    )
    pushed = exchange(push, "server")
    pushed = lax.all_gather(pushed, "core", axis=0, tiled=True)
    dense = call(scatter_kernel, shape((N_Y, TALL, 128), bf16), 1 << 28, pushed)
    shared = exchange(dense, "y")
    delta = call(update_kernel, shape((N_Y, TALL, 128), bf16), 1 << 20, shared, acc, acc_lin)
    deltas = exchange(delta, "y")
    deltas = lax.all_gather(deltas, "core", axis=0, tiled=True)
    new_factors, new_linear, new_acc, new_acc_lin = call(
        apply_kernel,
        [shape((ROWS, K), f32), shape((1, ROWS), f32), shape((SHARE, K), f32), shape((1, SHARE), f32)],
        1 << 20,
        deltas,
        wide,
        lin_row,
        shared,
        acc,
        acc_lin,
    )
    return new_factors, new_linear.reshape(ROWS), new_acc, new_acc_lin.reshape(SHARE)


def solution(mesh):
    mesh = Mesh(mesh.devices.reshape(OWNERS, N_Y, N_CORE), ("server", "y", "core"))
    every = ("server", "y", "core")
    in_specs = (
        P("server", None),
        P("server"),
        P(every, None),
        P(every),
        P(every, None),
        P(every, None),
        P(every),
    )
    out_specs = (P("server", None), P("server"), P(every, None), P(every))
    return jax.shard_map(body, mesh=mesh, in_specs=in_specs, out_specs=out_specs, check_vma=False)
```

```python
import jax
import jax.numpy as jnp
from jax import lax
from jax.experimental import pallas as pl
from jax.experimental.pallas import tpu as pltpu
from jax.sharding import Mesh, PartitionSpec as P

step_size = 0.5
bf16 = jnp.bfloat16
f32 = jnp.float32

OWNERS = 32
CAP = 16
SLOTS = OWNERS * CAP
ROWS = 512
K = 256
SAMPLES = 256
FIELDS = 39
N_Y = 8
N_CORE = 2
N_WORKER = N_Y * N_CORE
SHARE = ROWS // N_WORKER


def iota(shape, axis):
    return lax.broadcasted_iota(jnp.int32, shape, axis)


def dot(a, b, ca=1, cb=0):
    return lax.dot_general(a, b, (((ca,), (cb,)), ((), ())), preferred_element_type=f32)


def split_requests(req_t):
    high = jnp.bitwise_and(req_t, -16)
    low = jnp.bitwise_and(req_t, 15)
    pad = jnp.zeros((96, OWNERS), jnp.int32)
    return jnp.concatenate([high, low, pad], axis=0).astype(f32).astype(bf16)


def own_lists(req_t, rows):
    owner = jnp.right_shift(iota((OWNERS * rows, OWNERS), 0), 4 if rows == CAP else 3)
    mine = (owner == iota((OWNERS * rows, OWNERS), 1)).astype(f32).astype(bf16)
    lists = dot(mine, split_requests(req_t), 1, 1)
    lane = iota((OWNERS * rows, 128), 1)
    position = jnp.bitwise_and(iota((OWNERS * rows, 128), 0), rows - 1)
    keep = (lane < 2 * CAP) & (jnp.bitwise_and(lane, rows - 1) == position)
    return jnp.where(keep, lists, 0.0)


def asked_rows(got):
    got = got.astype(f32)
    lane = iota(got.shape, 2)
    upper = jnp.bitwise_and(lane, 8) == 8
    got = jnp.where(lane < 2 * CAP, got, 0.0)
    split = jnp.concatenate([jnp.where(upper, 0.0, got), jnp.where(upper, got, 0.0)], axis=1)
    return jnp.sum(split.reshape(SLOTS, 128), axis=1, keepdims=True)


def ones(dims, axis):
    return (iota(dims, axis) < 2 * CAP).astype(f32).astype(bf16)


def ask_kernel(req_t_hbm, lin_hbm, factors_hbm, out_ref, factors_ref, req_t_ref, lin_ref, sems):
    copies = [
        pltpu.make_async_copy(req_t_hbm, req_t_ref, sems.at[0]),
        pltpu.make_async_copy(lin_hbm, lin_ref, sems.at[1]),
        pltpu.make_async_copy(factors_hbm, factors_ref, sems.at[2]),
    ]
    for copy in copies:
        copy.start()
    for copy in copies[:2]:
        copy.wait()
    lists = own_lists(req_t_ref[...], 8)
    spread = (jnp.right_shift(iota((8, 4), 0), 1) == iota((8, 4), 1)).astype(f32).astype(bf16)
    lin = dot(spread, lin_ref[...].astype(bf16))
    odd = jnp.bitwise_and(iota((8, 128), 0), 1) == 1
    lin = jnp.where(odd, lin, pltpu.roll(lin, 64, 1))
    lin = jnp.where(iota((8, 128), 1) >= 64, lin, 0.0)
    out_ref[...] = (lists.reshape(OWNERS, 8, 128) + lin[None]).astype(bf16)
    copies[2].wait()


def of_share():
    return jnp.bitwise_and(iota((SHARE, 128), 1), SHARE - 1) == iota((SHARE, 128), 0)


def gather_kernel(got_ref, factors_ref, out_ref):
    asked = asked_rows(got_ref[...])
    hot = (asked == iota((SLOTS, ROWS), 1).astype(f32)).astype(f32).astype(bf16)
    out_ref[...] = dot(hot, factors_ref[...].astype(bf16)).astype(bf16).reshape(OWNERS, CAP, K)


def side_kernel(
    got_ref,
    req_t_ref,
    fs_t_ref,
    clicks_ref,
    acc_in,
    acc_lin_row_ref,
    linear_in,
    lin_ref,
    ids_ref,
    counts_t_ref,
    counts_ref,
    clicks_col_ref,
    acc_ref,
    acc_lin_ref,
    linear_ref,
):
    acc_ref[...] = acc_in[...]
    linear_ref[...] = linear_in[...]
    got = got_ref[...].astype(f32).reshape(8 * OWNERS, 128).astype(bf16)
    lists = own_lists(req_t_ref[...], CAP).astype(bf16)
    wanted = dot(lists, ones((128, 8 * OWNERS), 0)).astype(jnp.int32)
    first = jnp.right_shift(iota((SLOTS, 8 * OWNERS), 0), 4) * 8
    pick = iota((SLOTS, 8 * OWNERS), 1) == first + jnp.right_shift(wanted, 6)
    values = dot(pick.astype(f32).astype(bf16), got)
    here = iota((SLOTS, 128), 1) == jnp.bitwise_and(wanted[:, :128], 63) + 64
    lin_terms = jnp.where(here, values, 0.0).astype(bf16)
    spread = jnp.right_shift(iota((OWNERS, SLOTS), 1), 4) == iota((OWNERS, SLOTS), 0)
    lists = dot(split_requests(req_t_ref[...]), spread.astype(f32).astype(bf16))
    place = iota((128, SLOTS), 0)
    position = jnp.bitwise_and(iota((128, SLOTS), 1), CAP - 1)
    high = jnp.sum(jnp.where(place == position, lists, 0.0), axis=0, keepdims=True)
    low = jnp.sum(jnp.where(place == position + CAP, lists, 0.0), axis=0, keepdims=True)
    row = iota((8, SLOTS), 0)
    ids_ref[...] = jnp.where(row == 2, high, jnp.where(row == 3, low, 0.0))
    same_share = iota((SHARE, SHARE), 0) == iota((SHARE, SHARE), 1)
    acc_lin = jnp.sum(jnp.where(same_share, acc_lin_row_ref[...], 0.0), axis=1, keepdims=True)
    acc_lin_ref[...] = jnp.sum(jnp.where(of_share(), acc_lin, 0.0), axis=0, keepdims=True)
    chunk = 64

    def one(i, carry):
        base = pl.multiple_of(i * chunk, chunk)
        slots = iota((chunk, SAMPLES), 0) + base
        total = jnp.zeros((chunk, SAMPLES), f32)
        for f in range(FIELDS):
            total = total + jnp.where(fs_t_ref[pl.ds(f, 1), :] == slots, 1.0, 0.0)
        counts_t_ref[pl.ds(base, chunk), :] = total.astype(bf16)
        return carry

    lax.fori_loop(0, SLOTS // chunk, one, 0)
    counts = jnp.transpose(counts_t_ref[...].astype(f32)).astype(bf16)
    counts_ref[...] = counts
    lin_ref[...] = dot(counts, lin_terms)
    same = iota((SAMPLES, SAMPLES), 0) == iota((SAMPLES, SAMPLES), 1)
    clicks = clicks_ref[...].astype(f32)
    clicks_col_ref[...] = jnp.sum(jnp.where(same, clicks, 0.0), axis=1, keepdims=True)


def learn_kernel(rows_ref, counts_ref, counts_t_ref, clicks_ref, lin_ref, ids_ref, out_ref):
    rows = rows_ref[...].reshape(SLOTS, K)
    wide_rows = rows.astype(f32)
    counts = counts_ref[...]
    sums = dot(counts, rows)
    square = wide_rows * wide_rows
    square = square[:, :128] + square[:, 128:]
    high = square.astype(bf16)
    rest = square - high.astype(f32)
    middle = rest.astype(bf16)
    low = (rest - middle.astype(f32)).astype(bf16)
    terms = sums * sums - dot(counts, jnp.concatenate([high, middle], axis=1))
    terms = 0.5 * (terms[:, :128] + terms[:, 128:] - dot(counts, low)) + lin_ref[...]
    logits = jnp.sum(terms, axis=1, keepdims=True)
    errors = jnp.broadcast_to(jax.nn.sigmoid(logits) - clicks_ref[...], (SAMPLES, 128))
    first = errors.astype(bf16)
    second = (errors - first.astype(f32)).astype(bf16)
    weighted = (jnp.concatenate([errors, errors], axis=1) * sums).astype(bf16)
    counts_t = counts_t_ref[...]
    error_sums = dot(counts_t, jnp.concatenate([first, second], axis=1))
    error_sums = error_sums[:, :128] + error_sums[:, 128:]
    gathered = dot(counts_t, weighted)
    left = gathered[:, :128] - error_sums * wide_rows[:, :128]
    right = gathered[:, 128:] - error_sums * wide_rows[:, 128:]
    out_ref[:, :CAP, :] = left.astype(bf16).reshape(OWNERS, CAP, 128)
    out_ref[:, CAP : 2 * CAP, :] = right.astype(bf16).reshape(OWNERS, CAP, 128)
    place = lax.rem(lax.axis_index("server"), 8)
    pair = jnp.where(iota((SAMPLES, 128), 1) < 8, first.astype(f32), second.astype(f32)).astype(bf16)
    sums_row = dot(pair, counts, 0, 0)
    sums_row = sums_row[:8] + sums_row[8:16]
    high = sums_row.astype(bf16).astype(f32)
    row = iota((8, SLOTS), 0)
    sums_row = jnp.where(row == 0, high, jnp.where(row == 1, sums_row - high, ids_ref[...]))
    mine = jnp.right_shift(iota((8, 128), 1), 4) == place
    for owner in range(OWNERS):
        lanes = owner // 8 * 128
        turn = lax.rem(place + 8 - owner % 8, 8) * CAP
        tile = pltpu.roll(sums_row[:, lanes : lanes + 128], turn, 1)
        out_ref[owner, 2 * CAP :, :] = jnp.where(mine, tile, 0.0).astype(bf16)


def part_rows(x):
    rows = iota((8, x.shape[1]), 0)
    first = x.astype(bf16).astype(f32)
    rest = x - first
    second = rest.astype(bf16).astype(f32)
    third = rest - second
    return jnp.where(rows == 0, first, jnp.where(rows == 1, second, jnp.where(rows == 2, third, 0.0)))


def scatter_kernel(push_ref, out_ref):
    core = lax.axis_index("core")
    chunks = []
    for q in range(N_CORE * OWNERS // 8):
        chunk = push_ref[8 * q, 2 * CAP :, :].astype(f32)
        for i in range(1, 8):
            chunk = chunk + push_ref[8 * q + i, 2 * CAP :, :].astype(f32)
        chunks.append(chunk)
    tails = jnp.concatenate(chunks, axis=1)
    row = iota(tails.shape, 0)
    asked = jnp.sum(jnp.where((row == 2) | (row == 3), tails, 0.0), axis=0, keepdims=True)
    asked = asked.astype(jnp.int32)
    ours = jnp.bitwise_and(jnp.right_shift(asked, 5), 1) == core
    place = jnp.right_shift(asked, 6) * SHARE + jnp.bitwise_and(asked, SHARE - 1)
    place = jnp.where(ours, place, -1)
    hot = (iota((ROWS // N_CORE, N_CORE * SLOTS), 0) == place).astype(f32).astype(bf16)
    left = push_ref[:, :CAP, :].reshape(N_CORE * SLOTS, 128)
    right = push_ref[:, CAP : 2 * CAP, :].reshape(N_CORE * SLOTS, 128)
    total = dot(hot, jnp.concatenate([left, right], axis=1)).astype(bf16)
    out_ref[:, :SHARE, :] = total[:, :128].reshape(N_Y, SHARE, 128)
    out_ref[:, SHARE : 2 * SHARE, :] = total[:, 128:].reshape(N_Y, SHARE, 128)
    linear = dot(jnp.where(row < 2, tails, 0.0).astype(bf16), hot, 1, 1)
    linear = part_rows(jnp.sum(linear, axis=0, keepdims=True))
    for y in range(N_Y):
        lanes = y // 4 * 128
        turn = lax.rem(N_CORE * y + core + 4 - y % 4, 4) * SHARE
        out_ref[y, 2 * SHARE :, :] = pltpu.roll(linear[:, lanes : lanes + 128], turn, 1).astype(bf16)


def add_parts(part_ref):
    total = part_ref[0].astype(f32)
    for y in range(1, N_Y):
        total = total + part_ref[y].astype(f32)
    left, right = total[:SHARE], total[SHARE : 2 * SHARE]
    return left, right, jnp.sum(total[2 * SHARE :], axis=0, keepdims=True)


def my_lanes():
    me = lax.axis_index("y") * N_CORE + lax.axis_index("core")
    return jnp.right_shift(iota((1, 128), 1), 5) == lax.rem(me, 4)


def update_kernel(part_ref, acc_ref, acc_lin_ref, delta_ref):
    left, right, linear = add_parts(part_ref)
    acc = acc_ref[...]

    def step(grad, state):
        return step_size * grad / jnp.sqrt(state + grad * grad)

    left = step(left, acc[:, :128]).astype(bf16)
    right = step(right, acc[:, 128:]).astype(bf16)
    linear = part_rows(jnp.where(my_lanes(), step(linear, acc_lin_ref[...]), 0.0)).astype(bf16)
    for y in range(N_Y):
        delta_ref[y, :SHARE, :] = left
        delta_ref[y, SHARE : 2 * SHARE, :] = right
        delta_ref[y, 2 * SHARE :, :] = linear


def write_state(part_ref, acc_ref, acc_lin_ref, new_acc_ref, new_acc_lin_ref):
    left, right, linear = add_parts(part_ref)
    new_acc_ref[:, :128] = acc_ref[:, :128] + left * left
    new_acc_ref[:, 128:] = acc_ref[:, 128:] + right * right
    state = jnp.where(my_lanes(), acc_lin_ref[...] + linear * linear, 0.0)
    column = jnp.sum(jnp.where(of_share(), state, 0.0), axis=1, keepdims=True)
    same = iota((SHARE, SHARE), 0) == iota((SHARE, SHARE), 1)
    new_acc_lin_ref[...] = jnp.sum(jnp.where(same, column, 0.0), axis=0, keepdims=True)


def apply_kernel(
    delta_ref,
    factors_ref,
    linear_ref,
    part_ref,
    acc_ref,
    acc_lin_ref,
    new_factors_ref,
    new_linear_ref,
    new_acc_ref,
    new_acc_lin_ref,
):
    write_state(part_ref, acc_ref, acc_lin_ref, new_acc_ref, new_acc_lin_ref)
    for q in range(4):
        lin = jnp.zeros((8, 128), f32)
        for w in range(4 * q, 4 * q + 4):
            block = delta_ref[w % N_CORE * N_Y + w // N_CORE].astype(f32)
            here = pl.ds(w * SHARE, SHARE)
            new_factors_ref[here, :128] = factors_ref[here, :128] - block[:SHARE]
            new_factors_ref[here, 128:] = factors_ref[here, 128:] - block[SHARE : 2 * SHARE]
            lin = lin + block[2 * SHARE :]
        lanes = pl.ds(q * 128, 128)
        new_linear_ref[:, lanes] = linear_ref[:, lanes] - jnp.sum(lin, axis=0, keepdims=True)


def call(kernel, out, flops, *args, scratch=(), far=False):
    size = sum(a.size * a.dtype.itemsize for a in args)
    if far:
        args = [pltpu.with_memory_space_constraint(a, pltpu.HBM) for a in args]
    return pl.pallas_call(
        kernel,
        out_shape=out,
        in_specs=[pl.BlockSpec(memory_space=pltpu.HBM if far else pltpu.VMEM)] * len(args),
        out_specs=jax.tree.map(lambda _: pl.BlockSpec(memory_space=pltpu.VMEM), out),
        scratch_shapes=scratch,
        compiler_params=pltpu.CompilerParams(vmem_limit_bytes=24 * 1024 * 1024),
        cost_estimate=pl.CostEstimate(flops=flops, bytes_accessed=size, transcendentals=0),
    )(*args)


def shape(dims, dtype):
    return jax.ShapeDtypeStruct(dims, dtype)


def exchange(x, axis):
    return lax.all_to_all(x, axis, split_axis=0, concat_axis=0, tiled=True)


TALL = 2 * SHARE + 8


def body(factors, linear, acc_factors, acc_linear, feature_slot, requests, clicks):
    dma = pltpu.SemaphoreType.DMA
    req_t = requests.T
    ask, wide = call(
        ask_kernel,
        [shape((OWNERS, 8, 128), bf16), shape((ROWS, K), f32)],
        1 << 20,
        req_t,
        linear.reshape(4, 128),
        factors,
        scratch=[pltpu.VMEM((CAP, OWNERS), jnp.int32), pltpu.VMEM((4, 128), f32), dma((3,))],
        far=True,
    )
    got = exchange(ask, "server")
    found = call(gather_kernel, shape((OWNERS, CAP, K), bf16), 1 << 28, got, wide)
    rows = exchange(found, "server")
    lin_terms, ids, counts_t, counts, clicks_col, acc, acc_lin, lin_row = call(
        side_kernel,
        [
            shape((SAMPLES, 128), f32),
            shape((8, SLOTS), f32),
            shape((SLOTS, SAMPLES), bf16),
            shape((SAMPLES, SLOTS), bf16),
            shape((SAMPLES, 1), f32),
            shape((SHARE, K), f32),
            shape((1, 128), f32),
            shape((1, ROWS), f32),
        ],
        1 << 30,
        got,
        req_t,
        feature_slot.T,
        clicks.reshape(1, SAMPLES),
        acc_factors,
        acc_linear.reshape(1, SHARE),
        linear.reshape(1, ROWS),
    )
    push = call(
        learn_kernel,
        shape((OWNERS, 2 * CAP + 8, 128), bf16),
        1 << 28,
        rows,
        counts,
        counts_t,
        clicks_col,
        lin_terms,
        ids,
    )
    pushed = exchange(push, "server")
    pushed = lax.all_gather(pushed, "core", axis=0, tiled=True)
    dense = call(scatter_kernel, shape((N_Y, TALL, 128), bf16), 1 << 28, pushed)
    shared = exchange(dense, "y")
    delta = call(update_kernel, shape((N_Y, TALL, 128), bf16), 1 << 20, shared, acc, acc_lin)
    deltas = exchange(delta, "y")
    deltas = lax.all_gather(deltas, "core", axis=0, tiled=True)
    new_factors, new_linear, new_acc, new_acc_lin = call(
        apply_kernel,
        [shape((ROWS, K), f32), shape((1, ROWS), f32), shape((SHARE, K), f32), shape((1, SHARE), f32)],
        1 << 20,
        deltas,
        wide,
        lin_row,
        shared,
        acc,
        acc_lin,
    )
    return new_factors, new_linear.reshape(ROWS), new_acc, new_acc_lin.reshape(SHARE)


def solution(mesh):
    mesh = Mesh(mesh.devices.reshape(OWNERS, N_Y, N_CORE), ("server", "y", "core"))
    every = ("server", "y", "core")
    in_specs = (
        P("server", None),
        P("server"),
        P(every, None),
        P(every),
        P(every, None),
        P(every, None),
        P(every),
    )
    out_specs = (P("server", None), P("server"), P(every, None), P(every))
    return jax.shard_map(body, mesh=mesh, in_specs=in_specs, out_specs=out_specs, check_vma=False)
```

```python
import jax
import jax.numpy as jnp
from jax import lax
from jax.experimental import pallas as pl
from jax.experimental.pallas import tpu as pltpu
from jax.sharding import Mesh, PartitionSpec as P

step_size = 0.5
bf16 = jnp.bfloat16
f32 = jnp.float32

OWNERS = 32
CAP = 16
SLOTS = OWNERS * CAP
ROWS = 512
K = 256
SAMPLES = 256
FIELDS = 39
N_Y = 8
N_CORE = 2
N_WORKER = N_Y * N_CORE
SHARE = ROWS // N_WORKER


def iota(shape, axis):
    return lax.broadcasted_iota(jnp.int32, shape, axis)


def dot(a, b, ca=1, cb=0):
    return lax.dot_general(a, b, (((ca,), (cb,)), ((), ())), preferred_element_type=f32)


def split_requests(req_t):
    high = jnp.bitwise_and(req_t, -16)
    low = jnp.bitwise_and(req_t, 15)
    pad = jnp.zeros((96, OWNERS), jnp.int32)
    return jnp.concatenate([high, low, pad], axis=0).astype(f32).astype(bf16)


def own_lists(req_t, rows):
    owner = jnp.right_shift(iota((OWNERS * rows, OWNERS), 0), 4 if rows == CAP else 3)
    mine = (owner == iota((OWNERS * rows, OWNERS), 1)).astype(f32).astype(bf16)
    lists = dot(mine, split_requests(req_t), 1, 1)
    lane = iota((OWNERS * rows, 128), 1)
    position = jnp.bitwise_and(iota((OWNERS * rows, 128), 0), rows - 1)
    keep = (lane < 2 * CAP) & (jnp.bitwise_and(lane, rows - 1) == position)
    return jnp.where(keep, lists, 0.0)


def asked_rows(got):
    got = got.astype(f32)
    lane = iota(got.shape, 2)
    upper = jnp.bitwise_and(lane, 8) == 8
    got = jnp.where(lane < 2 * CAP, got, 0.0)
    split = jnp.concatenate([jnp.where(upper, 0.0, got), jnp.where(upper, got, 0.0)], axis=1)
    return jnp.sum(split.reshape(SLOTS, 128), axis=1, keepdims=True)


def ones(dims, axis):
    return (iota(dims, axis) < 2 * CAP).astype(f32).astype(bf16)


def ask_kernel(req_t_hbm, lin_hbm, factors_hbm, out_ref, factors_ref, req_t_ref, lin_ref, sems):
    copies = [
        pltpu.make_async_copy(req_t_hbm, req_t_ref, sems.at[0]),
        pltpu.make_async_copy(lin_hbm, lin_ref, sems.at[1]),
        pltpu.make_async_copy(factors_hbm, factors_ref, sems.at[2]),
    ]
    for copy in copies:
        copy.start()
    for copy in copies[:2]:
        copy.wait()
    lists = own_lists(req_t_ref[...], 8)
    spread = (jnp.right_shift(iota((8, 4), 0), 1) == iota((8, 4), 1)).astype(f32).astype(bf16)
    lin = dot(spread, lin_ref[...].astype(bf16))
    odd = jnp.bitwise_and(iota((8, 128), 0), 1) == 1
    lin = jnp.where(odd, lin, pltpu.roll(lin, 64, 1))
    lin = jnp.where(iota((8, 128), 1) >= 64, lin, 0.0)
    out_ref[...] = (lists.reshape(OWNERS, 8, 128) + lin[None]).astype(bf16)
    copies[2].wait()


def of_share():
    return jnp.bitwise_and(iota((SHARE, 128), 1), SHARE - 1) == iota((SHARE, 128), 0)


def gather_kernel(got_ref, factors_ref, out_ref):
    asked = asked_rows(got_ref[...])
    hot = (asked == iota((SLOTS, ROWS), 1).astype(f32)).astype(f32).astype(bf16)
    out_ref[...] = dot(hot, factors_ref[...].astype(bf16)).astype(bf16).reshape(OWNERS, CAP, K)


def side_kernel(
    got_ref,
    req_t_ref,
    fs_t_ref,
    clicks_ref,
    acc_in,
    acc_lin_row_ref,
    linear_in,
    lin_ref,
    ids_ref,
    counts_t_ref,
    counts_ref,
    clicks_col_ref,
    acc_ref,
    acc_lin_ref,
    linear_ref,
):
    acc_ref[...] = acc_in[...]
    linear_ref[...] = linear_in[...]
    got = got_ref[...].astype(f32).reshape(8 * OWNERS, 128).astype(bf16)
    lists = own_lists(req_t_ref[...], CAP).astype(bf16)
    wanted = dot(lists, ones((128, 8 * OWNERS), 0)).astype(jnp.int32)
    first = jnp.right_shift(iota((SLOTS, 8 * OWNERS), 0), 4) * 8
    pick = iota((SLOTS, 8 * OWNERS), 1) == first + jnp.right_shift(wanted, 6)
    values = dot(pick.astype(f32).astype(bf16), got)
    here = iota((SLOTS, 128), 1) == jnp.bitwise_and(wanted[:, :128], 63) + 64
    lin_terms = jnp.where(here, values, 0.0).astype(bf16)
    spread = jnp.right_shift(iota((OWNERS, SLOTS), 1), 4) == iota((OWNERS, SLOTS), 0)
    lists = dot(split_requests(req_t_ref[...]), spread.astype(f32).astype(bf16))
    place = iota((128, SLOTS), 0)
    position = jnp.bitwise_and(iota((128, SLOTS), 1), CAP - 1)
    high = jnp.sum(jnp.where(place == position, lists, 0.0), axis=0, keepdims=True)
    low = jnp.sum(jnp.where(place == position + CAP, lists, 0.0), axis=0, keepdims=True)
    row = iota((8, SLOTS), 0)
    ids_ref[...] = jnp.where(row == 2, high, jnp.where(row == 3, low, 0.0))
    same_share = iota((SHARE, SHARE), 0) == iota((SHARE, SHARE), 1)
    acc_lin = jnp.sum(jnp.where(same_share, acc_lin_row_ref[...], 0.0), axis=1, keepdims=True)
    acc_lin_ref[...] = jnp.sum(jnp.where(of_share(), acc_lin, 0.0), axis=0, keepdims=True)
    chunk = 64

    def one(i, carry):
        base = pl.multiple_of(i * chunk, chunk)
        slots = iota((chunk, SAMPLES), 0) + base
        total = jnp.zeros((chunk, SAMPLES), f32)
        for f in range(FIELDS):
            total = total + jnp.where(fs_t_ref[pl.ds(f, 1), :] == slots, 1.0, 0.0)
        counts_t_ref[pl.ds(base, chunk), :] = total.astype(bf16)
        return carry

    lax.fori_loop(0, SLOTS // chunk, one, 0)
    counts = jnp.transpose(counts_t_ref[...].astype(f32)).astype(bf16)
    counts_ref[...] = counts
    lin_ref[...] = dot(counts, lin_terms)
    same = iota((SAMPLES, SAMPLES), 0) == iota((SAMPLES, SAMPLES), 1)
    clicks = clicks_ref[...].astype(f32)
    clicks_col_ref[...] = jnp.sum(jnp.where(same, clicks, 0.0), axis=1, keepdims=True)


def learn_kernel(rows_ref, counts_ref, counts_t_ref, clicks_ref, lin_ref, ids_ref, out_ref):
    rows = rows_ref[...].reshape(SLOTS, K)
    wide_rows = rows.astype(f32)
    counts = counts_ref[...]
    sums = dot(counts, rows)
    square = wide_rows * wide_rows
    square = square[:, :128] + square[:, 128:]
    high = square.astype(bf16)
    rest = square - high.astype(f32)
    middle = rest.astype(bf16)
    low = (rest - middle.astype(f32)).astype(bf16)
    terms = sums * sums - dot(counts, jnp.concatenate([high, middle], axis=1))
    terms = 0.5 * (terms[:, :128] + terms[:, 128:] - dot(counts, low)) + lin_ref[...]
    logits = jnp.sum(terms, axis=1, keepdims=True)
    errors = jnp.broadcast_to(jax.nn.sigmoid(logits) - clicks_ref[...], (SAMPLES, 128))
    first = errors.astype(bf16)
    second = (errors - first.astype(f32)).astype(bf16)
    weighted = (jnp.concatenate([errors, errors], axis=1) * sums).astype(bf16)
    counts_t = counts_t_ref[...]
    error_sums = dot(counts_t, jnp.concatenate([first, second], axis=1))
    error_sums = error_sums[:, :128] + error_sums[:, 128:]
    gathered = dot(counts_t, weighted)
    left = gathered[:, :128] - error_sums * wide_rows[:, :128]
    right = gathered[:, 128:] - error_sums * wide_rows[:, 128:]
    out_ref[:, :CAP, :] = left.astype(bf16).reshape(OWNERS, CAP, 128)
    out_ref[:, CAP : 2 * CAP, :] = right.astype(bf16).reshape(OWNERS, CAP, 128)
    place = lax.rem(lax.axis_index("server"), 8)
    pair = jnp.where(iota((SAMPLES, 128), 1) < 8, first.astype(f32), second.astype(f32)).astype(bf16)
    sums_row = dot(pair, counts, 0, 0)
    sums_row = sums_row[:8] + sums_row[8:16]
    high = sums_row.astype(bf16).astype(f32)
    row = iota((8, SLOTS), 0)
    sums_row = jnp.where(row == 0, high, jnp.where(row == 1, sums_row - high, ids_ref[...]))
    mine = jnp.right_shift(iota((8, 128), 1), 4) == place
    for owner in range(OWNERS):
        lanes = owner // 8 * 128
        turn = lax.rem(place + 8 - owner % 8, 8) * CAP
        tile = pltpu.roll(sums_row[:, lanes : lanes + 128], turn, 1)
        out_ref[owner, 2 * CAP :, :] = jnp.where(mine, tile, 0.0).astype(bf16)


def part_rows(x):
    rows = iota((8, x.shape[1]), 0)
    first = x.astype(bf16).astype(f32)
    rest = x - first
    second = rest.astype(bf16).astype(f32)
    third = rest - second
    return jnp.where(rows == 0, first, jnp.where(rows == 1, second, jnp.where(rows == 2, third, 0.0)))


def scatter_kernel(push_ref, out_ref):
    core = lax.axis_index("core")
    chunks = []
    for q in range(N_CORE * OWNERS // 8):
        chunk = push_ref[8 * q, 2 * CAP :, :].astype(f32)
        for i in range(1, 8):
            chunk = chunk + push_ref[8 * q + i, 2 * CAP :, :].astype(f32)
        chunks.append(chunk)
    tails = jnp.concatenate(chunks, axis=1)
    row = iota(tails.shape, 0)
    asked = jnp.sum(jnp.where((row == 2) | (row == 3), tails, 0.0), axis=0, keepdims=True)
    hot = (iota((ROWS, N_CORE * SLOTS), 0) == asked.astype(jnp.int32)).astype(f32).astype(bf16)
    half = push_ref[:, pl.ds(pl.multiple_of(core * CAP, CAP), CAP), :].reshape(N_CORE * SLOTS, 128)
    out_ref[:, :SHARE, :] = dot(hot, half).astype(bf16).reshape(N_WORKER, SHARE, 128)
    linear = dot(jnp.where(row < 2, tails, 0.0).astype(bf16), hot, 1, 1)
    linear = part_rows(jnp.sum(linear, axis=0, keepdims=True)).astype(bf16)
    for w in range(N_WORKER):
        lanes = w // 4 * 128
        out_ref[w, SHARE:, :] = linear[:, lanes : lanes + 128]


def add_parts(part_ref):
    left, right = part_ref[0].astype(f32), part_ref[1].astype(f32)
    for y in range(1, N_Y):
        left = left + part_ref[N_CORE * y].astype(f32)
        right = right + part_ref[N_CORE * y + 1].astype(f32)
    return left[:SHARE], right[:SHARE], jnp.sum(left[SHARE:], axis=0, keepdims=True)


def my_lanes():
    me = lax.axis_index("y") * N_CORE + lax.axis_index("core")
    return jnp.right_shift(iota((1, 128), 1), 5) == lax.rem(me, 4)


def update_kernel(part_ref, acc_ref, acc_lin_ref, delta_ref):
    left, right, linear = add_parts(part_ref)
    acc = acc_ref[...]

    def step(grad, state):
        return step_size * grad / jnp.sqrt(state + grad * grad)

    left = step(left, acc[:, :128]).astype(bf16)
    right = step(right, acc[:, 128:]).astype(bf16)
    linear = part_rows(jnp.where(my_lanes(), step(linear, acc_lin_ref[...]), 0.0)).astype(bf16)
    for w in range(N_WORKER):
        delta_ref[w, :SHARE, :] = right if w % N_CORE else left
        delta_ref[w, SHARE:, :] = linear


def write_state(part_ref, acc_ref, acc_lin_ref, new_acc_ref, new_acc_lin_ref):
    left, right, linear = add_parts(part_ref)
    new_acc_ref[:, :128] = acc_ref[:, :128] + left * left
    new_acc_ref[:, 128:] = acc_ref[:, 128:] + right * right
    state = jnp.where(my_lanes(), acc_lin_ref[...] + linear * linear, 0.0)
    column = jnp.sum(jnp.where(of_share(), state, 0.0), axis=1, keepdims=True)
    same = iota((SHARE, SHARE), 0) == iota((SHARE, SHARE), 1)
    new_acc_lin_ref[...] = jnp.sum(jnp.where(same, column, 0.0), axis=0, keepdims=True)


def apply_kernel(
    delta_ref,
    factors_ref,
    linear_ref,
    part_ref,
    acc_ref,
    acc_lin_ref,
    new_factors_ref,
    new_linear_ref,
    new_acc_ref,
    new_acc_lin_ref,
):
    write_state(part_ref, acc_ref, acc_lin_ref, new_acc_ref, new_acc_lin_ref)
    for q in range(4):
        lin = jnp.zeros((8, 128), f32)
        for w in range(4 * q, 4 * q + 4):
            block = delta_ref[w].astype(f32)
            here = pl.ds(w * SHARE, SHARE)
            new_factors_ref[here, :128] = factors_ref[here, :128] - block[:SHARE]
            other = delta_ref[N_WORKER + w, :SHARE, :].astype(f32)
            new_factors_ref[here, 128:] = factors_ref[here, 128:] - other
            lin = lin + block[SHARE:]
        lanes = pl.ds(q * 128, 128)
        new_linear_ref[:, lanes] = linear_ref[:, lanes] - jnp.sum(lin, axis=0, keepdims=True)


def call(kernel, out, flops, *args, scratch=(), far=False):
    size = sum(a.size * a.dtype.itemsize for a in args)
    if far:
        args = [pltpu.with_memory_space_constraint(a, pltpu.HBM) for a in args]
    return pl.pallas_call(
        kernel,
        out_shape=out,
        in_specs=[pl.BlockSpec(memory_space=pltpu.HBM if far else pltpu.VMEM)] * len(args),
        out_specs=jax.tree.map(lambda _: pl.BlockSpec(memory_space=pltpu.VMEM), out),
        scratch_shapes=scratch,
        compiler_params=pltpu.CompilerParams(vmem_limit_bytes=24 * 1024 * 1024),
        cost_estimate=pl.CostEstimate(flops=flops, bytes_accessed=size, transcendentals=0),
    )(*args)


def shape(dims, dtype):
    return jax.ShapeDtypeStruct(dims, dtype)


def exchange(x, axis):
    return lax.all_to_all(x, axis, split_axis=0, concat_axis=0, tiled=True)


TALL = SHARE + 8


def body(factors, linear, acc_factors, acc_linear, feature_slot, requests, clicks):
    dma = pltpu.SemaphoreType.DMA
    req_t = requests.T
    ask, wide = call(
        ask_kernel,
        [shape((OWNERS, 8, 128), bf16), shape((ROWS, K), f32)],
        1 << 20,
        req_t,
        linear.reshape(4, 128),
        factors,
        scratch=[pltpu.VMEM((CAP, OWNERS), jnp.int32), pltpu.VMEM((4, 128), f32), dma((3,))],
        far=True,
    )
    got = exchange(ask, "server")
    found = call(gather_kernel, shape((OWNERS, CAP, K), bf16), 1 << 28, got, wide)
    rows = exchange(found, "server")
    lin_terms, ids, counts_t, counts, clicks_col, acc, acc_lin, lin_row = call(
        side_kernel,
        [
            shape((SAMPLES, 128), f32),
            shape((8, SLOTS), f32),
            shape((SLOTS, SAMPLES), bf16),
            shape((SAMPLES, SLOTS), bf16),
            shape((SAMPLES, 1), f32),
            shape((SHARE, K), f32),
            shape((1, 128), f32),
            shape((1, ROWS), f32),
        ],
        1 << 30,
        got,
        req_t,
        feature_slot.T,
        clicks.reshape(1, SAMPLES),
        acc_factors,
        acc_linear.reshape(1, SHARE),
        linear.reshape(1, ROWS),
    )
    push = call(
        learn_kernel,
        shape((OWNERS, 2 * CAP + 8, 128), bf16),
        1 << 28,
        rows,
        counts,
        counts_t,
        clicks_col,
        lin_terms,
        ids,
    )
    pushed = exchange(push, "server")
    pushed = lax.all_gather(pushed, "core", axis=0, tiled=True)
    dense = call(scatter_kernel, shape((N_WORKER, TALL, 128), bf16), 1 << 28, pushed)
    shared = exchange(dense, ("y", "core"))
    delta = call(update_kernel, shape((N_WORKER, TALL, 128), bf16), 1 << 20, shared, acc, acc_lin)
    deltas = exchange(delta, ("y", "core"))
    deltas = lax.all_gather(deltas, "core", axis=0, tiled=True)
    new_factors, new_linear, new_acc, new_acc_lin = call(
        apply_kernel,
        [shape((ROWS, K), f32), shape((1, ROWS), f32), shape((SHARE, K), f32), shape((1, SHARE), f32)],
        1 << 20,
        deltas,
        wide,
        lin_row,
        shared,
        acc,
        acc_lin,
    )
    return new_factors, new_linear.reshape(ROWS), new_acc, new_acc_lin.reshape(SHARE)


def solution(mesh):
    mesh = Mesh(mesh.devices.reshape(OWNERS, N_Y, N_CORE), ("server", "y", "core"))
    every = ("server", "y", "core")
    in_specs = (
        P("server", None),
        P("server"),
        P(every, None),
        P(every),
        P(every, None),
        P(every, None),
        P(every),
    )
    out_specs = (P("server", None), P("server"), P(every, None), P(every))
    return jax.shard_map(body, mesh=mesh, in_specs=in_specs, out_specs=out_specs, check_vma=False)
```

```python
import jax
import jax.numpy as jnp
from jax import lax
from jax.experimental import pallas as pl
from jax.experimental.pallas import tpu as pltpu
from jax.sharding import Mesh, PartitionSpec as P

step_size = 0.5
bf16 = jnp.bfloat16
f32 = jnp.float32

OWNERS = 32
CAP = 16
SLOTS = OWNERS * CAP
ROWS = 512
K = 256
SAMPLES = 256
FIELDS = 39
N_Y = 8
N_CORE = 2
N_WORKER = N_Y * N_CORE
SHARE = ROWS // N_WORKER


def iota(shape, axis):
    return lax.broadcasted_iota(jnp.int32, shape, axis)


def dot(a, b, ca=1, cb=0):
    return lax.dot_general(a, b, (((ca,), (cb,)), ((), ())), preferred_element_type=f32)


def split_requests(req_t):
    high = jnp.bitwise_and(req_t, -16)
    low = jnp.bitwise_and(req_t, 15)
    pad = jnp.zeros((96, OWNERS), jnp.int32)
    return jnp.concatenate([high, low, pad], axis=0).astype(f32).astype(bf16)


def own_lists(req_t, rows):
    owner = jnp.right_shift(iota((OWNERS * rows, OWNERS), 0), 4 if rows == CAP else 3)
    mine = (owner == iota((OWNERS * rows, OWNERS), 1)).astype(f32).astype(bf16)
    lists = dot(mine, split_requests(req_t), 1, 1)
    lane = iota((OWNERS * rows, 128), 1)
    position = jnp.bitwise_and(iota((OWNERS * rows, 128), 0), rows - 1)
    keep = (lane < 2 * CAP) & (jnp.bitwise_and(lane, rows - 1) == position)
    return jnp.where(keep, lists, 0.0)


def asked_rows(got):
    got = got.astype(f32)
    lane = iota(got.shape, 2)
    upper = jnp.bitwise_and(lane, 8) == 8
    got = jnp.where(lane < 2 * CAP, got, 0.0)
    split = jnp.concatenate([jnp.where(upper, 0.0, got), jnp.where(upper, got, 0.0)], axis=1)
    return jnp.sum(split.reshape(SLOTS, 128), axis=1, keepdims=True)


def ones(dims, axis):
    return (iota(dims, axis) < 2 * CAP).astype(f32).astype(bf16)


def ask_kernel(req_t_hbm, lin_hbm, out_ref, req_t_ref, lin_ref, sems):
    copies = [
        pltpu.make_async_copy(req_t_hbm, req_t_ref, sems.at[0]),
        pltpu.make_async_copy(lin_hbm, lin_ref, sems.at[1]),
    ]
    for copy in copies:
        copy.start()
    for copy in copies:
        copy.wait()
    lists = own_lists(req_t_ref[...], 8)
    spread = (jnp.right_shift(iota((8, 4), 0), 1) == iota((8, 4), 1)).astype(f32).astype(bf16)
    lin = dot(spread, lin_ref[...].astype(bf16))
    odd = jnp.bitwise_and(iota((8, 128), 0), 1) == 1
    lin = jnp.where(odd, lin, pltpu.roll(lin, 64, 1))
    lin = jnp.where(iota((8, 128), 1) >= 64, lin, 0.0)
    out_ref[...] = (lists.reshape(OWNERS, 8, 128) + lin[None]).astype(bf16)


def of_share():
    return jnp.bitwise_and(iota((SHARE, 128), 1), SHARE - 1) == iota((SHARE, 128), 0)


def gather_kernel(got_ref, narrow_ref, out_ref):
    asked = asked_rows(got_ref[...])
    hot = (asked == iota((SLOTS, ROWS), 1).astype(f32)).astype(f32).astype(bf16)
    out_ref[...] = dot(hot, narrow_ref[...]).astype(bf16).reshape(OWNERS, CAP, K)


def side_kernel(
    req_t_ref,
    factors_in,
    fs_t_ref,
    clicks_ref,
    acc_in,
    acc_lin_row_ref,
    linear_in,
    pick_ref,
    here_ref,
    ids_ref,
    narrow_ref,
    factors_ref,
    counts_t_ref,
    counts_ref,
    clicks_col_ref,
    acc_ref,
    acc_lin_ref,
    linear_ref,
):
    acc_ref[...] = acc_in[...]
    linear_ref[...] = linear_in[...]
    narrow_ref[...] = factors_in[...].astype(bf16)
    factors_ref[...] = factors_in[...]
    lists = own_lists(req_t_ref[...], CAP).astype(bf16)
    wanted = dot(lists, ones((128, 8 * OWNERS), 0)).astype(jnp.int32)
    first = jnp.right_shift(iota((SLOTS, 8 * OWNERS), 0), 4) * 8
    pick = iota((SLOTS, 8 * OWNERS), 1) == first + jnp.right_shift(wanted, 6)
    pick_ref[...] = pick.astype(f32).astype(bf16)
    here = iota((SLOTS, 128), 1) == jnp.bitwise_and(wanted[:, :128], 63) + 64
    here_ref[...] = here.astype(f32)
    spread = jnp.right_shift(iota((OWNERS, SLOTS), 1), 4) == iota((OWNERS, SLOTS), 0)
    lists = dot(split_requests(req_t_ref[...]), spread.astype(f32).astype(bf16))
    place = iota((128, SLOTS), 0)
    position = jnp.bitwise_and(iota((128, SLOTS), 1), CAP - 1)
    high = jnp.sum(jnp.where(place == position, lists, 0.0), axis=0, keepdims=True)
    low = jnp.sum(jnp.where(place == position + CAP, lists, 0.0), axis=0, keepdims=True)
    row = iota((8, SLOTS), 0)
    ids_ref[...] = jnp.where(row == 2, high, jnp.where(row == 3, low, 0.0))
    same_share = iota((SHARE, SHARE), 0) == iota((SHARE, SHARE), 1)
    acc_lin = jnp.sum(jnp.where(same_share, acc_lin_row_ref[...], 0.0), axis=1, keepdims=True)
    acc_lin_ref[...] = jnp.sum(jnp.where(of_share(), acc_lin, 0.0), axis=0, keepdims=True)
    chunk = 64

    def one(i, carry):
        base = pl.multiple_of(i * chunk, chunk)
        slots = iota((chunk, SAMPLES), 0) + base
        total = jnp.zeros((chunk, SAMPLES), f32)
        for f in range(FIELDS):
            total = total + jnp.where(fs_t_ref[pl.ds(f, 1), :] == slots, 1.0, 0.0)
        counts_t_ref[pl.ds(base, chunk), :] = total.astype(bf16)
        return carry

    lax.fori_loop(0, SLOTS // chunk, one, 0)
    counts_ref[...] = jnp.transpose(counts_t_ref[...].astype(f32)).astype(bf16)
    same = iota((SAMPLES, SAMPLES), 0) == iota((SAMPLES, SAMPLES), 1)
    clicks = clicks_ref[...].astype(f32)
    clicks_col_ref[...] = jnp.sum(jnp.where(same, clicks, 0.0), axis=1, keepdims=True)


def learn_kernel(
    rows_ref, counts_ref, counts_t_ref, clicks_ref, got_ref, pick_ref, here_ref, ids_ref, out_ref
):
    rows = rows_ref[...].reshape(SLOTS, K)
    wide_rows = rows.astype(f32)
    counts = counts_ref[...]
    sums = dot(counts, rows)
    got = got_ref[...].astype(f32).reshape(8 * OWNERS, 128).astype(bf16)
    linear = dot(counts, (dot(pick_ref[...], got) * here_ref[...]).astype(bf16))
    square = wide_rows * wide_rows
    square = square[:, :128] + square[:, 128:]
    high = square.astype(bf16)
    rest = square - high.astype(f32)
    middle = rest.astype(bf16)
    low = (rest - middle.astype(f32)).astype(bf16)
    terms = sums * sums - dot(counts, jnp.concatenate([high, middle], axis=1))
    terms = 0.5 * (terms[:, :128] + terms[:, 128:] - dot(counts, low)) + linear
    logits = jnp.sum(terms, axis=1, keepdims=True)
    errors = jnp.broadcast_to(jax.nn.sigmoid(logits) - clicks_ref[...], (SAMPLES, 128))
    first = errors.astype(bf16)
    second = (errors - first.astype(f32)).astype(bf16)
    weighted = (jnp.concatenate([errors, errors], axis=1) * sums).astype(bf16)
    counts_t = counts_t_ref[...]
    error_sums = dot(counts_t, jnp.concatenate([first, second], axis=1))
    error_sums = error_sums[:, :128] + error_sums[:, 128:]
    gathered = dot(counts_t, weighted)
    left = gathered[:, :128] - error_sums * wide_rows[:, :128]
    right = gathered[:, 128:] - error_sums * wide_rows[:, 128:]
    out_ref[:, :CAP, :] = left.astype(bf16).reshape(OWNERS, CAP, 128)
    out_ref[:, CAP : 2 * CAP, :] = right.astype(bf16).reshape(OWNERS, CAP, 128)
    place = lax.rem(lax.axis_index("server"), 8)
    pair = jnp.where(iota((SAMPLES, 128), 1) < 8, first.astype(f32), second.astype(f32)).astype(bf16)
    sums_row = dot(pair, counts, 0, 0)
    sums_row = sums_row[:8] + sums_row[8:16]
    high = sums_row.astype(bf16).astype(f32)
    row = iota((8, SLOTS), 0)
    sums_row = jnp.where(row == 0, high, jnp.where(row == 1, sums_row - high, ids_ref[...]))
    mine = jnp.right_shift(iota((8, 128), 1), 4) == place
    for owner in range(OWNERS):
        lanes = owner // 8 * 128
        turn = lax.rem(place + 8 - owner % 8, 8) * CAP
        tile = pltpu.roll(sums_row[:, lanes : lanes + 128], turn, 1)
        out_ref[owner, 2 * CAP :, :] = jnp.where(mine, tile, 0.0).astype(bf16)


def part_rows(x):
    rows = iota((8, x.shape[1]), 0)
    first = x.astype(bf16).astype(f32)
    rest = x - first
    second = rest.astype(bf16).astype(f32)
    third = rest - second
    return jnp.where(rows == 0, first, jnp.where(rows == 1, second, jnp.where(rows == 2, third, 0.0)))


def scatter_kernel(push_ref, out_ref):
    core = lax.axis_index("core")
    chunks = []
    for q in range(N_CORE * OWNERS // 8):
        chunk = push_ref[8 * q, 2 * CAP :, :].astype(f32)
        for i in range(1, 8):
            chunk = chunk + push_ref[8 * q + i, 2 * CAP :, :].astype(f32)
        chunks.append(chunk)
    tails = jnp.concatenate(chunks, axis=1)
    row = iota(tails.shape, 0)
    asked = jnp.sum(jnp.where((row == 2) | (row == 3), tails, 0.0), axis=0, keepdims=True)
    asked = asked.astype(jnp.int32)
    ours = jnp.bitwise_and(jnp.right_shift(asked, 5), 1) == core
    place = jnp.right_shift(asked, 6) * SHARE + jnp.bitwise_and(asked, SHARE - 1)
    place = jnp.where(ours, place, -1)
    hot = (iota((ROWS // N_CORE, N_CORE * SLOTS), 0) == place).astype(f32).astype(bf16)
    left = push_ref[:, :CAP, :].reshape(N_CORE * SLOTS, 128)
    right = push_ref[:, CAP : 2 * CAP, :].reshape(N_CORE * SLOTS, 128)
    total = dot(hot, jnp.concatenate([left, right], axis=1)).astype(bf16)
    out_ref[:, :SHARE, :] = total[:, :128].reshape(N_Y, SHARE, 128)
    out_ref[:, SHARE : 2 * SHARE, :] = total[:, 128:].reshape(N_Y, SHARE, 128)
    linear = dot(jnp.where(row < 2, tails, 0.0).astype(bf16), hot, 1, 1)
    linear = part_rows(jnp.sum(linear, axis=0, keepdims=True))
    for y in range(N_Y):
        lanes = y // 4 * 128
        turn = lax.rem(N_CORE * y + core + 4 - y % 4, 4) * SHARE
        out_ref[y, 2 * SHARE :, :] = pltpu.roll(linear[:, lanes : lanes + 128], turn, 1).astype(bf16)


def add_parts(part_ref):
    total = part_ref[0].astype(f32)
    for y in range(1, N_Y):
        total = total + part_ref[y].astype(f32)
    left, right = total[:SHARE], total[SHARE : 2 * SHARE]
    return left, right, jnp.sum(total[2 * SHARE :], axis=0, keepdims=True)


def my_lanes():
    me = lax.axis_index("y") * N_CORE + lax.axis_index("core")
    return jnp.right_shift(iota((1, 128), 1), 5) == lax.rem(me, 4)


def update_kernel(part_ref, acc_ref, acc_lin_ref, delta_ref):
    left, right, linear = add_parts(part_ref)
    acc = acc_ref[...]

    def step(grad, state):
        return step_size * grad / jnp.sqrt(state + grad * grad)

    left = step(left, acc[:, :128]).astype(bf16)
    right = step(right, acc[:, 128:]).astype(bf16)
    linear = part_rows(jnp.where(my_lanes(), step(linear, acc_lin_ref[...]), 0.0)).astype(bf16)
    for y in range(N_Y):
        delta_ref[y, :SHARE, :] = left
        delta_ref[y, SHARE : 2 * SHARE, :] = right
        delta_ref[y, 2 * SHARE :, :] = linear


def write_state(part_ref, acc_ref, acc_lin_ref, new_acc_ref, new_acc_lin_ref):
    left, right, linear = add_parts(part_ref)
    new_acc_ref[:, :128] = acc_ref[:, :128] + left * left
    new_acc_ref[:, 128:] = acc_ref[:, 128:] + right * right
    state = jnp.where(my_lanes(), acc_lin_ref[...] + linear * linear, 0.0)
    column = jnp.sum(jnp.where(of_share(), state, 0.0), axis=1, keepdims=True)
    same = iota((SHARE, SHARE), 0) == iota((SHARE, SHARE), 1)
    new_acc_lin_ref[...] = jnp.sum(jnp.where(same, column, 0.0), axis=0, keepdims=True)


def apply_kernel(
    delta_ref,
    factors_ref,
    linear_ref,
    part_ref,
    acc_ref,
    acc_lin_ref,
    new_factors_ref,
    new_linear_ref,
    new_acc_ref,
    new_acc_lin_ref,
):
    write_state(part_ref, acc_ref, acc_lin_ref, new_acc_ref, new_acc_lin_ref)
    for q in range(4):
        lin = jnp.zeros((8, 128), f32)
        for w in range(4 * q, 4 * q + 4):
            block = delta_ref[w % N_CORE * N_Y + w // N_CORE].astype(f32)
            here = pl.ds(w * SHARE, SHARE)
            new_factors_ref[here, :128] = factors_ref[here, :128] - block[:SHARE]
            new_factors_ref[here, 128:] = factors_ref[here, 128:] - block[SHARE : 2 * SHARE]
            lin = lin + block[2 * SHARE :]
        lanes = pl.ds(q * 128, 128)
        new_linear_ref[:, lanes] = linear_ref[:, lanes] - jnp.sum(lin, axis=0, keepdims=True)


def call(kernel, out, flops, *args, scratch=(), far=False):
    size = sum(a.size * a.dtype.itemsize for a in args)
    if far:
        args = [pltpu.with_memory_space_constraint(a, pltpu.HBM) for a in args]
    return pl.pallas_call(
        kernel,
        out_shape=out,
        in_specs=[pl.BlockSpec(memory_space=pltpu.HBM if far else pltpu.VMEM)] * len(args),
        out_specs=jax.tree.map(lambda _: pl.BlockSpec(memory_space=pltpu.VMEM), out),
        scratch_shapes=scratch,
        compiler_params=pltpu.CompilerParams(vmem_limit_bytes=24 * 1024 * 1024),
        cost_estimate=pl.CostEstimate(flops=flops, bytes_accessed=size, transcendentals=0),
    )(*args)


def shape(dims, dtype):
    return jax.ShapeDtypeStruct(dims, dtype)


def exchange(x, axis):
    return lax.all_to_all(x, axis, split_axis=0, concat_axis=0, tiled=True)


TALL = 2 * SHARE + 8


def body(factors, linear, acc_factors, acc_linear, feature_slot, requests, clicks):
    dma = pltpu.SemaphoreType.DMA
    req_t = requests.T
    ask = call(
        ask_kernel,
        shape((OWNERS, 8, 128), bf16),
        1 << 20,
        req_t,
        linear.reshape(4, 128),
        scratch=[pltpu.VMEM((CAP, OWNERS), jnp.int32), pltpu.VMEM((4, 128), f32), dma((2,))],
        far=True,
    )
    got = exchange(ask, "server")
    pick, here, ids, narrow, wide, counts_t, counts, clicks_col, acc, acc_lin, lin_row = call(
        side_kernel,
        [
            shape((SLOTS, 8 * OWNERS), bf16),
            shape((SLOTS, 128), f32),
            shape((8, SLOTS), f32),
            shape((ROWS, K), bf16),
            shape((ROWS, K), f32),
            shape((SLOTS, SAMPLES), bf16),
            shape((SAMPLES, SLOTS), bf16),
            shape((SAMPLES, 1), f32),
            shape((SHARE, K), f32),
            shape((1, 128), f32),
            shape((1, ROWS), f32),
        ],
        1 << 30,
        req_t,
        factors,
        feature_slot.T,
        clicks.reshape(1, SAMPLES),
        acc_factors,
        acc_linear.reshape(1, SHARE),
        linear.reshape(1, ROWS),
    )
    found = call(gather_kernel, shape((OWNERS, CAP, K), bf16), 1 << 28, got, narrow)
    rows = exchange(found, "server")
    push = call(
        learn_kernel,
        shape((OWNERS, 2 * CAP + 8, 128), bf16),
        1 << 28,
        rows,
        counts,
        counts_t,
        clicks_col,
        got,
        pick,
        here,
        ids,
    )
    pushed = exchange(push, "server")
    pushed = lax.all_gather(pushed, "core", axis=0, tiled=True)
    dense = call(scatter_kernel, shape((N_Y, TALL, 128), bf16), 1 << 28, pushed)
    shared = exchange(dense, "y")
    delta = call(update_kernel, shape((N_Y, TALL, 128), bf16), 1 << 20, shared, acc, acc_lin)
    deltas = exchange(delta, "y")
    deltas = lax.all_gather(deltas, "core", axis=0, tiled=True)
    new_factors, new_linear, new_acc, new_acc_lin = call(
        apply_kernel,
        [shape((ROWS, K), f32), shape((1, ROWS), f32), shape((SHARE, K), f32), shape((1, SHARE), f32)],
        1 << 20,
        deltas,
        wide,
        lin_row,
        shared,
        acc,
        acc_lin,
    )
    return new_factors, new_linear.reshape(ROWS), new_acc, new_acc_lin.reshape(SHARE)


def solution(mesh):
    mesh = Mesh(mesh.devices.reshape(OWNERS, N_Y, N_CORE), ("server", "y", "core"))
    every = ("server", "y", "core")
    in_specs = (
        P("server", None),
        P("server"),
        P(every, None),
        P(every),
        P(every, None),
        P(every, None),
        P(every),
    )
    out_specs = (P("server", None), P("server"), P(every, None), P(every))
    return jax.shard_map(body, mesh=mesh, in_specs=in_specs, out_specs=out_specs, check_vma=False)
```

```python
import jax
import jax.numpy as jnp
from jax import lax
from jax.experimental import pallas as pl
from jax.experimental.pallas import tpu as pltpu
from jax.sharding import Mesh, PartitionSpec as P

step_size = 0.5
bf16 = jnp.bfloat16
f32 = jnp.float32

OWNERS = 32
CAP = 16
SLOTS = OWNERS * CAP
ROWS = 512
K = 256
SAMPLES = 256
FIELDS = 39
N_Y = 8
N_CORE = 2
N_WORKER = N_Y * N_CORE
SHARE = ROWS // N_WORKER


def iota(shape, axis):
    return lax.broadcasted_iota(jnp.int32, shape, axis)


def dot(a, b, ca=1, cb=0):
    return lax.dot_general(a, b, (((ca,), (cb,)), ((), ())), preferred_element_type=f32)


def split_requests(req_t):
    high = jnp.bitwise_and(req_t, -16)
    low = jnp.bitwise_and(req_t, 15)
    pad = jnp.zeros((96, OWNERS), jnp.int32)
    return jnp.concatenate([high, low, pad], axis=0).astype(f32).astype(bf16)


def own_lists(req_t, rows):
    owner = jnp.right_shift(iota((OWNERS * rows, OWNERS), 0), 4 if rows == CAP else 3)
    mine = (owner == iota((OWNERS * rows, OWNERS), 1)).astype(f32).astype(bf16)
    lists = dot(mine, split_requests(req_t), 1, 1)
    lane = iota((OWNERS * rows, 128), 1)
    position = jnp.bitwise_and(iota((OWNERS * rows, 128), 0), rows - 1)
    keep = (lane < 2 * CAP) & (jnp.bitwise_and(lane, rows - 1) == position)
    return jnp.where(keep, lists, 0.0)


def asked_rows(got):
    got = got.astype(f32)
    lane = iota(got.shape, 2)
    upper = jnp.bitwise_and(lane, 8) == 8
    got = jnp.where(lane < 2 * CAP, got, 0.0)
    split = jnp.concatenate([jnp.where(upper, 0.0, got), jnp.where(upper, got, 0.0)], axis=1)
    return jnp.sum(split.reshape(SLOTS, 128), axis=1, keepdims=True)


def ones(dims, axis):
    return (iota(dims, axis) < 2 * CAP).astype(f32).astype(bf16)


def ask_kernel(req_t_hbm, lin_hbm, factors_hbm, out_ref, factors_ref, req_t_ref, lin_ref, sems):
    copies = [
        pltpu.make_async_copy(req_t_hbm, req_t_ref, sems.at[0]),
        pltpu.make_async_copy(lin_hbm, lin_ref, sems.at[1]),
        pltpu.make_async_copy(factors_hbm, factors_ref, sems.at[2]),
    ]
    for copy in copies[::-1]:
        copy.start()
    for copy in copies[:2]:
        copy.wait()
    lists = own_lists(req_t_ref[...], 8)
    spread = (jnp.right_shift(iota((8, 4), 0), 1) == iota((8, 4), 1)).astype(f32).astype(bf16)
    lin = dot(spread, lin_ref[...].astype(bf16))
    odd = jnp.bitwise_and(iota((8, 128), 0), 1) == 1
    lin = jnp.where(odd, lin, pltpu.roll(lin, 64, 1))
    lin = jnp.where(iota((8, 128), 1) >= 64, lin, 0.0)
    out_ref[...] = (lists.reshape(OWNERS, 8, 128) + lin[None]).astype(bf16)
    copies[2].wait()


def of_share():
    return jnp.bitwise_and(iota((SHARE, 128), 1), SHARE - 1) == iota((SHARE, 128), 0)


def gather_kernel(got_ref, factors_ref, out_ref):
    asked = asked_rows(got_ref[...])
    hot = (asked == iota((SLOTS, ROWS), 1).astype(f32)).astype(f32).astype(bf16)
    out_ref[...] = dot(hot, factors_ref[...].astype(bf16)).astype(bf16).reshape(OWNERS, CAP, K)


def side_kernel(
    got_ref,
    req_t_ref,
    fs_t_ref,
    clicks_ref,
    acc_in,
    acc_lin_row_ref,
    linear_in,
    lin_ref,
    ids_ref,
    counts_t_ref,
    counts_ref,
    clicks_col_ref,
    acc_ref,
    acc_lin_ref,
    linear_ref,
):
    acc_ref[...] = acc_in[...]
    linear_ref[...] = linear_in[...]
    got = got_ref[...].astype(f32).reshape(8 * OWNERS, 128).astype(bf16)
    lists = own_lists(req_t_ref[...], CAP).astype(bf16)
    wanted = dot(lists, ones((128, 8 * OWNERS), 0)).astype(jnp.int32)
    first = jnp.right_shift(iota((SLOTS, 8 * OWNERS), 0), 4) * 8
    pick = iota((SLOTS, 8 * OWNERS), 1) == first + jnp.right_shift(wanted, 6)
    values = dot(pick.astype(f32).astype(bf16), got)
    here = iota((SLOTS, 128), 1) == jnp.bitwise_and(wanted[:, :128], 63) + 64
    lin_terms = jnp.where(here, values, 0.0).astype(bf16)
    spread = jnp.right_shift(iota((OWNERS, SLOTS), 1), 4) == iota((OWNERS, SLOTS), 0)
    lists = dot(split_requests(req_t_ref[...]), spread.astype(f32).astype(bf16))
    place = iota((128, SLOTS), 0)
    position = jnp.bitwise_and(iota((128, SLOTS), 1), CAP - 1)
    high = jnp.sum(jnp.where(place == position, lists, 0.0), axis=0, keepdims=True)
    low = jnp.sum(jnp.where(place == position + CAP, lists, 0.0), axis=0, keepdims=True)
    row = iota((8, SLOTS), 0)
    ids_ref[...] = jnp.where(row == 2, high, jnp.where(row == 3, low, 0.0))
    same_share = iota((SHARE, SHARE), 0) == iota((SHARE, SHARE), 1)
    acc_lin = jnp.sum(jnp.where(same_share, acc_lin_row_ref[...], 0.0), axis=1, keepdims=True)
    acc_lin_ref[...] = jnp.sum(jnp.where(of_share(), acc_lin, 0.0), axis=0, keepdims=True)
    chunk = 64

    def one(i, carry):
        base = pl.multiple_of(i * chunk, chunk)
        slots = iota((chunk, SAMPLES), 0) + base
        total = jnp.zeros((chunk, SAMPLES), f32)
        for f in range(FIELDS):
            total = total + jnp.where(fs_t_ref[pl.ds(f, 1), :] == slots, 1.0, 0.0)
        counts_t_ref[pl.ds(base, chunk), :] = total.astype(bf16)
        return carry

    lax.fori_loop(0, SLOTS // chunk, one, 0)
    counts = jnp.transpose(counts_t_ref[...].astype(f32)).astype(bf16)
    counts_ref[...] = counts
    lin_ref[...] = dot(counts, lin_terms)
    same = iota((SAMPLES, SAMPLES), 0) == iota((SAMPLES, SAMPLES), 1)
    clicks = clicks_ref[...].astype(f32)
    clicks_col_ref[...] = jnp.sum(jnp.where(same, clicks, 0.0), axis=1, keepdims=True)


def learn_kernel(rows_ref, counts_ref, counts_t_ref, clicks_ref, lin_ref, ids_ref, out_ref):
    rows = rows_ref[...].reshape(SLOTS, K)
    wide_rows = rows.astype(f32)
    counts = counts_ref[...]
    sums = dot(counts, rows)
    square = wide_rows * wide_rows
    square = square[:, :128] + square[:, 128:]
    high = square.astype(bf16)
    rest = square - high.astype(f32)
    middle = rest.astype(bf16)
    low = (rest - middle.astype(f32)).astype(bf16)
    terms = sums * sums - dot(counts, jnp.concatenate([high, middle], axis=1))
    terms = 0.5 * (terms[:, :128] + terms[:, 128:] - dot(counts, low)) + lin_ref[...]
    logits = jnp.sum(terms, axis=1, keepdims=True)
    errors = jnp.broadcast_to(jax.nn.sigmoid(logits) - clicks_ref[...], (SAMPLES, 128))
    first = errors.astype(bf16)
    second = (errors - first.astype(f32)).astype(bf16)
    weighted = (jnp.concatenate([errors, errors], axis=1) * sums).astype(bf16)
    counts_t = counts_t_ref[...]
    error_sums = dot(counts_t, jnp.concatenate([first, second], axis=1))
    error_sums = error_sums[:, :128] + error_sums[:, 128:]
    gathered = dot(counts_t, weighted)
    left = gathered[:, :128] - error_sums * wide_rows[:, :128]
    right = gathered[:, 128:] - error_sums * wide_rows[:, 128:]
    out_ref[:, :CAP, :] = left.astype(bf16).reshape(OWNERS, CAP, 128)
    out_ref[:, CAP : 2 * CAP, :] = right.astype(bf16).reshape(OWNERS, CAP, 128)
    place = lax.rem(lax.axis_index("server"), 8)
    pair = jnp.where(iota((SAMPLES, 128), 1) < 8, first.astype(f32), second.astype(f32)).astype(bf16)
    sums_row = dot(pair, counts, 0, 0)
    sums_row = sums_row[:8] + sums_row[8:16]
    high = sums_row.astype(bf16).astype(f32)
    row = iota((8, SLOTS), 0)
    sums_row = jnp.where(row == 0, high, jnp.where(row == 1, sums_row - high, ids_ref[...]))
    mine = jnp.right_shift(iota((8, 128), 1), 4) == place
    for owner in range(OWNERS):
        lanes = owner // 8 * 128
        turn = lax.rem(place + 8 - owner % 8, 8) * CAP
        tile = pltpu.roll(sums_row[:, lanes : lanes + 128], turn, 1)
        out_ref[owner, 2 * CAP :, :] = jnp.where(mine, tile, 0.0).astype(bf16)


def part_rows(x):
    rows = iota((8, x.shape[1]), 0)
    first = x.astype(bf16).astype(f32)
    rest = x - first
    second = rest.astype(bf16).astype(f32)
    third = rest - second
    return jnp.where(rows == 0, first, jnp.where(rows == 1, second, jnp.where(rows == 2, third, 0.0)))


def scatter_kernel(push_ref, out_ref):
    core = lax.axis_index("core")
    chunks = []
    for q in range(N_CORE * OWNERS // 8):
        chunk = push_ref[8 * q, 2 * CAP :, :].astype(f32)
        for i in range(1, 8):
            chunk = chunk + push_ref[8 * q + i, 2 * CAP :, :].astype(f32)
        chunks.append(chunk)
    tails = jnp.concatenate(chunks, axis=1)
    row = iota(tails.shape, 0)
    asked = jnp.sum(jnp.where((row == 2) | (row == 3), tails, 0.0), axis=0, keepdims=True)
    asked = asked.astype(jnp.int32)
    ours = jnp.bitwise_and(jnp.right_shift(asked, 5), 1) == core
    place = jnp.right_shift(asked, 6) * SHARE + jnp.bitwise_and(asked, SHARE - 1)
    place = jnp.where(ours, place, -1)
    hot = (iota((ROWS // N_CORE, N_CORE * SLOTS), 0) == place).astype(f32).astype(bf16)
    left = push_ref[:, :CAP, :].reshape(N_CORE * SLOTS, 128)
    right = push_ref[:, CAP : 2 * CAP, :].reshape(N_CORE * SLOTS, 128)
    total = dot(hot, jnp.concatenate([left, right], axis=1)).astype(bf16)
    out_ref[:, :SHARE, :] = total[:, :128].reshape(N_Y, SHARE, 128)
    out_ref[:, SHARE : 2 * SHARE, :] = total[:, 128:].reshape(N_Y, SHARE, 128)
    linear = dot(jnp.where(row < 2, tails, 0.0).astype(bf16), hot, 1, 1)
    linear = part_rows(jnp.sum(linear, axis=0, keepdims=True))
    for y in range(N_Y):
        lanes = y // 4 * 128
        turn = lax.rem(N_CORE * y + core + 4 - y % 4, 4) * SHARE
        out_ref[y, 2 * SHARE :, :] = pltpu.roll(linear[:, lanes : lanes + 128], turn, 1).astype(bf16)


def add_parts(part_ref):
    total = part_ref[0].astype(f32)
    for y in range(1, N_Y):
        total = total + part_ref[y].astype(f32)
    left, right = total[:SHARE], total[SHARE : 2 * SHARE]
    return left, right, jnp.sum(total[2 * SHARE :], axis=0, keepdims=True)


def my_lanes():
    me = lax.axis_index("y") * N_CORE + lax.axis_index("core")
    return jnp.right_shift(iota((1, 128), 1), 5) == lax.rem(me, 4)


def update_kernel(part_ref, acc_ref, acc_lin_ref, delta_ref):
    left, right, linear = add_parts(part_ref)
    acc = acc_ref[...]

    def step(grad, state):
        return step_size * grad / jnp.sqrt(state + grad * grad)

    left = step(left, acc[:, :128]).astype(bf16)
    right = step(right, acc[:, 128:]).astype(bf16)
    linear = part_rows(jnp.where(my_lanes(), step(linear, acc_lin_ref[...]), 0.0)).astype(bf16)
    for y in range(N_Y):
        delta_ref[y, :SHARE, :] = left
        delta_ref[y, SHARE : 2 * SHARE, :] = right
        delta_ref[y, 2 * SHARE :, :] = linear


def write_state(part_ref, acc_ref, acc_lin_ref, new_acc_ref, new_acc_lin_ref):
    left, right, linear = add_parts(part_ref)
    new_acc_ref[:, :128] = acc_ref[:, :128] + left * left
    new_acc_ref[:, 128:] = acc_ref[:, 128:] + right * right
    state = jnp.where(my_lanes(), acc_lin_ref[...] + linear * linear, 0.0)
    column = jnp.sum(jnp.where(of_share(), state, 0.0), axis=1, keepdims=True)
    same = iota((SHARE, SHARE), 0) == iota((SHARE, SHARE), 1)
    new_acc_lin_ref[...] = jnp.sum(jnp.where(same, column, 0.0), axis=0, keepdims=True)


def apply_kernel(
    delta_ref,
    factors_ref,
    linear_ref,
    part_ref,
    acc_ref,
    acc_lin_ref,
    new_factors_ref,
    new_linear_ref,
    new_acc_ref,
    new_acc_lin_ref,
):
    write_state(part_ref, acc_ref, acc_lin_ref, new_acc_ref, new_acc_lin_ref)
    for q in range(4):
        lin = jnp.zeros((8, 128), f32)
        for w in range(4 * q, 4 * q + 4):
            block = delta_ref[w % N_CORE * N_Y + w // N_CORE].astype(f32)
            here = pl.ds(w * SHARE, SHARE)
            new_factors_ref[here, :128] = factors_ref[here, :128] - block[:SHARE]
            new_factors_ref[here, 128:] = factors_ref[here, 128:] - block[SHARE : 2 * SHARE]
            lin = lin + block[2 * SHARE :]
        lanes = pl.ds(q * 128, 128)
        new_linear_ref[:, lanes] = linear_ref[:, lanes] - jnp.sum(lin, axis=0, keepdims=True)


def call(kernel, out, flops, *args, scratch=(), far=False):
    size = sum(a.size * a.dtype.itemsize for a in args)
    if far:
        args = [pltpu.with_memory_space_constraint(a, pltpu.HBM) for a in args]
    return pl.pallas_call(
        kernel,
        out_shape=out,
        in_specs=[pl.BlockSpec(memory_space=pltpu.HBM if far else pltpu.VMEM)] * len(args),
        out_specs=jax.tree.map(lambda _: pl.BlockSpec(memory_space=pltpu.VMEM), out),
        scratch_shapes=scratch,
        compiler_params=pltpu.CompilerParams(vmem_limit_bytes=24 * 1024 * 1024),
        cost_estimate=pl.CostEstimate(flops=flops, bytes_accessed=size, transcendentals=0),
    )(*args)


def shape(dims, dtype):
    return jax.ShapeDtypeStruct(dims, dtype)


def exchange(x, axis):
    return lax.all_to_all(x, axis, split_axis=0, concat_axis=0, tiled=True)


TALL = 2 * SHARE + 8


def body(factors, linear, acc_factors, acc_linear, feature_slot, requests, clicks):
    dma = pltpu.SemaphoreType.DMA
    req_t = requests.T
    ask, wide = call(
        ask_kernel,
        [shape((OWNERS, 8, 128), bf16), shape((ROWS, K), f32)],
        1 << 20,
        req_t,
        linear.reshape(4, 128),
        factors,
        scratch=[pltpu.VMEM((CAP, OWNERS), jnp.int32), pltpu.VMEM((4, 128), f32), dma((3,))],
        far=True,
    )
    got = exchange(ask, "server")
    found = call(gather_kernel, shape((OWNERS, CAP, K), bf16), 1 << 28, got, wide)
    rows = exchange(found, "server")
    lin_terms, ids, counts_t, counts, clicks_col, acc, acc_lin, lin_row = call(
        side_kernel,
        [
            shape((SAMPLES, 128), f32),
            shape((8, SLOTS), f32),
            shape((SLOTS, SAMPLES), bf16),
            shape((SAMPLES, SLOTS), bf16),
            shape((SAMPLES, 1), f32),
            shape((SHARE, K), f32),
            shape((1, 128), f32),
            shape((1, ROWS), f32),
        ],
        1 << 30,
        got,
        req_t,
        feature_slot.T,
        clicks.reshape(1, SAMPLES),
        acc_factors,
        acc_linear.reshape(1, SHARE),
        linear.reshape(1, ROWS),
    )
    push = call(
        learn_kernel,
        shape((OWNERS, 2 * CAP + 8, 128), bf16),
        1 << 28,
        rows,
        counts,
        counts_t,
        clicks_col,
        lin_terms,
        ids,
    )
    pushed = exchange(push, "server")
    pushed = lax.all_gather(pushed, "core", axis=0, tiled=True)
    dense = call(scatter_kernel, shape((N_Y, TALL, 128), bf16), 1 << 28, pushed)
    shared = exchange(dense, "y")
    delta = call(update_kernel, shape((N_Y, TALL, 128), bf16), 1 << 20, shared, acc, acc_lin)
    deltas = exchange(delta, "y")
    deltas = lax.all_gather(deltas, "core", axis=0, tiled=True)
    new_factors, new_linear, new_acc, new_acc_lin = call(
        apply_kernel,
        [shape((ROWS, K), f32), shape((1, ROWS), f32), shape((SHARE, K), f32), shape((1, SHARE), f32)],
        1 << 20,
        deltas,
        wide,
        lin_row,
        shared,
        acc,
        acc_lin,
    )
    return new_factors, new_linear.reshape(ROWS), new_acc, new_acc_lin.reshape(SHARE)


def solution(mesh):
    mesh = Mesh(mesh.devices.reshape(OWNERS, N_Y, N_CORE), ("server", "y", "core"))
    every = ("server", "y", "core")
    in_specs = (
        P("server", None),
        P("server"),
        P(every, None),
        P(every),
        P(every, None),
        P(every, None),
        P(every),
    )
    out_specs = (P("server", None), P("server"), P(every, None), P(every))
    return jax.shard_map(body, mesh=mesh, in_specs=in_specs, out_specs=out_specs, check_vma=False)
```

```python
import jax
import jax.numpy as jnp
from jax import lax
from jax.experimental import pallas as pl
from jax.experimental.pallas import tpu as pltpu
from jax.sharding import Mesh, PartitionSpec as P

step_size = 0.5
bf16 = jnp.bfloat16
f32 = jnp.float32

OWNERS = 32
CAP = 16
SLOTS = OWNERS * CAP
ROWS = 512
K = 256
SAMPLES = 256
FIELDS = 39
N_Y = 8
N_CORE = 2
N_WORKER = N_Y * N_CORE
SHARE = ROWS // N_WORKER


def iota(shape, axis):
    return lax.broadcasted_iota(jnp.int32, shape, axis)


def dot(a, b, ca=1, cb=0):
    return lax.dot_general(a, b, (((ca,), (cb,)), ((), ())), preferred_element_type=f32)


def split_requests(req_t):
    high = jnp.bitwise_and(req_t, -16)
    low = jnp.bitwise_and(req_t, 15)
    pad = jnp.zeros((96, OWNERS), jnp.int32)
    return jnp.concatenate([high, low, pad], axis=0).astype(f32).astype(bf16)


def own_lists(req_t, rows):
    owner = jnp.right_shift(iota((OWNERS * rows, OWNERS), 0), 4 if rows == CAP else 3)
    mine = (owner == iota((OWNERS * rows, OWNERS), 1)).astype(f32).astype(bf16)
    lists = dot(mine, split_requests(req_t), 1, 1)
    lane = iota((OWNERS * rows, 128), 1)
    position = jnp.bitwise_and(iota((OWNERS * rows, 128), 0), rows - 1)
    keep = (lane < 2 * CAP) & (jnp.bitwise_and(lane, rows - 1) == position)
    return jnp.where(keep, lists, 0.0)


def asked_rows(got):
    got = got.astype(f32)
    lane = iota(got.shape, 2)
    upper = jnp.bitwise_and(lane, 8) == 8
    got = jnp.where(lane < 2 * CAP, got, 0.0)
    split = jnp.concatenate([jnp.where(upper, 0.0, got), jnp.where(upper, got, 0.0)], axis=1)
    return jnp.sum(split.reshape(SLOTS, 128), axis=1, keepdims=True)


def ones(dims, axis):
    return (iota(dims, axis) < 2 * CAP).astype(f32).astype(bf16)


def ask_kernel(req_t_hbm, lin_hbm, factors_hbm, out_ref, factors_ref, req_t_ref, lin_ref, sems):
    copies = [
        pltpu.make_async_copy(req_t_hbm, req_t_ref, sems.at[0]),
        pltpu.make_async_copy(lin_hbm, lin_ref, sems.at[1]),
        pltpu.make_async_copy(factors_hbm, factors_ref, sems.at[2]),
    ]
    for copy in copies:
        copy.start()
    for copy in copies[:2]:
        copy.wait()
    lists = own_lists(req_t_ref[...], 8)
    spread = (jnp.right_shift(iota((8, 4), 0), 1) == iota((8, 4), 1)).astype(f32).astype(bf16)
    lin = dot(spread, lin_ref[...].astype(bf16))
    odd = jnp.bitwise_and(iota((8, 128), 0), 1) == 1
    lin = jnp.where(odd, lin, pltpu.roll(lin, 64, 1))
    lin = jnp.where(iota((8, 128), 1) >= 64, lin, 0.0)
    out_ref[...] = (lists.reshape(OWNERS, 8, 128) + lin[None]).astype(bf16)
    copies[2].wait()


def of_share():
    return jnp.bitwise_and(iota((SHARE, 128), 1), SHARE - 1) == iota((SHARE, 128), 0)


def gather_kernel(got_ref, factors_ref, out_ref):
    asked = asked_rows(got_ref[...])
    hot = (asked == iota((SLOTS, ROWS), 1).astype(f32)).astype(f32).astype(bf16)
    out_ref[...] = dot(hot, factors_ref[...].astype(bf16)).astype(bf16).reshape(OWNERS, CAP, K)


def side_kernel(
    got_ref,
    req_t_ref,
    fs_t_ref,
    clicks_ref,
    acc_in,
    acc_lin_row_ref,
    linear_in,
    lin_ref,
    ids_ref,
    counts_t_ref,
    counts_ref,
    clicks_col_ref,
    acc_ref,
    acc_lin_ref,
    linear_ref,
):
    acc_ref[...] = acc_in[...]
    linear_ref[...] = linear_in[...]
    got = got_ref[...].astype(f32).reshape(8 * OWNERS, 128).astype(bf16)
    lists = own_lists(req_t_ref[...], CAP).astype(bf16)
    wanted = dot(lists, ones((128, 8 * OWNERS), 0)).astype(jnp.int32)
    first = jnp.right_shift(iota((SLOTS, 8 * OWNERS), 0), 4) * 8
    pick = iota((SLOTS, 8 * OWNERS), 1) == first + jnp.right_shift(wanted, 6)
    values = dot(pick.astype(f32).astype(bf16), got)
    here = iota((SLOTS, 128), 1) == jnp.bitwise_and(wanted[:, :128], 63) + 64
    lin_terms = jnp.where(here, values, 0.0).astype(bf16)
    spread = jnp.right_shift(iota((OWNERS, SLOTS), 1), 4) == iota((OWNERS, SLOTS), 0)
    lists = dot(split_requests(req_t_ref[...]), spread.astype(f32).astype(bf16))
    place = iota((128, SLOTS), 0)
    position = jnp.bitwise_and(iota((128, SLOTS), 1), CAP - 1)
    high = jnp.sum(jnp.where(place == position, lists, 0.0), axis=0, keepdims=True)
    low = jnp.sum(jnp.where(place == position + CAP, lists, 0.0), axis=0, keepdims=True)
    row = iota((8, SLOTS), 0)
    ids_ref[...] = jnp.where(row == 2, high, jnp.where(row == 3, low, 0.0))
    same_share = iota((SHARE, SHARE), 0) == iota((SHARE, SHARE), 1)
    acc_lin = jnp.sum(jnp.where(same_share, acc_lin_row_ref[...], 0.0), axis=1, keepdims=True)
    acc_lin_ref[...] = jnp.sum(jnp.where(of_share(), acc_lin, 0.0), axis=0, keepdims=True)
    chunk = 64

    def one(i, carry):
        base = pl.multiple_of(i * chunk, chunk)
        slots = iota((chunk, SAMPLES), 0) + base
        total = jnp.zeros((chunk, SAMPLES), f32)
        for f in range(FIELDS):
            total = total + jnp.where(fs_t_ref[pl.ds(f, 1), :] == slots, 1.0, 0.0)
        counts_t_ref[pl.ds(base, chunk), :] = total.astype(bf16)
        return carry

    lax.fori_loop(0, SLOTS // chunk, one, 0)
    counts = jnp.transpose(counts_t_ref[...].astype(f32)).astype(bf16)
    counts_ref[...] = counts
    lin_ref[...] = dot(counts, lin_terms)
    same = iota((SAMPLES, SAMPLES), 0) == iota((SAMPLES, SAMPLES), 1)
    clicks = clicks_ref[...].astype(f32)
    clicks_col_ref[...] = jnp.sum(jnp.where(same, clicks, 0.0), axis=1, keepdims=True)


def learn_kernel(rows_ref, counts_ref, counts_t_ref, clicks_ref, lin_ref, ids_ref, out_ref):
    rows = rows_ref[...].reshape(SLOTS, K)
    wide_rows = rows.astype(f32)
    counts = counts_ref[...]
    sums = dot(counts, rows)
    square = wide_rows * wide_rows
    square = square[:, :128] + square[:, 128:]
    high = square.astype(bf16)
    rest = square - high.astype(f32)
    middle = rest.astype(bf16)
    low = (rest - middle.astype(f32)).astype(bf16)
    terms = sums * sums - dot(counts, jnp.concatenate([high, middle], axis=1))
    terms = 0.5 * (terms[:, :128] + terms[:, 128:] - dot(counts, low)) + lin_ref[...]
    logits = jnp.sum(terms, axis=1, keepdims=True)
    errors = jnp.broadcast_to(jax.nn.sigmoid(logits) - clicks_ref[...], (SAMPLES, 128))
    first = errors.astype(bf16)
    second = (errors - first.astype(f32)).astype(bf16)
    weighted = (jnp.concatenate([errors, errors], axis=1) * sums).astype(bf16)
    counts_t = counts_t_ref[...]
    error_sums = dot(counts_t, jnp.concatenate([first, second], axis=1))
    error_sums = error_sums[:, :128] + error_sums[:, 128:]
    gathered = dot(counts_t, weighted)
    left = gathered[:, :128] - error_sums * wide_rows[:, :128]
    right = gathered[:, 128:] - error_sums * wide_rows[:, 128:]
    out_ref[:, :CAP, :] = left.astype(bf16).reshape(OWNERS, CAP, 128)
    out_ref[:, CAP : 2 * CAP, :] = right.astype(bf16).reshape(OWNERS, CAP, 128)
    place = lax.rem(lax.axis_index("server"), 8)
    pair = jnp.where(iota((SAMPLES, 128), 1) < 8, first.astype(f32), second.astype(f32)).astype(bf16)
    sums_row = dot(pair, counts, 0, 0)
    sums_row = sums_row[:8] + sums_row[8:16]
    high = sums_row.astype(bf16).astype(f32)
    row = iota((8, SLOTS), 0)
    sums_row = jnp.where(row == 0, high, jnp.where(row == 1, sums_row - high, ids_ref[...]))
    mine = jnp.right_shift(iota((8, 128), 1), 4) == place
    for owner in range(OWNERS):
        lanes = owner // 8 * 128
        turn = lax.rem(place + 8 - owner % 8, 8) * CAP
        tile = pltpu.roll(sums_row[:, lanes : lanes + 128], turn, 1)
        out_ref[owner, 2 * CAP :, :] = jnp.where(mine, tile, 0.0).astype(bf16)


def part_rows(x):
    rows = iota((8, x.shape[1]), 0)
    first = x.astype(bf16).astype(f32)
    rest = x - first
    second = rest.astype(bf16).astype(f32)
    third = rest - second
    return jnp.where(rows == 0, first, jnp.where(rows == 1, second, jnp.where(rows == 2, third, 0.0)))


def scatter_kernel(push_ref, out_ref):
    core = lax.axis_index("core")
    chunks = []
    for q in range(N_CORE * OWNERS // 8):
        chunk = push_ref[8 * q, 2 * CAP :, :]
        for i in range(1, 8):
            chunk = chunk + push_ref[8 * q + i, 2 * CAP :, :]
        chunks.append(chunk.astype(f32))
    tails = jnp.concatenate(chunks, axis=1)
    row = iota(tails.shape, 0)
    asked = jnp.sum(jnp.where((row == 2) | (row == 3), tails, 0.0), axis=0, keepdims=True)
    asked = asked.astype(jnp.int32)
    ours = jnp.bitwise_and(jnp.right_shift(asked, 5), 1) == core
    place = jnp.right_shift(asked, 6) * SHARE + jnp.bitwise_and(asked, SHARE - 1)
    place = jnp.where(ours, place, -1)
    hot = (iota((ROWS // N_CORE, N_CORE * SLOTS), 0) == place).astype(f32).astype(bf16)
    left = push_ref[:, :CAP, :].reshape(N_CORE * SLOTS, 128)
    right = push_ref[:, CAP : 2 * CAP, :].reshape(N_CORE * SLOTS, 128)
    total = dot(hot, jnp.concatenate([left, right], axis=1)).astype(bf16)
    out_ref[:, :SHARE, :] = total[:, :128].reshape(N_Y, SHARE, 128)
    out_ref[:, SHARE : 2 * SHARE, :] = total[:, 128:].reshape(N_Y, SHARE, 128)
    linear = dot(jnp.where(row < 2, tails, 0.0).astype(bf16), hot, 1, 1)
    linear = part_rows(jnp.sum(linear, axis=0, keepdims=True))
    for y in range(N_Y):
        lanes = y // 4 * 128
        turn = lax.rem(N_CORE * y + core + 4 - y % 4, 4) * SHARE
        out_ref[y, 2 * SHARE :, :] = pltpu.roll(linear[:, lanes : lanes + 128], turn, 1).astype(bf16)


def add_parts(part_ref):
    total = part_ref[0].astype(f32)
    for y in range(1, N_Y):
        total = total + part_ref[y].astype(f32)
    left, right = total[:SHARE], total[SHARE : 2 * SHARE]
    return left, right, jnp.sum(total[2 * SHARE :], axis=0, keepdims=True)


def my_lanes():
    me = lax.axis_index("y") * N_CORE + lax.axis_index("core")
    return jnp.right_shift(iota((1, 128), 1), 5) == lax.rem(me, 4)


def update_kernel(part_ref, acc_ref, acc_lin_ref, delta_ref):
    left, right, linear = add_parts(part_ref)
    acc = acc_ref[...]

    def step(grad, state):
        return step_size * grad / jnp.sqrt(state + grad * grad)

    left = step(left, acc[:, :128]).astype(bf16)
    right = step(right, acc[:, 128:]).astype(bf16)
    linear = part_rows(jnp.where(my_lanes(), step(linear, acc_lin_ref[...]), 0.0)).astype(bf16)
    for y in range(N_Y):
        delta_ref[y, :SHARE, :] = left
        delta_ref[y, SHARE : 2 * SHARE, :] = right
        delta_ref[y, 2 * SHARE :, :] = linear


def write_state(part_ref, acc_ref, acc_lin_ref, new_acc_ref, new_acc_lin_ref):
    left, right, linear = add_parts(part_ref)
    new_acc_ref[:, :128] = acc_ref[:, :128] + left * left
    new_acc_ref[:, 128:] = acc_ref[:, 128:] + right * right
    state = jnp.where(my_lanes(), acc_lin_ref[...] + linear * linear, 0.0)
    column = jnp.sum(jnp.where(of_share(), state, 0.0), axis=1, keepdims=True)
    same = iota((SHARE, SHARE), 0) == iota((SHARE, SHARE), 1)
    new_acc_lin_ref[...] = jnp.sum(jnp.where(same, column, 0.0), axis=0, keepdims=True)


def apply_kernel(
    delta_ref,
    factors_ref,
    linear_ref,
    part_ref,
    acc_ref,
    acc_lin_ref,
    new_factors_ref,
    new_linear_ref,
    new_acc_ref,
    new_acc_lin_ref,
):
    write_state(part_ref, acc_ref, acc_lin_ref, new_acc_ref, new_acc_lin_ref)
    for q in range(4):
        lin = jnp.zeros((8, 128), f32)
        for w in range(4 * q, 4 * q + 4):
            block = delta_ref[w % N_CORE * N_Y + w // N_CORE].astype(f32)
            here = pl.ds(w * SHARE, SHARE)
            new_factors_ref[here, :128] = factors_ref[here, :128] - block[:SHARE]
            new_factors_ref[here, 128:] = factors_ref[here, 128:] - block[SHARE : 2 * SHARE]
            lin = lin + block[2 * SHARE :]
        lanes = pl.ds(q * 128, 128)
        new_linear_ref[:, lanes] = linear_ref[:, lanes] - jnp.sum(lin, axis=0, keepdims=True)


def call(kernel, out, flops, *args, scratch=(), far=False):
    size = sum(a.size * a.dtype.itemsize for a in args)
    if far:
        args = [pltpu.with_memory_space_constraint(a, pltpu.HBM) for a in args]
    return pl.pallas_call(
        kernel,
        out_shape=out,
        in_specs=[pl.BlockSpec(memory_space=pltpu.HBM if far else pltpu.VMEM)] * len(args),
        out_specs=jax.tree.map(lambda _: pl.BlockSpec(memory_space=pltpu.VMEM), out),
        scratch_shapes=scratch,
        compiler_params=pltpu.CompilerParams(vmem_limit_bytes=24 * 1024 * 1024),
        cost_estimate=pl.CostEstimate(flops=flops, bytes_accessed=size, transcendentals=0),
    )(*args)


def shape(dims, dtype):
    return jax.ShapeDtypeStruct(dims, dtype)


def exchange(x, axis):
    return lax.all_to_all(x, axis, split_axis=0, concat_axis=0, tiled=True)


TALL = 2 * SHARE + 8


def body(factors, linear, acc_factors, acc_linear, feature_slot, requests, clicks):
    dma = pltpu.SemaphoreType.DMA
    req_t = requests.T
    ask, wide = call(
        ask_kernel,
        [shape((OWNERS, 8, 128), bf16), shape((ROWS, K), f32)],
        1 << 20,
        req_t,
        linear.reshape(4, 128),
        factors,
        scratch=[pltpu.VMEM((CAP, OWNERS), jnp.int32), pltpu.VMEM((4, 128), f32), dma((3,))],
        far=True,
    )
    got = exchange(ask, "server")
    found = call(gather_kernel, shape((OWNERS, CAP, K), bf16), 1 << 28, got, wide)
    rows = exchange(found, "server")
    lin_terms, ids, counts_t, counts, clicks_col, acc, acc_lin, lin_row = call(
        side_kernel,
        [
            shape((SAMPLES, 128), f32),
            shape((8, SLOTS), f32),
            shape((SLOTS, SAMPLES), bf16),
            shape((SAMPLES, SLOTS), bf16),
            shape((SAMPLES, 1), f32),
            shape((SHARE, K), f32),
            shape((1, 128), f32),
            shape((1, ROWS), f32),
        ],
        1 << 30,
        got,
        req_t,
        feature_slot.T,
        clicks.reshape(1, SAMPLES),
        acc_factors,
        acc_linear.reshape(1, SHARE),
        linear.reshape(1, ROWS),
    )
    push = call(
        learn_kernel,
        shape((OWNERS, 2 * CAP + 8, 128), bf16),
        1 << 28,
        rows,
        counts,
        counts_t,
        clicks_col,
        lin_terms,
        ids,
    )
    pushed = exchange(push, "server")
    pushed = lax.all_gather(pushed, "core", axis=0, tiled=True)
    dense = call(scatter_kernel, shape((N_Y, TALL, 128), bf16), 1 << 28, pushed)
    shared = exchange(dense, "y")
    delta = call(update_kernel, shape((N_Y, TALL, 128), bf16), 1 << 20, shared, acc, acc_lin)
    deltas = exchange(delta, "y")
    deltas = lax.all_gather(deltas, "core", axis=0, tiled=True)
    new_factors, new_linear, new_acc, new_acc_lin = call(
        apply_kernel,
        [shape((ROWS, K), f32), shape((1, ROWS), f32), shape((SHARE, K), f32), shape((1, SHARE), f32)],
        1 << 20,
        deltas,
        wide,
        lin_row,
        shared,
        acc,
        acc_lin,
    )
    return new_factors, new_linear.reshape(ROWS), new_acc, new_acc_lin.reshape(SHARE)


def solution(mesh):
    mesh = Mesh(mesh.devices.reshape(OWNERS, N_Y, N_CORE), ("server", "y", "core"))
    every = ("server", "y", "core")
    in_specs = (
        P("server", None),
        P("server"),
        P(every, None),
        P(every),
        P(every, None),
        P(every, None),
        P(every),
    )
    out_specs = (P("server", None), P("server"), P(every, None), P(every))
    return jax.shard_map(body, mesh=mesh, in_specs=in_specs, out_specs=out_specs, check_vma=False)
```
